512 devices in a mesh: rows: 128 (over y, z, core), serve: 4 (over x).
Axes of the slice: x: 4, y: 4, z: 16, core: 2. Of those that a mesh axis runs over, the one named last changes fastest.
Arguments:
- table_rows: float32 [131072, 128], P('rows'), may hold values from -3 to 3
- row_accum: float32 [131072], P('rows'), may hold values from 0.002 to 0.05
- lookup_rows: int32 [4, 128, 1536], P('serve', 'rows'), may hold values from 0 to 1023
- bag_lengths: int32 [4, 128, 512], P('serve', 'rows'), may hold values from 1 to 8, 1536 in all within a row
- bag_owner: int32 [4, 128, 512, 1], P('serve', 'rows'), may hold values from 0 to 127; in each aligned block of 512 rows (0 to 511, 512 to 1023, ..., all dimensions but the last counted through in order) at most 8 rows name the same one
- bag_target: int32 [4, 128, 512], P('serve', 'rows'), may hold values from 0 to 3327
- bottom_in: bfloat16 [4, 16384, 256], P('serve', 'rows'), may hold values from -6 to 6
- labels: int32 [4, 16384], P('serve', 'rows'), may hold values 0 or 1
- w_bottom: bfloat16 [256, 128], replicated, may hold values from -0.375 to 0.375
- cross_u: bfloat16 [3456, 256], replicated, may hold values from -0.109375 to 0.109375
- cross_v: bfloat16 [256, 3456], replicated, may hold values from -0.375 to 0.375
- cross_bias: float32 [3456], replicated, may hold values from -3 to 3
- w_out: float32 [3456], replicated, may hold values from -0.109375 to 0.109375
- serve_owner: int32 [131072, 1], P('rows'), may hold values from 0 to 127; in each aligned block of 1024 rows (0 to 1023, 1024 to 2047, ...) at most 16 rows name the same one
Outputs:
- new_rows: float32 [131072, 128], P('rows', 'serve')
- new_accum: float32 [131072], P('rows')
- serving_delta: bfloat16 [128, 128, 16, 128], P('rows', None, None, 'serve')
- grad_bottom: float32 [256, 128], replicated
The draws below stay inside these ranges and needn't reach their ends.
Inputs may be any that keep to these rules, and one draw needn't show every extreme that they name: `bag_lengths`: for each s and r the 512 lengths sum to 1536. `bag_owner`: among the 512 partial bags of one device no owner occurs more than 8 times, and on some device one owner occurs exactly 8 times. `serve_owner`: among the 1024 rows of one row shard no serving owner occurs more than 16 times, and on some shard one occurs exactly 16 times.
All inputs are finite; a program needn't handle non-finite values. No bound on the sum of `labels` on one device may be relied on, other than what follows from the above.
Results may differ from the reference program's by a relative error of at most 0.0057.
Values may be sent and summed in bfloat16 or wider, within the bound.
No kernel may reach another device: no remote copies, remote signals or barrier semaphores. Data moves between devices by JAX's collectives and lax.ppermute only.
A program may use at most 64 MiB of HBM per device.

```python
import math
import jax
import jax.numpy as jnp
import numpy as np
from jax import lax

EMB = 128
TABLES = 26
CROSS_W = 3456
RANK = 256
BOT_IN = 256
B_DEV = 128
TOUCH_DEV = 1024
LMAX = 8
PB_DEV = 512
LOOK_DEV = 1536
CAP = 8
DCAP = 16
ROWS_ALL = 131072
N_ROWS = 128
N_SERVE = 4


def with_ends(values, own_key, smallest, top_value):
    spot = [jax.random.randint(jax.random.fold_in(own_key, axis), (), 0, length) for axis, length in enumerate(values.shape)]
    widest = values.shape.index(max(values.shape))
    next_to = spot[:widest] + [(spot[widest] + 1) % values.shape[widest]] + spot[widest + 1:]
    return values.at[tuple(spot)].set(smallest).at[tuple(next_to)].set(top_value)


def level_of(own_key, dims, split, smallest, largest):
    gain, own = 1.0, jax.random.fold_in(own_key, 6)
    for position, shards_of in split:
        draws = jnp.exp(jax.random.uniform(jax.random.fold_in(own, position), (shards_of,), jnp.float32, smallest / len(split), largest / len(split)))
        gain = gain * jnp.repeat(draws, dims[position] // shards_of).reshape([-1 if axis == position else 1 for axis in range(len(dims))])
    return gain


def rank_bounds(amount, skew):
    weights = [(1 << 20) // math.isqrt(rank ** skew) + 1 for rank in range(1, amount + 1)]
    width = 1 + sum(weights) // (1 << 30)
    return np.cumsum(np.array([max(1, weight // width) for weight in weights]))


def skewed_ids(stream_key, extent, amount, skew):
    table = rank_bounds(amount, skew)
    ticket = jax.random.randint(jax.random.fold_in(stream_key, 1), extent, 0, int(table[amount - 1]))
    rank = jnp.searchsorted(jnp.asarray(table, jnp.int32), ticket, side="right")
    return jax.random.permutation(jax.random.fold_in(stream_key, 2), amount)[rank].astype(jnp.int32)


def length_profile(amount, total, bound, skew):
    loads = [(1 << 20) // math.isqrt(rank ** skew) + 1 for rank in range(2, amount + 1)]
    surplus, counts = total - bound - (amount - 1), [1] * (amount - 1)
    while surplus > 0:
        candidates = [i for i in range(amount - 1) if counts[i] < bound]
        pool, left = sum([loads[i] for i in candidates]), surplus
        for i in candidates:
            extra = min(bound - counts[i], max(1, left * loads[i] // pool), surplus)
            counts[i] = counts[i] + extra
            surplus = surplus - extra
    return np.array([bound] + counts)


def ragged_sizes(stream_key, number_of, total, most, skew):
    if number_of == 2:
        one = jax.random.randint(stream_key, (), max(1, total - most), min(most, total - 1) + 1)
        return jnp.stack([one, total - one])
    sizes = jnp.asarray(length_profile(number_of, total, most, skew), jnp.int32)
    pairs = (number_of - 1) // 2
    source_of, taker = sizes[1:1 + 2 * pairs:2], sizes[2:2 + 2 * pairs:2]
    slack = jnp.minimum(source_of - 1, most - taker)
    moved = jax.random.randint(jax.random.fold_in(stream_key, 1), (pairs,), 0, 1 << 20) % (slack + 1)
    sizes = sizes.at[1:1 + 2 * pairs:2].set(source_of - moved).at[2:2 + 2 * pairs:2].set(taker + moved)
    return sizes[jax.random.permutation(jax.random.fold_in(stream_key, 2), number_of)]


def routed_block(rng, own, number, rows, count, top, reach, slope):
    sequence = jax.random.permutation(rng, count)
    crowded, ordinary = load_shares(count, rows * top, reach, slope, True), load_shares(count, rows * top, reach, slope, False)
    places = jnp.arange(count)

    def named(tallies, offset_by):
        used = int((tallies > 0).sum())
        fixed = max(1, used // 4)
        shifted = fixed + (places - fixed + offset_by * (used - fixed)) % max(1, count - fixed)
        return jnp.zeros((count,), jnp.int32).at[sequence[jnp.where(places < fixed, places, shifted)]].set(jnp.asarray(tallies, jnp.int32))

    tallies = jnp.where(number % 4 == 0, named(crowded, number // 4), named(ordinary, number - number // 4 - 1))
    mixed = jax.random.permutation(jax.random.fold_in(own, 3), count)
    source_of, sink = mixed[0:count // 2 * 2:2], mixed[1:count // 2 * 2:2]
    room = jnp.minimum(tallies[source_of] - 1, reach - tallies[sink]) // 2
    room = jnp.where((source_of == sequence[0]) | (sink == sequence[0]) | (tallies[sink] == 0), 0, jnp.maximum(room, 0))
    shifted = jax.random.randint(jax.random.fold_in(own, 4), (count // 2,), 0, 1 << 20) % (room + 1)
    tallies = tallies.at[source_of].add(-shifted).at[sink].add(shifted)
    items = jnp.searchsorted(jnp.cumsum(tallies), jnp.arange(rows * top), side="right").astype(jnp.int32)
    listing = items.reshape(top, rows).T
    listing = listing[jax.random.permutation(jax.random.fold_in(own, 1), rows)]
    offset_by = jax.random.randint(jax.random.fold_in(own, 2), (rows, 1), 0, top)
    return jnp.take_along_axis(listing, (jnp.arange(top)[None, :] + offset_by) % top, axis=1)


def load_shares(amount, total, reach, lean, full):
    loads = [(1 << 20) // math.isqrt(standing ** lean) + 1 for standing in range(1, amount + 1)]
    largest = reach if full else min(reach, max(-(-total // amount), total * loads[0] // sum(loads)))
    least = 1 if total - largest >= amount - 1 else 0
    counts, spare = [largest] + [least] * (amount - 1), total - largest - least * (amount - 1)
    while spare > 0:
        candidates = [i for i in range(1, amount) if counts[i] < largest] or [i for i in range(1, amount) if counts[i] < reach]
        pool, remaining = sum([loads[i] for i in candidates]), spare
        for i in candidates:
            addition = min(reach - counts[i], max(1, remaining * loads[i] // pool), spare)
            counts[i] = counts[i] + addition
            spare = spare - addition
    return np.array(counts)


def noise(rng, extent, width, limit, split=(), kind=jnp.bfloat16):
    entries = width * jax.random.normal(rng, extent, jnp.float32)
    if split:
        entries = entries * level_of(rng, extent, split, -0.22, 0.18)
    return jnp.clip(entries, -limit, limit).astype(kind)


def setup_inputs(seed: int = 0) -> dict:
    keys = jax.random.split(jax.random.key(seed), 15)
    table_rows = noise(keys[0], (ROWS_ALL, EMB), 0.5, 3.0, ((0, 128),), jnp.float32)
    row_accum = jnp.clip(jnp.exp(math.log(0.05) - 3.218876 * jax.random.uniform(keys[1], (ROWS_ALL,), jnp.float32) ** level_of(keys[1], (ROWS_ALL,), ((0, 128),), -0.2, 0.2)), 0.002, 0.05)
    lookup_rows = with_ends(skewed_ids(keys[2], (N_SERVE, N_ROWS, LOOK_DEV), TOUCH_DEV, 2), jax.random.fold_in(keys[2], 3), 0, TOUCH_DEV - 1).astype(jnp.int32)
    bag_lengths = jax.vmap(lambda own: ragged_sizes(own, PB_DEV, LOOK_DEV, LMAX, 2))(jax.random.split(keys[3], N_SERVE * N_ROWS)).reshape((N_SERVE, N_ROWS, PB_DEV)).astype(jnp.int32)
    bag_owner_keys = jax.random.split(jax.random.fold_in(keys[4], 1), N_SERVE * N_ROWS * PB_DEV // PB_DEV)
    bag_owner_turns = jax.random.permutation(jax.random.fold_in(keys[4], 3), N_SERVE * N_ROWS * PB_DEV // PB_DEV)
    bag_owner = jax.vmap(lambda own, number: routed_block(jax.random.fold_in(keys[4], 2), own, number, PB_DEV, N_ROWS, 1, CAP, 1))(bag_owner_keys, bag_owner_turns).reshape((N_SERVE, N_ROWS, PB_DEV, 1))
    bag_target = with_ends(jax.random.randint(keys[5], (N_SERVE, N_ROWS, PB_DEV), 0, B_DEV * TABLES), jax.random.fold_in(keys[5], 1), 0, (B_DEV * TABLES) - 1).astype(jnp.int32)
    bottom_in = noise(keys[6], (N_SERVE, N_ROWS * B_DEV, BOT_IN), 1.0, 6.0, ((0, 4), (1, 128)))
    labels = with_ends((jax.random.randint(keys[7], (N_SERVE, N_ROWS * B_DEV), 0, 2) < 1).astype(jnp.int32), jax.random.fold_in(keys[7], 1), 0, 1)
    w_bottom = noise(keys[8], (BOT_IN, EMB), BOT_IN ** -0.5, 0.375)
    cross_u = noise(keys[9], (CROSS_W, RANK), CROSS_W ** -0.5, 0.109375)
    cross_v = noise(keys[10], (RANK, CROSS_W), RANK ** -0.5, 0.375)
    cross_bias = noise(keys[11], (CROSS_W,), 0.5, 3.0, (), jnp.float32)
    w_out = noise(keys[12], (CROSS_W,), CROSS_W ** -0.5, 0.109375, (), jnp.float32)
    serve_owner_keys = jax.random.split(jax.random.fold_in(keys[13], 1), ROWS_ALL // TOUCH_DEV)
    serve_owner_turns = jax.random.permutation(jax.random.fold_in(keys[13], 3), ROWS_ALL // TOUCH_DEV)
    serve_owner = jax.vmap(lambda own, number: routed_block(jax.random.fold_in(keys[13], 2), own, number, TOUCH_DEV, N_ROWS, 1, DCAP, 2))(serve_owner_keys, serve_owner_turns).reshape((ROWS_ALL, 1))
    return {"table_rows": table_rows, "row_accum": row_accum, "lookup_rows": lookup_rows, "bag_lengths": bag_lengths, "bag_owner": bag_owner, "bag_target": bag_target, "bottom_in": bottom_in, "labels": labels, "w_bottom": w_bottom, "cross_u": cross_u, "cross_v": cross_v, "cross_bias": cross_bias, "w_out": w_out, "serve_owner": serve_owner}


LEARN_RATE = 0.1

def bag_index(lengths, count):
    return jnp.repeat(jnp.arange(lengths.shape[0], dtype=jnp.int32), lengths, total_repeat_length=count)

def owner_ranks(owners, groups):
    onehot = (owners[:, None] == jnp.arange(groups, dtype=jnp.int32)[None, :]).astype(jnp.int32)
    before = jnp.cumsum(onehot, axis=0) - onehot
    return lax.optimization_barrier(jnp.sum(before * onehot, axis=1)).astype(jnp.int32)

def silu_slope(values):
    sigma = jax.nn.sigmoid(values)
    return sigma * (1.0 + values * (1.0 - sigma))

def pool_shard(items):
    shard_rows, lookups, lengths = items
    bag_of = bag_index(lengths, lookups.shape[0])
    return jax.ops.segment_sum(shard_rows[lookups], bag_of, num_segments=lengths.shape[0]).astype(jnp.bfloat16)

def return_shard(items):
    bag_grad, lookups, lengths = items
    bag_of = bag_index(lengths, lookups.shape[0])
    return jax.ops.segment_sum(bag_grad[bag_of].astype(jnp.float32), lookups, num_segments=TOUCH_DEV)

def dense_owner(weights, items):
    embedded, dense_in, targets = items
    w_bottom, cross_u, cross_v, cross_bias, w_out = weights
    dense_f = dense_in.astype(jnp.float32)
    pre_act = jnp.dot(dense_f, w_bottom.astype(jnp.float32), preferred_element_type=jnp.float32)
    cross_in = jnp.concatenate([jax.nn.silu(pre_act), embedded], axis=1).astype(jnp.bfloat16)
    cross_f = cross_in.astype(jnp.float32)
    low_rank = jnp.dot(cross_f, cross_u.astype(jnp.float32), preferred_element_type=jnp.float32).astype(jnp.bfloat16)
    mixed = jnp.dot(low_rank.astype(jnp.float32), cross_v.astype(jnp.float32), preferred_element_type=jnp.float32) + cross_bias
    logits = lax.optimization_barrier(jnp.sum((cross_f * mixed + cross_f) * w_out[None, :], axis=1))
    logit_grad = jax.nn.sigmoid(logits) - targets.astype(jnp.float32)
    out_grad = logit_grad[:, None] * w_out[None, :]
    mix_grad = (out_grad * cross_f).astype(jnp.bfloat16)
    low_grad = jnp.dot(mix_grad.astype(jnp.float32), cross_v.astype(jnp.float32).T, preferred_element_type=jnp.float32).astype(jnp.bfloat16)
    in_grad = out_grad * (mixed + 1.0) + jnp.dot(low_grad.astype(jnp.float32), cross_u.astype(jnp.float32).T, preferred_element_type=jnp.float32)
    emb_width = w_bottom.shape[1]
    embed_grad = in_grad[:, emb_width:].astype(jnp.bfloat16).reshape(-1, emb_width)
    pre_grad = (in_grad[:, :emb_width] * silu_slope(pre_act)).astype(jnp.bfloat16)
    bottom_part = jnp.dot(dense_f.T, pre_grad.astype(jnp.float32), preferred_element_type=jnp.float32)
    return (embed_grad, bottom_part)

def partial_dense(weights):

    def apply_owner(items):
        return dense_owner(weights, items)
    return apply_owner

def reference(table_rows, row_accum, lookup_rows, bag_lengths, bag_owner, bag_target, bottom_in, labels, w_bottom, cross_u, cross_v, cross_bias, w_out, serve_owner):
    shard_rows = table_rows.reshape(N_ROWS, TOUCH_DEV, EMB)
    slots = B_DEV * TABLES
    weights = (w_bottom, cross_u, cross_v, cross_bias, w_out)
    grads = jnp.zeros((N_ROWS, TOUCH_DEV, EMB), jnp.float32)
    grad_bottom = jnp.zeros((BOT_IN, EMB), jnp.float32)
    for replica in range(N_SERVE):
        lookups = lookup_rows[replica]
        lengths = bag_lengths[replica]
        owners = bag_owner[replica][:, :, 0]
        pooled = lax.map(pool_shard, (shard_rows, lookups, lengths))
        flat_ids = (owners * slots + bag_target[replica]).reshape(-1).astype(jnp.int32)
        embedded = jax.ops.segment_sum(pooled.reshape(-1, EMB).astype(jnp.float32), flat_ids, num_segments=N_ROWS * slots)
        embedded = embedded.reshape(N_ROWS, B_DEV, TABLES * EMB)
        dense_in = bottom_in[replica].reshape(N_ROWS, B_DEV, BOT_IN)
        targets = labels[replica].reshape(N_ROWS, B_DEV)
        embed_grad, bottom_parts = lax.map(partial_dense(weights), (embedded, dense_in, targets))
        grad_bottom = grad_bottom + lax.optimization_barrier(jnp.sum(bottom_parts, axis=0))
        bag_grad = embed_grad.reshape(N_ROWS * slots, EMB)[flat_ids].reshape(N_ROWS, PB_DEV, EMB)
        grads = grads + lax.map(return_shard, (bag_grad, lookups, lengths))
    row_grad = grads.reshape(ROWS_ALL, EMB)
    new_accum = row_accum + lax.optimization_barrier(jnp.mean(row_grad * row_grad, axis=1))
    step = row_grad / jnp.sqrt(new_accum)[:, None]
    new_rows = table_rows - LEARN_RATE * step
    owner_rows = serve_owner[:, 0].reshape(N_ROWS, TOUCH_DEV)
    ranks = jax.vmap(lambda owners_row: owner_ranks(owners_row, N_ROWS))(owner_rows)
    sources = jnp.broadcast_to(jnp.arange(N_ROWS, dtype=jnp.int32)[:, None], (N_ROWS, TOUCH_DEV))
    serving_delta = jnp.zeros((N_ROWS, N_ROWS, DCAP, EMB), jnp.bfloat16)
    serving_delta = serving_delta.at[owner_rows.reshape(-1), sources.reshape(-1), ranks.reshape(-1)].set(step.astype(jnp.bfloat16))
    return (new_rows, new_accum, serving_delta, grad_bottom)
```

```python
import functools

import jax
import jax.numpy as jnp
from jax import lax
from jax.experimental import pallas as pl
from jax.experimental.pallas import tpu as pltpu
from jax.sharding import PartitionSpec as P

TABLES = 26
LEARN_RATE = 0.1
EMB = 128
PEERS = 128
CAP = 8
ROWS_A = 10
ALL_A = PEERS * ROWS_A
ROWS_D = 6
ALL_D = PEERS * ROWS_D
F32 = jnp.float32
BF16 = jnp.bfloat16
VMEM_LIMIT = 48 * 1024 * 1024


def dot(a, b, ca=1, cb=0):
    return lax.dot_general(a, b, (((ca,), (cb,)), ((), ())), preferred_element_type=F32)


def iota(shape, dim):
    return lax.broadcasted_iota(jnp.int32, shape, dim)


def onehot(mask):
    return jnp.where(mask, 1.0, 0.0).astype(BF16)


def divide_floor(values, by):
    return jnp.floor((values.astype(F32) + 0.5) * (1.0 / by)).astype(jnp.int32)


def owner_place(owners):
    return owners


def pool_kernel(table_ref, lookups_ref, lengths_ref, owners_ref, targets_ref, out_ref, counts_ref, slots_ref):
    bags = lengths_ref.shape[1]
    looks = lookups_ref.shape[1]
    touched = table_ref.shape[0]
    lens = jnp.broadcast_to(lengths_ref[...].astype(F32), (8, bags)).astype(BF16)
    row_id = iota((bags, bags), 0)
    col_id = iota((bags, bags), 1)
    starts = dot(onehot(col_id < row_id), lens, 1, 1)[:, 0:1].astype(jnp.int32)
    ends = dot(onehot(col_id <= row_id), lens, 1, 1)[:, 0:1].astype(jnp.int32)
    place = iota((bags, looks), 1)
    in_bag = onehot((place >= starts) & (place < ends))
    of_row = onehot(iota((touched, looks), 0) == lookups_ref[...])
    counts = dot(in_bag, of_row, 1, 1).astype(BF16)
    counts_ref[...] = counts
    table = table_ref[...]
    high = table.astype(BF16)
    low = (table - high.astype(F32)).astype(BF16)
    sums = dot(counts, jnp.concatenate([high, low], axis=1))
    pooled = (sums[:, :EMB] + sums[:, EMB:]).astype(BF16)
    owners = owners_ref[...]
    of_owner = jnp.where(iota((PEERS, bags), 0) == owners, 1.0, 0.0)
    before = dot(of_owner.astype(BF16), onehot(row_id < col_id))
    rank = jnp.sum(before * of_owner, axis=0, keepdims=True).astype(jnp.int32)
    first = owner_place(owners) * ROWS_A
    slots = first + rank
    slots_ref[...] = slots
    slot_id = iota((ALL_A, bags), 0)
    payload = dot(onehot(slot_id == slots), pooled)
    targets = targets_ref[...]
    sample = divide_floor(targets, TABLES)
    table_of = targets - sample * TABLES
    lane = iota((EMB, bags), 0)
    names = jnp.where(lane == rank, sample + 1, 0) + jnp.where(lane == rank + CAP, table_of, 0)
    payload = payload + dot(onehot(slot_id == first + CAP), names.astype(F32).astype(BF16), 1, 1)
    out_ref[...] = payload.astype(BF16)


def silu_slope(values, sigma):
    return sigma * (1.0 + values * (1.0 - sigma))


def owner_kernel(
    arrived_ref,
    dense_ref,
    labels_ref,
    w_bottom_ref,
    cross_u_ref,
    cross_v_ref,
    bias_ref,
    w_out_ref,
    out_ref,
    cross_ref,
    mixed_ref,
    embed_ref,
    member_ref,
    table_ref,
):
    samples = dense_ref.shape[0]
    width = cross_u_ref.shape[0]
    peer = iota((PEERS, ALL_A), 0)
    slot = iota((PEERS, ALL_A), 1)
    names = dot(onehot(slot == peer * ROWS_A + CAP), arrived_ref[...]).astype(BF16)
    chunk_row = divide_floor(iota((1, ALL_A), 1), ROWS_A)
    place_row = iota((1, ALL_A), 1) - chunk_row * ROWS_A
    spread = dot(names, onehot(peer == chunk_row), 0, 0)
    picks = iota((CAP, ALL_A), 0) == place_row
    sample_row = jnp.sum(jnp.where(picks, spread[:CAP], 0.0), axis=0, keepdims=True)
    table_row = jnp.sum(jnp.where(picks, spread[CAP : 2 * CAP], 0.0), axis=0, keepdims=True)
    slot_t = iota((ALL_A, PEERS), 0)
    lane_t = iota((ALL_A, PEERS), 1)
    chunk_t = divide_floor(slot_t, ROWS_A)
    place_t = slot_t - chunk_t * ROWS_A
    spread_t = dot(onehot(lane_t == chunk_t), names).astype(BF16)
    ones = jnp.ones((PEERS, PEERS), BF16)
    held = place_t < CAP
    sample_t = dot(jnp.where(held & (lane_t == place_t), spread_t, 0.0).astype(BF16), ones)
    table_t = dot(jnp.where(held & (lane_t == place_t + CAP), spread_t, 0.0).astype(BF16), ones)
    member_ref[...] = onehot(sample_t.astype(jnp.int32) == lane_t + 1)
    table_ref[...] = table_t.astype(BF16)
    member = onehot(sample_row.astype(jnp.int32) == iota((samples, ALL_A), 0) + 1)
    table_row = table_row.astype(jnp.int32)

    dense = dense_ref[...]
    pre_act = dot(dense, w_bottom_ref[...])
    sigma = jax.nn.sigmoid(pre_act)
    cross_ref[:, :EMB] = (pre_act * sigma).astype(BF16)
    arrived = arrived_ref[...]
    for t in range(0, TABLES, 2):
        both = jnp.concatenate([member * onehot(table_row == t), member * onehot(table_row == t + 1)], axis=0)
        embedded = dot(both, arrived).astype(BF16)
        cross_ref[:, (t + 1) * EMB : (t + 2) * EMB] = embedded[:samples]
        cross_ref[:, (t + 2) * EMB : (t + 3) * EMB] = embedded[samples:]

    low_rank = dot(cross_ref[...], cross_u_ref[...]).astype(BF16)
    mixed_ref[...] = dot(low_rank, cross_v_ref[...]) + bias_ref[...]
    cross_f = cross_ref[...].astype(F32)
    w_out = w_out_ref[...]
    logits = jnp.sum((cross_f * mixed_ref[...] + cross_f) * w_out, axis=1, keepdims=True)
    logit_grad = jax.nn.sigmoid(logits) - labels_ref[...].astype(F32)
    mix_grad = (logit_grad * w_out * cross_f).astype(BF16)
    low_grad = dot(mix_grad, cross_v_ref[...], 1, 1).astype(BF16)
    in_grad = logit_grad * w_out * (mixed_ref[...] + 1.0) + dot(low_grad, cross_u_ref[...], 1, 1)
    pre_grad = (in_grad[:, :EMB] * silu_slope(pre_act, sigma)).astype(BF16)
    for t in range(TABLES):
        embed_ref[t * samples : (t + 1) * samples, :] = in_grad[:, (t + 1) * EMB : (t + 2) * EMB].astype(BF16)
    bottom = dot(dense, pre_grad, 0, 0).astype(BF16)

    step = 256
    for c in range(ALL_A // step):
        rows = slice(c * step, (c + 1) * step)
        member_c = member_ref[rows, :]
        table_c = table_ref[rows, :]
        wide = jnp.concatenate(
            [jnp.where(table_c == t, member_c, 0.0).astype(BF16) for t in range(TABLES)], axis=1
        )
        reply = dot(wide, embed_ref[...])
        slot_c = iota((step, 2 * PEERS), 0) + c * step
        chunk_c = divide_floor(slot_c, ROWS_A)
        place_c = slot_c - chunk_c * ROWS_A
        wanted = (place_c >= CAP) & (iota((step, 2 * PEERS), 1) == 2 * chunk_c + place_c - CAP)
        reply = reply + dot(onehot(wanted), bottom)
        out_ref[rows, :] = reply.astype(BF16)


def return_kernel(returned_ref, counts_ref, slots_ref, grads_ref, bottom_ref):
    returned = returned_ref[...]
    bags = slots_ref.shape[1]
    pick = onehot(iota((ALL_A, bags), 0) == slots_ref[...])
    bag_grads = dot(returned, pick, 0, 0).astype(BF16)
    grads_ref[...] = dot(bag_grads, counts_ref[...]).astype(BF16)
    slot = iota((8, ALL_A), 1)
    place = slot - divide_floor(slot, ROWS_A) * ROWS_A
    bottom_ref[...] = dot(onehot(place == iota((8, ALL_A), 0) + CAP), returned)


def total_kernel(grads_ref, bottom_ref, total_ref, message_ref):
    total = grads_ref[0].astype(F32)
    for s in range(1, grads_ref.shape[0]):
        total = total + grads_ref[s].astype(F32)
    total_ref[...] = total
    squares = jnp.sum(total * total, axis=0, keepdims=True)
    bottom = bottom_ref[...]
    message = jnp.concatenate([squares, bottom[0:1], bottom[1:2]], axis=1)
    for s in range(message_ref.shape[0]):
        message_ref[s] = message


def serving_rank_kernel(owners_ref, rank_ref):
    rows = owners_ref.shape[1]
    owners = owners_ref[...]
    of_owner = jnp.where(iota((PEERS, rows), 0) == owners, 1.0, 0.0)
    before = dot(of_owner.astype(BF16), onehot(iota((rows, rows), 0) < iota((rows, rows), 1)))
    rank_ref[...] = jnp.sum(before * of_owner, axis=0, keepdims=True).astype(jnp.int32)


def step_kernel(message_ref, total_ref, accum_ref, table_ref, owners_ref, rank_ref, rows_ref, accum_out_ref, out_ref):
    rows = accum_ref.shape[1]
    message = message_ref[0]
    for s in range(1, message_ref.shape[0]):
        message = message + message_ref[s]
    accum = accum_ref[...] + message[:, :rows] * (1.0 / EMB)
    accum_out_ref[...] = accum
    step = total_ref[...] / jnp.sqrt(accum)
    rows_ref[...] = table_ref[...] - LEARN_RATE * step.T
    rank = rank_ref[...]
    row_of = lax.shift_right_logical(rank, 2)
    block = rank - 4 * row_of
    cols = step.shape[0]
    wide = jnp.concatenate([jnp.where(block == a, step, 0.0) for a in range(4)], axis=0).astype(BF16)
    place = owner_place(owners_ref[...]) * ROWS_D + row_of
    payload = dot(onehot(iota((ALL_D, rows), 0) == place), wide, 1, 1)
    slot = iota((ALL_D, EMB), 0)
    place = slot - divide_floor(slot, ROWS_D) * ROWS_D
    payload = jnp.where(place == 4, message[:, rows : rows + EMB], payload)
    payload = jnp.where(place == 5, message[:, rows + EMB : rows + 2 * EMB], payload)
    out_ref[...] = payload.astype(BF16)


def call(kernel, outs, *args, scratch=(), flops=0):
    moved = sum(x.size * x.dtype.itemsize for x in args)
    return pl.pallas_call(
        kernel,
        out_shape=[jax.ShapeDtypeStruct(shape, kind) for shape, kind in outs],
        scratch_shapes=list(scratch),
        compiler_params=pltpu.CompilerParams(vmem_limit_bytes=VMEM_LIMIT),
        cost_estimate=pl.CostEstimate(flops=flops, bytes_accessed=moved, transcendentals=0),
    )(*args)


def over_rows(chunks, rows):
    split = chunks.reshape(PEERS, rows // 2, 2, EMB)
    split = lax.all_to_all(split, "rows", split_axis=0, concat_axis=0, tiled=True)
    return split.reshape(PEERS * rows, EMB)


def per_device(
    table_rows,
    row_accum,
    lookup_rows,
    bag_lengths,
    bag_owner,
    bag_target,
    bottom_in,
    labels,
    w_bottom,
    cross_u,
    cross_v,
    cross_bias,
    w_out,
    serve_owner,
):
    touched = table_rows.shape[0]
    lookups = lookup_rows.reshape(1, -1)
    lengths = bag_lengths.reshape(1, -1)
    bags = lengths.shape[1]
    owners = bag_owner.reshape(1, -1)
    targets = bag_target.reshape(1, -1)
    dense_in = bottom_in.reshape(-1, bottom_in.shape[-1])
    samples = dense_in.shape[0]
    width = cross_u.shape[0]
    serves = lax.axis_size("serve")
    cols = EMB // serves

    outgoing, counts, slots = call(
        pool_kernel,
        [((ALL_A, EMB), BF16), ((bags, touched), BF16), ((1, bags), jnp.int32)],
        table_rows,
        lookups,
        lengths,
        owners,
        targets,
        flops=2 * 1100 * 10**6,
    )
    arrived = over_rows(outgoing, ROWS_A)
    destinations = serve_owner.reshape(1, -1)
    (serve_rank,) = call(
        serving_rank_kernel, [((1, touched), jnp.int32)], destinations, flops=2 * 134 * 10**6
    )
    table_cols = lax.dynamic_slice_in_dim(table_rows, lax.axis_index("serve") * cols, cols, 1)
    (replies,) = call(
        owner_kernel,
        [((ALL_A, EMB), BF16)],
        arrived,
        dense_in,
        labels.reshape(-1, 1),
        w_bottom,
        cross_u,
        cross_v,
        cross_bias.reshape(1, -1),
        w_out.reshape(1, -1),
        scratch=(
            pltpu.VMEM((samples, width), BF16),
            pltpu.VMEM((samples, width), F32),
            pltpu.VMEM((samples * TABLES, EMB), BF16),
            pltpu.VMEM((ALL_A, PEERS), BF16),
            pltpu.VMEM((ALL_A, PEERS), BF16),
        ),
        flops=2 * 1600 * 10**6,
    )
    returned = over_rows(replies, ROWS_A)
    grads, bottom = call(
        return_kernel,
        [((EMB, touched), BF16), ((8, EMB), F32)],
        returned,
        counts,
        slots,
        flops=2 * 160 * 10**6,
    )
    pieces = lax.all_to_all(
        grads.reshape(serves, cols, touched), "serve", split_axis=0, concat_axis=0, tiled=True
    )
    total, message = call(
        total_kernel,
        [((cols, touched), F32), ((serves, 1, touched + 2 * EMB), F32)],
        pieces,
        bottom,
    )
    messages = lax.all_to_all(message, "serve", split_axis=0, concat_axis=0, tiled=True)
    new_rows, new_accum, steps = call(
        step_kernel,
        [((touched, cols), F32), ((1, touched), F32), ((ALL_D, EMB), BF16)],
        messages,
        total,
        row_accum.reshape(1, -1),
        table_cols,
        destinations,
        serve_rank,
        flops=2 * 100 * 10**6,
    )
    served = over_rows(steps, ROWS_D).reshape(PEERS, ROWS_D, EMB)
    serving = served[:, :4].reshape(1, PEERS, 16, cols)
    grad_bottom = served[:, 4:].reshape(2 * PEERS, EMB).astype(F32)
    return (new_rows, new_accum.reshape(-1), serving, grad_bottom)


def solution(mesh):
    return jax.shard_map(
        per_device,
        mesh=mesh,
        in_specs=(
            P("rows", None),
            P("rows"),
            P("serve", "rows", None),
            P("serve", "rows", None),
            P("serve", "rows", None, None),
            P("serve", "rows", None),
            P("serve", "rows", None),
            P("serve", "rows"),
            P(),
            P(),
            P(),
            P(),
            P(),
            P("rows", None),
        ),
        out_specs=(P("rows", "serve"), P("rows"), P("rows", None, None, "serve"), P()),
        check_vma=False,
    )
```

```python
import functools

import jax
import jax.numpy as jnp
from jax import lax
from jax.experimental import pallas as pl
from jax.experimental.pallas import tpu as pltpu
from jax.sharding import PartitionSpec as P

TABLES = 26
LEARN_RATE = 0.1
EMB = 128
PEERS = 128
CAP = 8
ROWS_A = 10
ALL_A = PEERS * ROWS_A
ROWS_D = 6
ALL_D = PEERS * ROWS_D
F32 = jnp.float32
BF16 = jnp.bfloat16
VMEM_LIMIT = 32 * 1024 * 1024


def dot(a, b, ca=1, cb=0):
    return lax.dot_general(a, b, (((ca,), (cb,)), ((), ())), preferred_element_type=F32)


def iota(shape, dim):
    return lax.broadcasted_iota(jnp.int32, shape, dim)


def onehot(mask):
    return jnp.where(mask, 1.0, 0.0).astype(BF16)


def divide_floor(values, by):
    return jnp.floor((values.astype(F32) + 0.5) * (1.0 / by)).astype(jnp.int32)


def owner_place(owners):
    return owners


def fetch(sources, targets, sems):
    copies = [pltpu.make_async_copy(s, t, sems.at[i]) for i, (s, t) in enumerate(zip(sources, targets))]
    for copy in copies:
        copy.start()
    return copies


def pool_kernel(
    lengths_hbm,
    lookups_hbm,
    owners_hbm,
    targets_hbm,
    table_hbm,
    out_ref,
    counts_ref,
    slots_ref,
    lengths_ref,
    lookups_ref,
    owners_ref,
    targets_ref,
    table_ref,
    sems,
):
    copies = fetch(
        (lengths_hbm, lookups_hbm, owners_hbm, targets_hbm, table_hbm),
        (lengths_ref, lookups_ref, owners_ref, targets_ref, table_ref),
        sems,
    )
    bags = lengths_ref.shape[1]
    looks = lookups_ref.shape[1]
    touched = table_ref.shape[0]
    row_id = iota((bags, bags), 0)
    col_id = iota((bags, bags), 1)
    place = iota((bags, looks), 1)
    for copy in copies[:4]:
        copy.wait()
    lens = jnp.broadcast_to(lengths_ref[...].astype(F32), (8, bags)).astype(BF16)
    starts = dot(onehot(col_id < row_id), lens, 1, 1)[:, 0:1].astype(jnp.int32)
    ends = dot(onehot(col_id <= row_id), lens, 1, 1)[:, 0:1].astype(jnp.int32)
    in_bag = onehot((place >= starts) & (place < ends))
    of_row = onehot(iota((touched, looks), 0) == lookups_ref[...])
    counts = dot(in_bag, of_row, 1, 1).astype(BF16)
    counts_ref[...] = counts
    copies[4].wait()
    table = table_ref[...]
    high = table.astype(BF16)
    low = (table - high.astype(F32)).astype(BF16)
    sums = dot(counts, jnp.concatenate([high, low], axis=1))
    pooled = (sums[:, :EMB] + sums[:, EMB:]).astype(BF16)
    owners = owners_ref[...]
    of_owner = jnp.where(iota((PEERS, bags), 0) == owners, 1.0, 0.0)
    before = dot(of_owner.astype(BF16), onehot(row_id < col_id))
    rank = jnp.sum(before * of_owner, axis=0, keepdims=True).astype(jnp.int32)
    first = owner_place(owners) * ROWS_A
    slots = first + rank
    slots_ref[...] = slots
    targets = targets_ref[...]
    sample = divide_floor(targets, TABLES)
    table_of = targets - sample * TABLES
    lane = iota((EMB, bags), 0)
    names = jnp.where(lane == rank, sample + 1, 0) + jnp.where(lane == rank + CAP, table_of, 0)
    slot_id = iota((ALL_A, bags), 0)
    payload = dot(onehot(slot_id == slots), pooled)
    payload = payload + dot(onehot(slot_id == first + CAP), names.astype(F32).astype(BF16), 1, 1)
    out_ref[...] = payload.astype(BF16)


def ready_kernel(
    counts_ref,
    slots_ref,
    owners_ref,
    table_ref,
    cross_u_ref,
    cross_v_ref,
    name_row_ref,
    chunk_ref,
    wanted_ref,
    routed_ref,
    steps_ref,
    block_ref,
    cols_ref,
    u_turned_ref,
    v_turned_ref,
    turned_ref,
):
    rows = owners_ref.shape[1]
    bags = slots_ref.shape[1]
    peer = iota((PEERS, ALL_A), 0)
    slot = iota((PEERS, ALL_A), 1)
    name_row_ref[...] = onehot(slot == peer * ROWS_A + CAP)
    chunk_ref[...] = onehot((slot >= peer * ROWS_A) & (slot < (peer + 1) * ROWS_A))
    slot = iota((ALL_A, 2 * PEERS), 0)
    line = iota((ALL_A, 2 * PEERS), 1)
    wanted_ref[...] = onehot(slot == lax.shift_right_logical(line, 1) * ROWS_A + CAP + (line & 1))
    routed_ref[...] = dot(onehot(iota((ALL_A, bags), 0) == slots_ref[...]), counts_ref[...]).astype(BF16)
    owners = owners_ref[...]
    of_owner = jnp.where(iota((PEERS, rows), 0) == owners, 1.0, 0.0)
    before = dot(of_owner.astype(BF16), onehot(iota((rows, rows), 0) < iota((rows, rows), 1)))
    rank = jnp.sum(before * of_owner, axis=0, keepdims=True).astype(jnp.int32)
    row_of = lax.shift_right_logical(rank, 2)
    block_ref[...] = rank - 4 * row_of
    steps_ref[...] = onehot(iota((ALL_D, rows), 0) == owner_place(owners) * ROWS_D + row_of)
    cols = cols_ref.shape[0]
    turned_ref[...] = table_ref[...].T
    u_turned_ref[...] = cross_u_ref[...].T
    v_turned_ref[...] = cross_v_ref[...].T
    cols_ref[...] = turned_ref[pl.ds(pl.multiple_of(lax.axis_index("serve") * cols, cols), cols), :]


def owner_kernel(
    arrived_ref,
    name_row_ref,
    chunk_ref,
    wanted_ref,
    dense_ref,
    labels_ref,
    w_bottom_ref,
    bias_ref,
    w_out_ref,
    cross_u_ref,
    cross_v_ref,
    u_turned_ref,
    v_turned_ref,
    out_ref,
    cross_ref,
    mixed_ref,
    embed_ref,
    member_ref,
    table_ref,
):
    samples = dense_ref.shape[0]
    arrived = arrived_ref[...]
    names = dot(name_row_ref[...], arrived).astype(BF16)
    spread = dot(names, chunk_ref[...], 0, 0)
    place = iota((CAP, ALL_A), 1)
    place = place - divide_floor(place, ROWS_A) * ROWS_A
    picks = iota((CAP, ALL_A), 0) == place
    sample_row = jnp.sum(jnp.where(picks, spread[:CAP], 0.0), axis=0, keepdims=True)
    table_row = jnp.sum(jnp.where(picks, spread[CAP : 2 * CAP], 0.0), axis=0, keepdims=True)
    member_f = jnp.where(sample_row.astype(jnp.int32) == iota((samples, ALL_A), 0) + 1, 1.0, 0.0)
    member = member_f.astype(BF16)
    member_ref[...] = member_f.T.astype(BF16)
    table_ref[...] = jnp.broadcast_to(table_row, (samples, ALL_A)).T.astype(BF16)

    dense = dense_ref[...]
    pre_act = dot(dense, w_bottom_ref[...])
    sigma = jax.nn.sigmoid(pre_act)
    cross_ref[:, :EMB] = (pre_act * sigma).astype(BF16)
    group = TABLES // 2
    for t in range(0, TABLES, group):
        both = jnp.concatenate([member * onehot(table_row == t + u) for u in range(group)], axis=0)
        embedded = dot(both, arrived).astype(BF16)
        for u in range(group):
            cross_ref[:, (t + u + 1) * EMB : (t + u + 2) * EMB] = embedded[u * samples : (u + 1) * samples]

    low_rank = dot(cross_ref[...], cross_u_ref[...]).astype(BF16)
    w_out = w_out_ref[...]
    mixed_ref[...] = (dot(low_rank, cross_v_ref[...]) + (bias_ref[...] + 1.0)) * w_out
    cross_f = cross_ref[...].astype(F32)
    logits = jnp.sum(cross_f * mixed_ref[...], axis=1, keepdims=True)
    logit_grad = jax.nn.sigmoid(logits) - labels_ref[...].astype(F32)
    mix_grad = (logit_grad * w_out * cross_f).astype(BF16)
    low_grad = dot(mix_grad, v_turned_ref[...]).astype(BF16)
    in_grad = logit_grad * mixed_ref[...] + dot(low_grad, u_turned_ref[...])
    pre_grad = (in_grad[:, :EMB] * (sigma * (1.0 + pre_act * (1.0 - sigma)))).astype(BF16)
    for t in range(TABLES):
        embed_ref[t * samples : (t + 1) * samples, :] = in_grad[:, (t + 1) * EMB : (t + 2) * EMB].astype(BF16)
    embed_ref[TABLES * samples :, :] = dot(dense, pre_grad, 0, 0).astype(BF16)

    step = ALL_A // 2
    for c in range(ALL_A // step):
        rows = slice(c * step, (c + 1) * step)
        member_c = member_ref[rows, :]
        table_c = table_ref[rows, :]
        wide = [jnp.where(table_c == t, member_c, 0.0).astype(BF16) for t in range(TABLES)]
        wide = jnp.concatenate(wide + [wanted_ref[rows, :]], axis=1)
        out_ref[rows, :] = dot(wide, embed_ref[...]).astype(BF16)


def return_kernel(returned_ref, routed_ref, own_ref, one_ref, two_ref, three_ref, bottom_ref, grads_ref):
    returned = returned_ref[...]
    grads_ref[...] = dot(returned, routed_ref[...], 0, 0)
    cols = own_ref.shape[0]
    me = lax.axis_index("serve")
    for away, ref in enumerate((own_ref, one_ref, two_ref, three_ref)):
        start = lax.rem(me + away, 4) * cols
        ref[...] = grads_ref[pl.ds(pl.multiple_of(start, cols), cols), :].astype(BF16)
    slot = iota((8, ALL_A), 1)
    place = slot - divide_floor(slot, ROWS_A) * ROWS_A
    bottom_ref[...] = dot(onehot(place == iota((8, ALL_A), 0) + CAP), returned)


def total_kernel(own_ref, one_ref, two_ref, three_ref, bottom_ref, total_ref, message_ref):
    total = own_ref[...].astype(F32) + one_ref[...].astype(F32) + two_ref[...].astype(F32) + three_ref[...].astype(F32)
    total_ref[...] = total
    squares = jnp.sum(total * total, axis=0, keepdims=True)
    bottom = bottom_ref[...]
    message_ref[...] = jnp.concatenate([squares, bottom[0:1], bottom[1:2]], axis=1)


def step_kernel(
    own_ref, one_ref, two_ref, three_ref, total_ref, accum_ref, table_ref, steps_ref, block_ref, rows_ref, accum_out_ref, out_ref
):
    rows = accum_ref.shape[1]
    message = (own_ref[...] + two_ref[...]) + (one_ref[...] + three_ref[...])
    accum = accum_ref[...] + message[:, :rows] * (1.0 / EMB)
    accum_out_ref[...] = accum
    step = total_ref[...] * (1.0 / jnp.sqrt(accum))
    rows_ref[...] = table_ref[...] - LEARN_RATE * step
    block = block_ref[...]
    wide = jnp.concatenate([jnp.where(block == a, step, 0.0) for a in range(4)], axis=0).astype(BF16)
    payload = dot(steps_ref[...], wide, 1, 1)
    slot = iota((ALL_D, EMB), 0)
    place = slot - divide_floor(slot, ROWS_D) * ROWS_D
    payload = jnp.where(place == 4, message[:, rows : rows + EMB], payload)
    payload = jnp.where(place == 5, message[:, rows + EMB : rows + 2 * EMB], payload)
    out_ref[...] = payload.astype(BF16)


def final_kernel(served_ref, serving_ref, bottom_ref):
    served = served_ref[...]
    slot = iota((ALL_D, PEERS), 0)
    peer = iota((ALL_D, PEERS), 1)
    for r in range(4):
        pick = onehot(slot == peer * ROWS_D + r)
        serving_ref[r * EMB : (r + 1) * EMB, :] = dot(served, pick, 0, 0).astype(BF16)
    line = iota((2 * PEERS, ALL_D), 0)
    slot = iota((2 * PEERS, ALL_D), 1)
    pick = onehot(slot == lax.shift_right_logical(line, 1) * ROWS_D + 4 + (line & 1))
    bottom_ref[...] = dot(pick, served)


def call(kernel, outs, *args, scratch=(), flops=0, hbm=(), limit=VMEM_LIMIT):
    moved = sum(x.size * x.dtype.itemsize for x in args)
    spaces = [pltpu.HBM if i in hbm else pltpu.VMEM for i in range(len(args))]
    return pl.pallas_call(
        kernel,
        out_shape=[jax.ShapeDtypeStruct(shape, kind) for shape, kind in outs],
        in_specs=[pl.BlockSpec(memory_space=space) for space in spaces],
        scratch_shapes=list(scratch),
        compiler_params=pltpu.CompilerParams(vmem_limit_bytes=limit),
        cost_estimate=pl.CostEstimate(flops=flops, bytes_accessed=moved, transcendentals=0),
    )(*args)


def over_rows(chunks, rows):
    split = chunks.reshape(PEERS, rows // 2, 2, EMB)
    split = lax.all_to_all(split, "rows", split_axis=0, concat_axis=0, tiled=True)
    return split.reshape(PEERS * rows, EMB)


def over_serve(pieces):
    count = len(pieces)
    return pieces[:1] + [
        lax.ppermute(pieces[d], "serve", [(i, (i + d) % count) for i in range(count)]) for d in range(1, count)
    ]


def per_device(
    table_rows,
    row_accum,
    lookup_rows,
    bag_lengths,
    bag_owner,
    bag_target,
    bottom_in,
    labels,
    w_bottom,
    cross_u,
    cross_v,
    cross_bias,
    w_out,
    serve_owner,
):
    touched = table_rows.shape[0]
    lookups = lookup_rows.reshape(1, -1)
    lengths = bag_lengths.reshape(1, -1)
    bags = lengths.shape[1]
    owners = bag_owner.reshape(1, -1)
    targets = bag_target.reshape(1, -1)
    dense_in = bottom_in.reshape(-1, bottom_in.shape[-1])
    samples = dense_in.shape[0]
    width = cross_u.shape[0]
    serves = lax.axis_size("serve")
    cols = EMB // serves

    outgoing, counts, slots = call(
        pool_kernel,
        [((ALL_A, EMB), BF16), ((bags, touched), BF16), ((1, bags), jnp.int32)],
        lengths,
        lookups,
        owners,
        targets,
        table_rows,
        scratch=(
            pltpu.VMEM(lengths.shape, jnp.int32),
            pltpu.VMEM(lookups.shape, jnp.int32),
            pltpu.VMEM(owners.shape, jnp.int32),
            pltpu.VMEM(targets.shape, jnp.int32),
            pltpu.VMEM(table_rows.shape, F32),
            pltpu.SemaphoreType.DMA((5,)),
        ),
        flops=2 * 1100 * 10**6,
        hbm=range(5),
        limit=60 * 1024 * 1024,
    )
    arrived = over_rows(outgoing, ROWS_A)
    name_row, chunk, wanted, routed, steps_to, block, table_cols, u_turned, v_turned = call(
        ready_kernel,
        [
            ((PEERS, ALL_A), BF16),
            ((PEERS, ALL_A), BF16),
            ((ALL_A, 2 * PEERS), BF16),
            ((ALL_A, touched), BF16),
            ((ALL_D, touched), BF16),
            ((1, touched), jnp.int32),
            ((cols, touched), F32),
            (cross_u.shape[::-1], BF16),
            (cross_v.shape[::-1], BF16),
        ],
        counts,
        slots,
        serve_owner.reshape(1, -1),
        table_rows,
        cross_u,
        cross_v,
        scratch=(pltpu.VMEM((EMB, touched), F32),),
        flops=2 * 800 * 10**6,
    )
    (replies,) = call(
        owner_kernel,
        [((ALL_A, EMB), BF16)],
        arrived,
        name_row,
        chunk,
        wanted,
        dense_in,
        labels.reshape(-1, 1),
        w_bottom,
        cross_bias.reshape(1, -1),
        w_out.reshape(1, -1),
        cross_u,
        cross_v,
        u_turned,
        v_turned,
        scratch=(
            pltpu.VMEM((samples, width), BF16),
            pltpu.VMEM((samples, width), F32),
            pltpu.VMEM((samples * TABLES + 2 * PEERS, EMB), BF16),
            pltpu.VMEM((ALL_A, PEERS), BF16),
            pltpu.VMEM((ALL_A, PEERS), BF16),
        ),
        flops=2 * 1600 * 10**6,
    )
    returned = over_rows(replies, ROWS_A)
    *pieces, bottom = call(
        return_kernel,
        [((cols, touched), BF16)] * serves + [((8, EMB), F32)],
        returned,
        routed,
        scratch=(pltpu.VMEM((EMB, touched), F32),),
        flops=2 * 160 * 10**6,
    )
    pieces = over_serve(pieces)
    total, message = call(
        total_kernel, [((cols, touched), F32), ((1, touched + 2 * EMB), F32)], *pieces, bottom
    )
    messages = over_serve([message] * serves)
    new_rows, new_accum, steps = call(
        step_kernel,
        [((cols, touched), F32), ((1, touched), F32), ((ALL_D, EMB), BF16)],
        *messages,
        total,
        row_accum.reshape(1, -1),
        table_cols,
        steps_to,
        block,
        flops=2 * 100 * 10**6,
    )
    served = over_rows(steps, ROWS_D)
    serving, grad_bottom = call(
        final_kernel, [((4 * EMB, PEERS), BF16), ((2 * PEERS, EMB), F32)], served, flops=2 * 50 * 10**6
    )
    serving = serving.reshape(16, cols, PEERS).transpose(2, 0, 1)[None]
    return (new_rows.T, new_accum.reshape(-1), serving, grad_bottom)


def solution(mesh):
    return jax.shard_map(
        per_device,
        mesh=mesh,
        in_specs=(
            P("rows", None),
            P("rows"),
            P("serve", "rows", None),
            P("serve", "rows", None),
            P("serve", "rows", None, None),
            P("serve", "rows", None),
            P("serve", "rows", None),
            P("serve", "rows"),
            P(),
            P(),
            P(),
            P(),
            P(),
            P("rows", None),
        ),
        out_specs=(P("rows", "serve"), P("rows"), P("rows", None, None, "serve"), P()),
        check_vma=False,
    )
```

```python
import functools

import jax
import jax.numpy as jnp
from jax import lax
from jax.experimental import pallas as pl
from jax.experimental.pallas import tpu as pltpu
from jax.sharding import PartitionSpec as P

TABLES = 26
LEARN_RATE = 0.1
EMB = 128
PEERS = 128
CAP = 8
ROWS_A = 10
ALL_A = PEERS * ROWS_A
ROWS_D = 6
ALL_D = PEERS * ROWS_D
F32 = jnp.float32
BF16 = jnp.bfloat16
VMEM_LIMIT = 32 * 1024 * 1024


def dot(a, b, ca=1, cb=0):
    return lax.dot_general(a, b, (((ca,), (cb,)), ((), ())), preferred_element_type=F32)


def iota(shape, dim):
    return lax.broadcasted_iota(jnp.int32, shape, dim)


def onehot(mask):
    return jnp.where(mask, 1.0, 0.0).astype(BF16)


def divide_floor(values, by):
    return jnp.floor((values.astype(F32) + 0.5) * (1.0 / by)).astype(jnp.int32)


def owner_place(owners):
    return owners


def fetch(sources, targets, sems):
    copies = [pltpu.make_async_copy(s, t, sems.at[i]) for i, (s, t) in enumerate(zip(sources, targets))]
    for copy in copies:
        copy.start()
    return copies


def pool_kernel(
    lengths_hbm,
    lookups_hbm,
    owners_hbm,
    targets_hbm,
    table_hbm,
    out_ref,
    counts_ref,
    slots_ref,
    lengths_ref,
    lookups_ref,
    owners_ref,
    targets_ref,
    table_ref,
    sems,
):
    copies = fetch(
        (lengths_hbm, lookups_hbm, owners_hbm, targets_hbm, table_hbm),
        (lengths_ref, lookups_ref, owners_ref, targets_ref, table_ref),
        sems,
    )
    bags = lengths_ref.shape[1]
    looks = lookups_ref.shape[1]
    touched = table_ref.shape[0]
    row_id = iota((bags, bags), 0)
    col_id = iota((bags, bags), 1)
    place = iota((bags, looks), 1)
    for copy in copies[:4]:
        copy.wait()
    lens = jnp.broadcast_to(lengths_ref[...].astype(F32), (8, bags)).astype(BF16)
    starts = dot(onehot(col_id < row_id), lens, 1, 1)[:, 0:1].astype(jnp.int32)
    ends = dot(onehot(col_id <= row_id), lens, 1, 1)[:, 0:1].astype(jnp.int32)
    in_bag = onehot((place >= starts) & (place < ends))
    of_row = onehot(iota((touched, looks), 0) == lookups_ref[...])
    counts = dot(in_bag, of_row, 1, 1).astype(BF16)
    counts_ref[...] = counts
    copies[4].wait()
    table = table_ref[...]
    high = table.astype(BF16)
    low = (table - high.astype(F32)).astype(BF16)
    sums = dot(counts, jnp.concatenate([high, low], axis=1))
    pooled = (sums[:, :EMB] + sums[:, EMB:]).astype(BF16)
    owners = owners_ref[...]
    of_owner = jnp.where(iota((PEERS, bags), 0) == owners, 1.0, 0.0)
    before = dot(of_owner.astype(BF16), onehot(row_id < col_id))
    rank = jnp.sum(before * of_owner, axis=0, keepdims=True).astype(jnp.int32)
    first = owner_place(owners) * ROWS_A
    slots = first + rank
    slots_ref[...] = slots
    targets = targets_ref[...]
    sample = divide_floor(targets, TABLES)
    table_of = targets - sample * TABLES
    lane = iota((EMB, bags), 0)
    names = jnp.where(lane == rank, sample + 1, 0) + jnp.where(lane == rank + CAP, table_of, 0)
    slot_id = iota((ALL_A, bags), 0)
    payload = dot(onehot(slot_id == slots), pooled)
    payload = payload + dot(onehot(slot_id == first + CAP), names.astype(F32).astype(BF16), 1, 1)
    out_ref[...] = payload.astype(BF16)


def ready_kernel(
    counts_ref,
    slots_ref,
    owners_ref,
    table_ref,
    cross_u_ref,
    cross_v_ref,
    name_row_ref,
    chunk_ref,
    wanted_ref,
    routed_ref,
    steps_ref,
    block_ref,
    cols_ref,
    u_turned_ref,
    v_turned_ref,
    turned_ref,
):
    rows = owners_ref.shape[1]
    bags = slots_ref.shape[1]

    def block(index):
        return pl.ds(pl.multiple_of(index * 128, 128), 128)

    @pl.loop(0, ALL_A // 128)
    def _(i):
        first = i * 128
        peer = iota((PEERS, 128), 0) * ROWS_A
        slot = iota((PEERS, 128), 1) + first
        name_row_ref[:, block(i)] = onehot(slot == peer + CAP)
        chunk_ref[:, block(i)] = onehot((slot >= peer) & (slot < peer + ROWS_A))
        slot = iota((128, 2 * PEERS), 0) + first
        line = iota((128, 2 * PEERS), 1)
        wanted_ref[block(i), :] = onehot(slot == lax.shift_right_logical(line, 1) * ROWS_A + CAP + (line & 1))
        slot = iota((128, bags), 0) + first
        routed_ref[block(i), :] = dot(onehot(slot == slots_ref[...]), counts_ref[...]).astype(BF16)

    @pl.loop(0, rows // 128)
    def _(i):
        owners = owners_ref[:, block(i)]
        of_all = onehot(iota((PEERS, rows), 0) == owners_ref[...])
        before = dot(of_all, onehot(iota((rows, 128), 0) < iota((rows, 128), 1) + i * 128))
        of_owner = iota((PEERS, 128), 0) == owners
        rank = jnp.sum(jnp.where(of_owner, before, 0.0), axis=0, keepdims=True).astype(jnp.int32)
        row_of = lax.shift_right_logical(rank, 2)
        block_ref[:, block(i)] = rank - 4 * row_of
        steps_ref[:, block(i)] = onehot(iota((ALL_D, 128), 0) == owner_place(owners) * ROWS_D + row_of)
        turned_ref[:, block(i)] = table_ref[block(i), :].T

    @pl.loop(0, cross_u_ref.shape[0] // 128)
    def _(i):
        u_turned_ref[:, block(i)] = cross_u_ref[block(i), :].T
        v_turned_ref[block(i), :] = cross_v_ref[:, block(i)].T

    cols = cols_ref.shape[0]
    cols_ref[...] = turned_ref[pl.ds(pl.multiple_of(lax.axis_index("serve") * cols, cols), cols), :]


def owner_kernel(*refs):
    count = (len(refs) - 7) // 2
    sources, out_ref = refs[:count], refs[count]
    targets = refs[count + 1 : 2 * count + 1]
    cross_ref, mixed_ref, embed_ref, member_ref, table_ref, sems = refs[2 * count + 1 :]
    copies = fetch(sources, targets, sems)
    arrived_ref, name_row_ref, chunk_ref, dense_ref, w_bottom_ref, *late = targets
    cross_u_ref, bias_ref, w_out_ref, cross_v_ref, labels_ref, v_turned_ref, u_turned_ref, wanted_ref = late
    samples = dense_ref.shape[0]
    for copy in copies[:5]:
        copy.wait()
    arrived = arrived_ref[...]
    names = dot(name_row_ref[...], arrived).astype(BF16)
    spread = dot(names, chunk_ref[...], 0, 0)
    place = iota((CAP, ALL_A), 1)
    place = place - divide_floor(place, ROWS_A) * ROWS_A
    picks = iota((CAP, ALL_A), 0) == place
    sample_row = jnp.sum(jnp.where(picks, spread[:CAP], 0.0), axis=0, keepdims=True)
    table_row = jnp.sum(jnp.where(picks, spread[CAP : 2 * CAP], 0.0), axis=0, keepdims=True)
    member_f = jnp.where(sample_row.astype(jnp.int32) == iota((samples, ALL_A), 0) + 1, 1.0, 0.0)
    member = member_f.astype(BF16)
    member_ref[...] = member_f.T.astype(BF16)
    table_ref[...] = jnp.broadcast_to(table_row, (samples, ALL_A)).T.astype(BF16)

    dense = dense_ref[...]
    pre_act = dot(dense, w_bottom_ref[...])
    sigma = jax.nn.sigmoid(pre_act)
    cross_ref[:, :EMB] = (pre_act * sigma).astype(BF16)
    group = TABLES // 2
    for t in range(0, TABLES, group):
        both = jnp.concatenate([member * onehot(table_row == t + u) for u in range(group)], axis=0)
        embedded = dot(both, arrived).astype(BF16)
        for u in range(group):
            cross_ref[:, (t + u + 1) * EMB : (t + u + 2) * EMB] = embedded[u * samples : (u + 1) * samples]

    for copy in copies[5:]:
        copy.wait()
    low_rank = dot(cross_ref[...], cross_u_ref[...]).astype(BF16)
    w_out = w_out_ref[...]
    mixed_ref[...] = (dot(low_rank, cross_v_ref[...]) + (bias_ref[...] + 1.0)) * w_out
    cross_f = cross_ref[...].astype(F32)
    logits = jnp.sum(cross_f * mixed_ref[...], axis=1, keepdims=True)
    logit_grad = jax.nn.sigmoid(logits) - labels_ref[...].astype(F32)
    mix_grad = (logit_grad * w_out * cross_f).astype(BF16)
    low_grad = dot(mix_grad, v_turned_ref[...]).astype(BF16)
    in_grad = logit_grad * mixed_ref[...] + dot(low_grad, u_turned_ref[...])
    pre_grad = (in_grad[:, :EMB] * (sigma * (1.0 + pre_act * (1.0 - sigma)))).astype(BF16)
    for t in range(TABLES):
        embed_ref[t * samples : (t + 1) * samples, :] = in_grad[:, (t + 1) * EMB : (t + 2) * EMB].astype(BF16)
    embed_ref[TABLES * samples :, :] = dot(dense, pre_grad, 0, 0).astype(BF16)

    step = ALL_A // 2
    for c in range(ALL_A // step):
        rows = slice(c * step, (c + 1) * step)
        member_c = member_ref[rows, :]
        table_c = table_ref[rows, :]
        wide = [jnp.where(table_c == t, member_c, 0.0).astype(BF16) for t in range(TABLES)]
        wide = jnp.concatenate(wide + [wanted_ref[rows, :]], axis=1)
        out_ref[rows, :] = dot(wide, embed_ref[...]).astype(BF16)


def return_kernel(returned_ref, routed_ref, grads_ref, bottom_ref):
    returned = returned_ref[...]
    grads_ref[...] = dot(returned, routed_ref[...], 0, 0).astype(BF16)
    slot = iota((8, ALL_A), 1)
    place = slot - divide_floor(slot, ROWS_A) * ROWS_A
    bottom_ref[...] = dot(onehot(place == iota((8, ALL_A), 0) + CAP), returned)


def total_kernel(grads_ref, bottom_ref, total_ref, message_ref):
    total = grads_ref[0].astype(F32)
    for s in range(1, grads_ref.shape[0]):
        total = total + grads_ref[s].astype(F32)
    total_ref[...] = total
    squares = jnp.sum(total * total, axis=0, keepdims=True)
    bottom = bottom_ref[...]
    message = jnp.concatenate([squares, bottom[0:1], bottom[1:2]], axis=1)
    for s in range(message_ref.shape[0]):
        message_ref[s] = message


def step_kernel(
    message_ref, total_ref, accum_ref, table_ref, steps_ref, block_ref, rows_ref, accum_out_ref, out_ref
):
    rows = accum_ref.shape[1]
    message = message_ref[0]
    for s in range(1, message_ref.shape[0]):
        message = message + message_ref[s]
    accum = accum_ref[...] + message[:, :rows] * (1.0 / EMB)
    accum_out_ref[...] = accum
    step = total_ref[...] * (1.0 / jnp.sqrt(accum))
    rows_ref[...] = table_ref[...] - LEARN_RATE * step
    block = block_ref[...]
    wide = jnp.concatenate([jnp.where(block == a, step, 0.0) for a in range(4)], axis=0).astype(BF16)
    payload = dot(steps_ref[...], wide, 1, 1)
    slot = iota((ALL_D, EMB), 0)
    place = slot - divide_floor(slot, ROWS_D) * ROWS_D
    payload = jnp.where(place == 4, message[:, rows : rows + EMB], payload)
    payload = jnp.where(place == 5, message[:, rows + EMB : rows + 2 * EMB], payload)
    out_ref[...] = payload.astype(BF16)


def final_kernel(served_ref, serving_ref, bottom_ref):
    served = served_ref[...]
    slot = iota((ALL_D, PEERS), 0)
    peer = iota((ALL_D, PEERS), 1)
    for r in range(4):
        pick = onehot(slot == peer * ROWS_D + r)
        serving_ref[r * EMB : (r + 1) * EMB, :] = dot(served, pick, 0, 0).astype(BF16)
    line = iota((2 * PEERS, ALL_D), 0)
    slot = iota((2 * PEERS, ALL_D), 1)
    pick = onehot(slot == lax.shift_right_logical(line, 1) * ROWS_D + 4 + (line & 1))
    bottom_ref[...] = dot(pick, served)


def call(kernel, outs, *args, scratch=(), flops=0, hbm=(), limit=VMEM_LIMIT):
    moved = sum(x.size * x.dtype.itemsize for x in args)
    spaces = [pltpu.HBM if i in hbm else pltpu.VMEM for i in range(len(args))]
    return pl.pallas_call(
        kernel,
        out_shape=[jax.ShapeDtypeStruct(shape, kind) for shape, kind in outs],
        in_specs=[pl.BlockSpec(memory_space=space) for space in spaces],
        scratch_shapes=list(scratch),
        compiler_params=pltpu.CompilerParams(vmem_limit_bytes=limit),
        cost_estimate=pl.CostEstimate(flops=flops, bytes_accessed=moved, transcendentals=0),
    )(*args)


def over_rows(chunks, rows):
    split = chunks.reshape(PEERS, rows // 2, 2, EMB)
    split = lax.all_to_all(split, "rows", split_axis=0, concat_axis=0, tiled=True)
    return split.reshape(PEERS * rows, EMB)


def over_serve(pieces):
    return lax.all_to_all(pieces, "serve", split_axis=0, concat_axis=0, tiled=True)


def per_device(
    table_rows,
    row_accum,
    lookup_rows,
    bag_lengths,
    bag_owner,
    bag_target,
    bottom_in,
    labels,
    w_bottom,
    cross_u,
    cross_v,
    cross_bias,
    w_out,
    serve_owner,
):
    touched = table_rows.shape[0]
    lookups = lookup_rows.reshape(1, -1)
    lengths = bag_lengths.reshape(1, -1)
    bags = lengths.shape[1]
    owners = bag_owner.reshape(1, -1)
    targets = bag_target.reshape(1, -1)
    dense_in = bottom_in.reshape(-1, bottom_in.shape[-1])
    samples = dense_in.shape[0]
    width = cross_u.shape[0]
    serves = lax.axis_size("serve")
    cols = EMB // serves

    outgoing, counts, slots = call(
        pool_kernel,
        [((ALL_A, EMB), BF16), ((bags, touched), BF16), ((1, bags), jnp.int32)],
        lengths,
        lookups,
        owners,
        targets,
        table_rows,
        scratch=(
            pltpu.VMEM(lengths.shape, jnp.int32),
            pltpu.VMEM(lookups.shape, jnp.int32),
            pltpu.VMEM(owners.shape, jnp.int32),
            pltpu.VMEM(targets.shape, jnp.int32),
            pltpu.VMEM(table_rows.shape, F32),
            pltpu.SemaphoreType.DMA((5,)),
        ),
        flops=2 * 1100 * 10**6,
        hbm=range(5),
        limit=60 * 1024 * 1024,
    )
    arrived = over_rows(outgoing, ROWS_A)
    name_row, chunk, wanted, routed, steps_to, block, table_cols, u_turned, v_turned = call(
        ready_kernel,
        [
            ((PEERS, ALL_A), BF16),
            ((PEERS, ALL_A), BF16),
            ((ALL_A, 2 * PEERS), BF16),
            ((ALL_A, touched), BF16),
            ((ALL_D, touched), BF16),
            ((1, touched), jnp.int32),
            ((cols, touched), F32),
            (cross_u.shape[::-1], BF16),
            (cross_v.shape[::-1], BF16),
        ],
        counts,
        slots,
        serve_owner.reshape(1, -1),
        table_rows,
        cross_u,
        cross_v,
        scratch=(pltpu.VMEM((EMB, touched), F32),),
        flops=2 * 800 * 10**6,
        limit=60 * 1024 * 1024,
    )
    operands = (
        arrived,
        name_row,
        chunk,
        dense_in,
        w_bottom,
        cross_u,
        cross_bias.reshape(1, -1),
        w_out.reshape(1, -1),
        cross_v,
        labels.reshape(-1, 1),
        v_turned,
        u_turned,
        wanted,
    )
    (replies,) = call(
        owner_kernel,
        [((ALL_A, EMB), BF16)],
        *operands,
        scratch=tuple(pltpu.VMEM(x.shape, x.dtype) for x in operands)
        + (
            pltpu.VMEM((samples, width), BF16),
            pltpu.VMEM((samples, width), F32),
            pltpu.VMEM((samples * TABLES + 2 * PEERS, EMB), BF16),
            pltpu.VMEM((ALL_A, PEERS), BF16),
            pltpu.VMEM((ALL_A, PEERS), BF16),
            pltpu.SemaphoreType.DMA((len(operands),)),
        ),
        flops=2 * 1600 * 10**6,
        hbm=range(len(operands)),
        limit=60 * 1024 * 1024,
    )
    returned = over_rows(replies, ROWS_A)
    grads, bottom = call(
        return_kernel,
        [((EMB, touched), BF16), ((8, EMB), F32)],
        returned,
        routed,
        flops=2 * 160 * 10**6,
    )
    pieces = over_serve(grads.reshape(serves, cols, touched))
    total, message = call(
        total_kernel,
        [((cols, touched), F32), ((serves, 1, touched + 2 * EMB), F32)],
        pieces,
        bottom,
    )
    messages = over_serve(message)
    new_rows, new_accum, steps = call(
        step_kernel,
        [((cols, touched), F32), ((1, touched), F32), ((ALL_D, EMB), BF16)],
        messages,
        total,
        row_accum.reshape(1, -1),
        table_cols,
        steps_to,
        block,
        flops=2 * 100 * 10**6,
    )
    served = over_rows(steps, ROWS_D)
    serving, grad_bottom = call(
        final_kernel, [((4 * EMB, PEERS), BF16), ((2 * PEERS, EMB), F32)], served, flops=2 * 50 * 10**6
    )
    serving = serving.reshape(16, cols, PEERS).transpose(2, 0, 1)[None]
    return (new_rows.T, new_accum.reshape(-1), serving, grad_bottom)


def solution(mesh):
    return jax.shard_map(
        per_device,
        mesh=mesh,
        in_specs=(
            P("rows", None),
            P("rows"),
            P("serve", "rows", None),
            P("serve", "rows", None),
            P("serve", "rows", None, None),
            P("serve", "rows", None),
            P("serve", "rows", None),
            P("serve", "rows"),
            P(),
            P(),
            P(),
            P(),
            P(),
            P("rows", None),
        ),
        out_specs=(P("rows", "serve"), P("rows"), P("rows", None, None, "serve"), P()),
        check_vma=False,
    )
```

```python
import functools

import jax
import jax.numpy as jnp
from jax import lax
from jax.experimental import pallas as pl
from jax.experimental.pallas import tpu as pltpu
from jax.sharding import PartitionSpec as P

TABLES = 26
LEARN_RATE = 0.1
EMB = 128
PEERS = 128
CAP = 8
ROWS_A = 10
ALL_A = PEERS * ROWS_A
ROWS_D = 6
ALL_D = PEERS * ROWS_D
F32 = jnp.float32
BF16 = jnp.bfloat16
VMEM_LIMIT = 32 * 1024 * 1024


def dot(a, b, ca=1, cb=0):
    return lax.dot_general(a, b, (((ca,), (cb,)), ((), ())), preferred_element_type=F32)


def iota(shape, dim):
    return lax.broadcasted_iota(jnp.int32, shape, dim)


def onehot(mask):
    return jnp.where(mask, 1.0, 0.0).astype(BF16)


def divide_floor(values, by):
    return jnp.floor((values.astype(F32) + 0.5) * (1.0 / by)).astype(jnp.int32)


def owner_place(owners):
    return owners


def fetch(sources, targets, sems):
    copies = [pltpu.make_async_copy(s, t, sems.at[i]) for i, (s, t) in enumerate(zip(sources, targets))]
    for copy in copies:
        copy.start()
    return copies


def bag_ends(lengths_ref):
    bags = lengths_ref.shape[1]
    row_id = iota((bags, bags), 0)
    col_id = iota((bags, bags), 1)
    lens = jnp.broadcast_to(lengths_ref[...].astype(F32), (8, bags)).astype(BF16)
    starts = dot(onehot(col_id < row_id), lens, 1, 1)[:, 0:1].astype(jnp.int32)
    ends = dot(onehot(col_id <= row_id), lens, 1, 1)[:, 0:1].astype(jnp.int32)
    return starts, ends


def pool_kernel(
    lengths_hbm,
    lookups_hbm,
    owners_hbm,
    targets_hbm,
    table_hbm,
    out_ref,
    slots_ref,
    lengths_ref,
    lookups_ref,
    owners_ref,
    targets_ref,
    table_ref,
    sems,
):
    copies = fetch(
        (lengths_hbm, lookups_hbm, owners_hbm, targets_hbm, table_hbm),
        (lengths_ref, lookups_ref, owners_ref, targets_ref, table_ref),
        sems,
    )
    bags = lengths_ref.shape[1]
    looks = lookups_ref.shape[1]
    touched = table_ref.shape[0]
    for copy in copies[:4]:
        copy.wait()
    owners = owners_ref[...]
    of_owner = jnp.where(iota((PEERS, bags), 0) == owners, 1.0, 0.0)
    before = dot(of_owner.astype(BF16), onehot(iota((bags, bags), 0) < iota((bags, bags), 1)))
    rank = jnp.sum(before * of_owner, axis=0, keepdims=True).astype(jnp.int32)
    slots = owner_place(owners) * ROWS_A + rank
    slots_ref[...] = slots
    targets = targets_ref[...]
    sample = divide_floor(targets, TABLES)
    table_of = targets - sample * TABLES
    lane = iota((EMB, bags), 0)
    names = jnp.where(lane == rank, sample + 1, 0) + jnp.where(lane == rank + CAP, table_of, 0)
    names = dot(of_owner.astype(BF16), names.astype(F32).astype(BF16), 1, 1).astype(BF16)
    copies[4].wait()
    table = table_ref[...]
    high = table.astype(BF16)
    low = (table - high.astype(F32)).astype(BF16)
    starts, ends = bag_ends(lengths_ref)
    place = iota((bags, looks), 1)
    in_bag = onehot((place >= starts) & (place < ends))
    lookups = jnp.broadcast_to(lookups_ref[...].astype(F32), (128, looks)).T.astype(jnp.int32)
    both = jnp.concatenate([high, low], axis=1)
    lane = iota((512, 128), 1)
    sums = 0.0
    for first in range(0, looks, 512):
        part = lookups[first : first + 512]
        goes = jnp.concatenate([onehot(part == lane + c) for c in range(0, touched, 128)], axis=1)
        sums = sums + dot(in_bag[:, first : first + 512], dot(goes, both).astype(BF16))
    pooled = (sums[:, :EMB] + sums[:, EMB:]).astype(BF16)
    payload = dot(onehot(iota((ALL_A, bags), 0) == slots), pooled)
    ninth = onehot(iota((ALL_A, PEERS), 0) == owner_place(iota((ALL_A, PEERS), 1)) * ROWS_A + CAP)
    out_ref[...] = (payload + dot(ninth, names)).astype(BF16)


def ready_kernel(
    lengths_ref,
    lookups_ref,
    slots_ref,
    owners_ref,
    table_ref,
    cross_u_ref,
    cross_v_ref,
    routed_ref,
    steps_ref,
    block_ref,
    cols_ref,
    u_turned_ref,
    v_turned_ref,
    turned_ref,
):
    rows = owners_ref.shape[1]
    bags = slots_ref.shape[1]
    looks = lookups_ref.shape[1]
    u_turned_ref[...] = cross_u_ref[...].T
    v_turned_ref[...] = cross_v_ref[...].T
    starts, ends = bag_ends(lengths_ref)
    place = iota((bags, looks), 1)
    in_bag = onehot((place >= starts) & (place < ends))
    of_row = onehot(iota((rows, looks), 0) == lookups_ref[...])
    counts = dot(in_bag, of_row, 1, 1).astype(BF16)
    routed_ref[...] = dot(onehot(iota((ALL_A, bags), 0) == slots_ref[...]), counts).astype(BF16)
    owners = owners_ref[...]
    of_owner = jnp.where(iota((PEERS, rows), 0) == owners, 1.0, 0.0)
    before = dot(of_owner.astype(BF16), onehot(iota((rows, rows), 0) < iota((rows, rows), 1)))
    rank = jnp.sum(before * of_owner, axis=0, keepdims=True).astype(jnp.int32)
    row_of = lax.shift_right_logical(rank, 2)
    block_ref[...] = rank - 4 * row_of
    steps_ref[...] = onehot(iota((ALL_D, rows), 0) == owner_place(owners) * ROWS_D + row_of)
    turned_ref[...] = table_ref[...].T
    cols = cols_ref.shape[0]
    cols_ref[...] = turned_ref[pl.ds(pl.multiple_of(lax.axis_index("serve") * cols, cols), cols), :]


def owner_kernel(*refs):
    arrived_ref, *refs = refs
    count = (len(refs) - 8) // 2
    sources, out_ref = refs[:count], refs[count]
    targets = refs[count + 1 : 2 * count + 1]
    cross_ref, mixed_ref, embed_ref, member_ref, table_ref, wanted_ref, sems = refs[2 * count + 1 :]
    copies = fetch(sources, targets, sems)
    dense_ref, w_bottom_ref, cross_u_ref, bias_ref, w_out_ref, cross_v_ref, *late = targets
    labels_ref, v_turned_ref, u_turned_ref = late
    samples = dense_ref.shape[0]
    peer = iota((PEERS, ALL_A), 0) * ROWS_A
    slot = iota((PEERS, ALL_A), 1)
    name_row = onehot(slot == peer + CAP)
    chunk = onehot((slot >= peer) & (slot < peer + ROWS_A))
    arrived = arrived_ref[...]
    names = dot(name_row, arrived).astype(BF16)
    spread = dot(names, chunk, 0, 0)
    place = iota((CAP, ALL_A), 1)
    place = place - divide_floor(place, ROWS_A) * ROWS_A
    picks = iota((CAP, ALL_A), 0) == place
    sample_row = jnp.sum(jnp.where(picks, spread[:CAP], 0.0), axis=0, keepdims=True)
    table_row = jnp.sum(jnp.where(picks, spread[CAP : 2 * CAP], 0.0), axis=0, keepdims=True)
    member_f = jnp.where(sample_row.astype(jnp.int32) == iota((samples, ALL_A), 0) + 1, 1.0, 0.0)
    member = member_f.astype(BF16)
    member_ref[...] = member_f.T.astype(BF16)
    table_ref[...] = jnp.broadcast_to(table_row, (samples, ALL_A)).T.astype(BF16)

    for copy in copies[:2]:
        copy.wait()
    dense = dense_ref[...]
    pre_act = dot(dense, w_bottom_ref[...])
    sigma = jax.nn.sigmoid(pre_act)
    cross_ref[:, :EMB] = (pre_act * sigma).astype(BF16)
    table_t = table_ref[...]
    for t in range(0, TABLES, 2):
        both = [jnp.where(table_t == t + u, arrived, 0.0).astype(BF16) for u in range(2)]
        cross_ref[:, (t + 1) * EMB : (t + 3) * EMB] = dot(member, jnp.concatenate(both, axis=1)).astype(BF16)

    for copy in copies[2:5]:
        copy.wait()
    low_rank = dot(cross_ref[...], cross_u_ref[...]).astype(BF16)
    copies[5].wait()
    w_out = w_out_ref[...]
    mixed_ref[...] = (dot(low_rank, cross_v_ref[...]) + (bias_ref[...] + 1.0)) * w_out
    cross_f = cross_ref[...].astype(F32)
    logits = jnp.sum(cross_f * mixed_ref[...], axis=1, keepdims=True)
    for copy in copies[6:8]:
        copy.wait()
    logit_grad = jax.nn.sigmoid(logits) - labels_ref[...].astype(F32)
    mix_grad = (logit_grad * w_out * cross_f).astype(BF16)
    low_grad = dot(mix_grad, v_turned_ref[...]).astype(BF16)
    copies[8].wait()
    in_grad = logit_grad * mixed_ref[...] + dot(low_grad, u_turned_ref[...])
    pre_grad = (in_grad[:, :EMB] * (sigma * (1.0 + pre_act * (1.0 - sigma)))).astype(BF16)
    for t in range(TABLES):
        embed_ref[t * samples : (t + 1) * samples, :] = in_grad[:, (t + 1) * EMB : (t + 2) * EMB].astype(BF16)
    line = iota((1, 2 * PEERS), 1)
    line = lax.shift_right_logical(line, 1) * ROWS_A + CAP + (line & 1)
    wanted_ref[...] = onehot(iota((ALL_A, 2 * PEERS), 0) == line)
    embed_ref[TABLES * samples :, :] = dot(dense, pre_grad, 0, 0).astype(BF16)

    step = ALL_A // 2
    for c in range(ALL_A // step):
        rows = slice(c * step, (c + 1) * step)
        member_c = member_ref[rows, :]
        table_c = table_ref[rows, :]
        wide = [jnp.where(table_c == t, member_c, 0.0).astype(BF16) for t in range(TABLES)]
        wide = jnp.concatenate(wide + [wanted_ref[rows, :]], axis=1)
        out_ref[rows, :] = dot(wide, embed_ref[...]).astype(BF16)


def return_kernel(returned_ref, routed_ref, grads_ref, bottom_ref):
    returned = returned_ref[...]
    grads_ref[...] = dot(returned, routed_ref[...], 0, 0).astype(BF16)
    slot = iota((8, ALL_A), 1)
    place = slot - divide_floor(slot, ROWS_A) * ROWS_A
    bottom_ref[...] = dot(onehot(place == iota((8, ALL_A), 0) + CAP), returned)


def total_kernel(grads_ref, bottom_ref, total_ref, message_ref):
    total = grads_ref[0].astype(F32)
    for s in range(1, grads_ref.shape[0]):
        total = total + grads_ref[s].astype(F32)
    total_ref[...] = total
    squares = jnp.sum(total * total, axis=0, keepdims=True)
    bottom = bottom_ref[...]
    message = jnp.concatenate([squares, bottom[0:1], bottom[1:2]], axis=1)
    for s in range(message_ref.shape[0]):
        message_ref[s] = message


def step_kernel(
    message_ref, total_ref, accum_ref, table_ref, steps_ref, block_ref, rows_ref, accum_out_ref, out_ref
):
    rows = accum_ref.shape[1]
    message = message_ref[0]
    for s in range(1, message_ref.shape[0]):
        message = message + message_ref[s]
    accum = accum_ref[...] + message[:, :rows] * (1.0 / EMB)
    accum_out_ref[...] = accum
    step = total_ref[...] * (1.0 / jnp.sqrt(accum))
    rows_ref[...] = table_ref[...] - LEARN_RATE * step
    block = block_ref[...]
    wide = jnp.concatenate([jnp.where(block == a, step, 0.0) for a in range(4)], axis=0).astype(BF16)
    payload = dot(steps_ref[...], wide, 1, 1)
    slot = iota((ALL_D, EMB), 0)
    place = slot - divide_floor(slot, ROWS_D) * ROWS_D
    payload = jnp.where(place == 4, message[:, rows : rows + EMB], payload)
    payload = jnp.where(place == 5, message[:, rows + EMB : rows + 2 * EMB], payload)
    out_ref[...] = payload.astype(BF16)


def final_kernel(served_ref, serving_ref, bottom_ref):
    served = served_ref[...]
    slot = iota((ALL_D, PEERS), 0)
    peer = iota((ALL_D, PEERS), 1)
    for r in range(4):
        pick = onehot(slot == peer * ROWS_D + r)
        serving_ref[r * EMB : (r + 1) * EMB, :] = dot(served, pick, 0, 0).astype(BF16)
    line = iota((2 * PEERS, ALL_D), 0)
    slot = iota((2 * PEERS, ALL_D), 1)
    pick = onehot(slot == lax.shift_right_logical(line, 1) * ROWS_D + 4 + (line & 1))
    bottom_ref[...] = dot(pick, served)


def call(kernel, outs, *args, scratch=(), flops=0, hbm=(), limit=VMEM_LIMIT):
    moved = sum(x.size * x.dtype.itemsize for x in args)
    spaces = [pltpu.HBM if i in hbm else pltpu.VMEM for i in range(len(args))]
    return pl.pallas_call(
        kernel,
        out_shape=[jax.ShapeDtypeStruct(shape, kind) for shape, kind in outs],
        in_specs=[pl.BlockSpec(memory_space=space) for space in spaces],
        scratch_shapes=list(scratch),
        compiler_params=pltpu.CompilerParams(vmem_limit_bytes=limit),
        cost_estimate=pl.CostEstimate(flops=flops, bytes_accessed=moved, transcendentals=0),
    )(*args)


def over_rows(chunks, rows):
    split = chunks.reshape(PEERS, rows // 2, 2, EMB)
    split = lax.all_to_all(split, "rows", split_axis=0, concat_axis=0, tiled=True)
    return split.reshape(PEERS * rows, EMB)


def over_serve(pieces):
    return lax.all_to_all(pieces, "serve", split_axis=0, concat_axis=0, tiled=True)


def per_device(
    table_rows,
    row_accum,
    lookup_rows,
    bag_lengths,
    bag_owner,
    bag_target,
    bottom_in,
    labels,
    w_bottom,
    cross_u,
    cross_v,
    cross_bias,
    w_out,
    serve_owner,
):
    touched = table_rows.shape[0]
    lookups = lookup_rows.reshape(1, -1)
    lengths = bag_lengths.reshape(1, -1)
    bags = lengths.shape[1]
    owners = bag_owner.reshape(1, -1)
    targets = bag_target.reshape(1, -1)
    dense_in = bottom_in.reshape(-1, bottom_in.shape[-1])
    samples = dense_in.shape[0]
    width = cross_u.shape[0]
    serves = lax.axis_size("serve")
    cols = EMB // serves

    outgoing, slots = call(
        pool_kernel,
        [((ALL_A, EMB), BF16), ((1, bags), jnp.int32)],
        lengths,
        lookups,
        owners,
        targets,
        table_rows,
        scratch=(
            pltpu.VMEM(lengths.shape, jnp.int32),
            pltpu.VMEM(lookups.shape, jnp.int32),
            pltpu.VMEM(owners.shape, jnp.int32),
            pltpu.VMEM(targets.shape, jnp.int32),
            pltpu.VMEM(table_rows.shape, F32),
            pltpu.SemaphoreType.DMA((5,)),
        ),
        flops=2 * 700 * 10**6,
        hbm=range(5),
        limit=60 * 1024 * 1024,
    )
    arrived = over_rows(outgoing, ROWS_A)
    routed, steps_to, block, table_cols, u_turned, v_turned = call(
        ready_kernel,
        [
            ((ALL_A, touched), BF16),
            ((ALL_D, touched), BF16),
            ((1, touched), jnp.int32),
            ((cols, touched), F32),
            (cross_u.shape[::-1], BF16),
            (cross_v.shape[::-1], BF16),
        ],
        lengths,
        lookups,
        slots,
        serve_owner.reshape(1, -1),
        table_rows,
        cross_u,
        cross_v,
        scratch=(pltpu.VMEM((EMB, touched), F32),),
        flops=2 * 1600 * 10**6,
        limit=60 * 1024 * 1024,
    )
    operands = (
        arrived,
        dense_in,
        w_bottom,
        cross_u,
        cross_bias.reshape(1, -1),
        w_out.reshape(1, -1),
        cross_v,
        labels.reshape(-1, 1),
        v_turned,
        u_turned,
    )
    (replies,) = call(
        owner_kernel,
        [((ALL_A, EMB), BF16)],
        *operands,
        scratch=tuple(pltpu.VMEM(x.shape, x.dtype) for x in operands[1:])
        + (
            pltpu.VMEM((samples, width), BF16),
            pltpu.VMEM((samples, width), F32),
            pltpu.VMEM((samples * TABLES + 2 * PEERS, EMB), BF16),
            pltpu.VMEM((ALL_A, PEERS), BF16),
            pltpu.VMEM((ALL_A, PEERS), BF16),
            pltpu.VMEM((ALL_A, 2 * PEERS), BF16),
            pltpu.SemaphoreType.DMA((len(operands) - 1,)),
        ),
        flops=2 * 1600 * 10**6,
        hbm=range(1, len(operands)),
        limit=59 * 1024 * 1024,
    )
    returned = over_rows(replies, ROWS_A)
    grads, bottom = call(
        return_kernel,
        [((EMB, touched), BF16), ((8, EMB), F32)],
        returned,
        routed,
        flops=2 * 160 * 10**6,
    )
    pieces = over_serve(grads.reshape(serves, cols, touched))
    total, message = call(
        total_kernel,
        [((cols, touched), F32), ((serves, 1, touched + 2 * EMB), F32)],
        pieces,
        bottom,
    )
    messages = over_serve(message)
    new_rows, new_accum, steps = call(
        step_kernel,
        [((cols, touched), F32), ((1, touched), F32), ((ALL_D, EMB), BF16)],
        messages,
        total,
        row_accum.reshape(1, -1),
        table_cols,
        steps_to,
        block,
        flops=2 * 100 * 10**6,
    )
    served = over_rows(steps, ROWS_D)
    serving, grad_bottom = call(
        final_kernel, [((4 * EMB, PEERS), BF16), ((2 * PEERS, EMB), F32)], served, flops=2 * 50 * 10**6
    )
    serving = serving.reshape(16, cols, PEERS).transpose(2, 0, 1)[None]
    return (new_rows.T, new_accum.reshape(-1), serving, grad_bottom)


def solution(mesh):
    return jax.shard_map(
        per_device,
        mesh=mesh,
        in_specs=(
            P("rows", None),
            P("rows"),
            P("serve", "rows", None),
            P("serve", "rows", None),
            P("serve", "rows", None, None),
            P("serve", "rows", None),
            P("serve", "rows", None),
            P("serve", "rows"),
            P(),
            P(),
            P(),
            P(),
            P(),
            P("rows", None),
        ),
        out_specs=(P("rows", "serve"), P("rows"), P("rows", None, None, "serve"), P()),
        check_vma=False,
    )
```

```python
import functools

import jax
import jax.numpy as jnp
from jax import lax
from jax.experimental import pallas as pl
from jax.experimental.pallas import tpu as pltpu
from jax.sharding import PartitionSpec as P

TABLES = 26
LEARN_RATE = 0.1
EMB = 128
PEERS = 128
CAP = 8
ROWS_A = 10
ALL_A = PEERS * ROWS_A
ROWS_D = 6
ALL_D = PEERS * ROWS_D
F32 = jnp.float32
BF16 = jnp.bfloat16
VMEM_LIMIT = 32 * 1024 * 1024


def dot(a, b, ca=1, cb=0):
    return lax.dot_general(a, b, (((ca,), (cb,)), ((), ())), preferred_element_type=F32)


def iota(shape, dim):
    return lax.broadcasted_iota(jnp.int32, shape, dim)


def onehot(mask):
    return jnp.where(mask, 1.0, 0.0).astype(BF16)


def divide_floor(values, by):
    return jnp.floor((values.astype(F32) + 0.5) * (1.0 / by)).astype(jnp.int32)


def owner_place(owners):
    return owners


def fetch(sources, targets, sems):
    copies = [pltpu.make_async_copy(s, t, sems.at[i]) for i, (s, t) in enumerate(zip(sources, targets))]
    for copy in copies:
        copy.start()
    return copies


def bag_ends(lengths_ref):
    bags = lengths_ref.shape[1]
    row_id = iota((bags, bags), 0)
    col_id = iota((bags, bags), 1)
    lens = jnp.broadcast_to(lengths_ref[...].astype(F32), (8, bags)).astype(BF16)
    starts = dot(onehot(col_id < row_id), lens, 1, 1)[:, 0:1].astype(jnp.int32)
    ends = dot(onehot(col_id <= row_id), lens, 1, 1)[:, 0:1].astype(jnp.int32)
    return starts, ends


def pool_kernel(
    lengths_hbm,
    lookups_hbm,
    owners_hbm,
    targets_hbm,
    table_hbm,
    out_ref,
    slots_ref,
    lengths_ref,
    lookups_ref,
    owners_ref,
    targets_ref,
    table_ref,
    sems,
):
    copies = fetch(
        (lengths_hbm, lookups_hbm, owners_hbm, targets_hbm, table_hbm),
        (lengths_ref, lookups_ref, owners_ref, targets_ref, table_ref),
        sems,
    )
    bags = lengths_ref.shape[1]
    looks = lookups_ref.shape[1]
    touched = table_ref.shape[0]
    for copy in copies[:4]:
        copy.wait()
    owners = owners_ref[...]
    of_owner = jnp.where(iota((PEERS, bags), 0) == owners, 1.0, 0.0)
    before = dot(of_owner.astype(BF16), onehot(iota((bags, bags), 0) < iota((bags, bags), 1)))
    rank = jnp.sum(before * of_owner, axis=0, keepdims=True).astype(jnp.int32)
    slots = owner_place(owners) * ROWS_A + rank
    slots_ref[...] = slots
    targets = targets_ref[...]
    sample = divide_floor(targets, TABLES)
    table_of = targets - sample * TABLES
    lane = iota((EMB, bags), 0)
    names = jnp.where(lane == rank, sample + 1, 0) + jnp.where(lane == rank + CAP, table_of, 0)
    names = dot(of_owner.astype(BF16), names.astype(F32).astype(BF16), 1, 1).astype(BF16)
    copies[4].wait()
    table = table_ref[...]
    high = table.astype(BF16)
    low = (table - high.astype(F32)).astype(BF16)
    starts, ends = bag_ends(lengths_ref)
    place = iota((bags, looks), 1)
    in_bag = onehot((place >= starts) & (place < ends))
    lookups = jnp.broadcast_to(lookups_ref[...].astype(F32), (128, looks)).T.astype(jnp.int32)
    both = jnp.concatenate([high, low], axis=1)
    lane = iota((512, 128), 1)
    sums = 0.0
    for first in range(0, looks, 512):
        part = lookups[first : first + 512]
        goes = jnp.concatenate([onehot(part == lane + c) for c in range(0, touched, 128)], axis=1)
        sums = sums + dot(in_bag[:, first : first + 512], dot(goes, both).astype(BF16))
    pooled = (sums[:, :EMB] + sums[:, EMB:]).astype(BF16)
    payload = dot(onehot(iota((ALL_A, bags), 0) == slots), pooled)
    ninth = onehot(iota((ALL_A, PEERS), 0) == owner_place(iota((ALL_A, PEERS), 1)) * ROWS_A + CAP)
    out_ref[...] = (payload + dot(ninth, names)).astype(BF16)


def ready_kernel(
    lengths_ref,
    lookups_ref,
    slots_ref,
    owners_ref,
    table_ref,
    cross_u_ref,
    routed_ref,
    steps_ref,
    block_ref,
    cols_ref,
    u_turned_ref,
    turned_ref,
):
    rows = owners_ref.shape[1]
    bags = slots_ref.shape[1]
    looks = lookups_ref.shape[1]
    u_turned_ref[...] = cross_u_ref[...].T
    starts, ends = bag_ends(lengths_ref)
    place = iota((bags, looks), 1)
    in_bag = onehot((place >= starts) & (place < ends))
    of_row = onehot(iota((rows, looks), 0) == lookups_ref[...])
    counts = dot(in_bag, of_row, 1, 1).astype(BF16)
    routed_ref[...] = dot(onehot(iota((ALL_A, bags), 0) == slots_ref[...]), counts).astype(BF16)
    owners = owners_ref[...]
    of_owner = jnp.where(iota((PEERS, rows), 0) == owners, 1.0, 0.0)
    before = dot(of_owner.astype(BF16), onehot(iota((rows, rows), 0) < iota((rows, rows), 1)))
    rank = jnp.sum(before * of_owner, axis=0, keepdims=True).astype(jnp.int32)
    row_of = lax.shift_right_logical(rank, 2)
    block_ref[...] = rank - 4 * row_of
    steps_ref[...] = onehot(iota((ALL_D, rows), 0) == owner_place(owners) * ROWS_D + row_of)
    turned_ref[...] = table_ref[...].T
    cols = cols_ref.shape[0]
    cols_ref[...] = turned_ref[pl.ds(pl.multiple_of(lax.axis_index("serve") * cols, cols), cols), :]


def owner_kernel(*refs):
    arrived_ref, *refs = refs
    count = (len(refs) - 8) // 2
    sources, out_ref = refs[:count], refs[count]
    targets = refs[count + 1 : 2 * count + 1]
    cross_ref, mixed_ref, embed_ref, member_ref, table_ref, wanted_ref, sems = refs[2 * count + 1 :]
    copies = [pltpu.make_async_copy(s, t, sems.at[i]) for i, (s, t) in enumerate(zip(sources, targets))]
    dense_ref, w_bottom_ref, cross_u_ref, bias_ref, w_out_ref, labels_ref, cross_v_ref, u_turned_ref = targets
    for copy in copies[:7]:
        copy.start()
    samples = dense_ref.shape[0]
    peer = iota((PEERS, ALL_A), 0) * ROWS_A
    slot = iota((PEERS, ALL_A), 1)
    name_row = onehot(slot == peer + CAP)
    chunk = onehot((slot >= peer) & (slot < peer + ROWS_A))
    arrived = arrived_ref[...]
    names = dot(name_row, arrived).astype(BF16)
    spread = dot(names, chunk, 0, 0)
    place = iota((CAP, ALL_A), 1)
    place = place - divide_floor(place, ROWS_A) * ROWS_A
    picks = iota((CAP, ALL_A), 0) == place
    sample_row = jnp.sum(jnp.where(picks, spread[:CAP], 0.0), axis=0, keepdims=True)
    table_row = jnp.sum(jnp.where(picks, spread[CAP : 2 * CAP], 0.0), axis=0, keepdims=True)
    member_f = jnp.where(sample_row.astype(jnp.int32) == iota((samples, ALL_A), 0) + 1, 1.0, 0.0)
    member = member_f.astype(BF16)
    member_ref[...] = member_f.T.astype(BF16)
    table_ref[...] = jnp.broadcast_to(table_row, (samples, ALL_A)).T.astype(BF16)

    for copy in copies[:2]:
        copy.wait()
    dense = dense_ref[...]
    pre_act = dot(dense, w_bottom_ref[...])
    sigma = jax.nn.sigmoid(pre_act)
    cross_ref[:, :EMB] = (pre_act * sigma).astype(BF16)
    table_t = table_ref[...]
    for t in range(0, TABLES, 2):
        if t == 16:
            copies[7].start()
        both = [jnp.where(table_t == t + u, arrived, 0.0).astype(BF16) for u in range(2)]
        cross_ref[:, (t + 1) * EMB : (t + 3) * EMB] = dot(member, jnp.concatenate(both, axis=1)).astype(BF16)

    for copy in copies[2:7]:
        copy.wait()
    low_rank = dot(cross_ref[...], cross_u_ref[...]).astype(BF16)
    w_out = w_out_ref[...]
    mixed_ref[...] = (dot(low_rank, cross_v_ref[...]) + (bias_ref[...] + 1.0)) * w_out
    cross_f = cross_ref[...].astype(F32)
    logits = jnp.sum(cross_f * mixed_ref[...], axis=1, keepdims=True)
    logit_grad = jax.nn.sigmoid(logits) - labels_ref[...].astype(F32)
    mix_grad = (logit_grad * w_out * cross_f).astype(BF16)
    low_grad = dot(mix_grad, cross_v_ref[...], 1, 1).astype(BF16)
    copies[7].wait()
    in_grad = logit_grad * mixed_ref[...] + dot(low_grad, u_turned_ref[...])
    pre_grad = (in_grad[:, :EMB] * (sigma * (1.0 + pre_act * (1.0 - sigma)))).astype(BF16)
    for t in range(TABLES):
        embed_ref[t * samples : (t + 1) * samples, :] = in_grad[:, (t + 1) * EMB : (t + 2) * EMB].astype(BF16)
    line = iota((1, 2 * PEERS), 1)
    line = lax.shift_right_logical(line, 1) * ROWS_A + CAP + (line & 1)
    wanted_ref[...] = onehot(iota((ALL_A, 2 * PEERS), 0) == line)
    embed_ref[TABLES * samples :, :] = dot(dense, pre_grad, 0, 0).astype(BF16)

    step = ALL_A // 2
    for c in range(ALL_A // step):
        rows = slice(c * step, (c + 1) * step)
        member_c = member_ref[rows, :]
        table_c = table_ref[rows, :]
        wide = [jnp.where(table_c == t, member_c, 0.0).astype(BF16) for t in range(TABLES)]
        wide = jnp.concatenate(wide + [wanted_ref[rows, :]], axis=1)
        out_ref[rows, :] = dot(wide, embed_ref[...]).astype(BF16)


def return_kernel(returned_ref, routed_ref, grads_ref, bottom_ref):
    returned = returned_ref[...]
    grads_ref[...] = dot(returned, routed_ref[...], 0, 0).astype(BF16)
    slot = iota((8, ALL_A), 1)
    place = slot - divide_floor(slot, ROWS_A) * ROWS_A
    bottom_ref[...] = dot(onehot(place == iota((8, ALL_A), 0) + CAP), returned)


def total_kernel(grads_ref, bottom_ref, total_ref, message_ref):
    total = grads_ref[0].astype(F32)
    for s in range(1, grads_ref.shape[0]):
        total = total + grads_ref[s].astype(F32)
    total_ref[...] = total
    squares = jnp.sum(total * total, axis=0, keepdims=True)
    bottom = bottom_ref[...]
    message = jnp.concatenate([squares, bottom[0:1], bottom[1:2]], axis=1)
    for s in range(message_ref.shape[0]):
        message_ref[s] = message


def step_kernel(
    message_ref, total_ref, accum_ref, table_ref, steps_ref, block_ref, rows_ref, accum_out_ref, out_ref
):
    rows = accum_ref.shape[1]
    message = message_ref[0]
    for s in range(1, message_ref.shape[0]):
        message = message + message_ref[s]
    accum = accum_ref[...] + message[:, :rows] * (1.0 / EMB)
    accum_out_ref[...] = accum
    step = total_ref[...] * (1.0 / jnp.sqrt(accum))
    rows_ref[...] = table_ref[...] - LEARN_RATE * step
    block = block_ref[...]
    wide = jnp.concatenate([jnp.where(block == a, step, 0.0) for a in range(4)], axis=0).astype(BF16)
    payload = dot(steps_ref[...], wide, 1, 1)
    slot = iota((ALL_D, EMB), 0)
    place = slot - divide_floor(slot, ROWS_D) * ROWS_D
    payload = jnp.where(place == 4, message[:, rows : rows + EMB], payload)
    payload = jnp.where(place == 5, message[:, rows + EMB : rows + 2 * EMB], payload)
    out_ref[...] = payload.astype(BF16)


def final_kernel(served_ref, serving_ref, bottom_ref):
    served = served_ref[...]
    slot = iota((ALL_D, PEERS), 0)
    peer = iota((ALL_D, PEERS), 1)
    for r in range(4):
        pick = onehot(slot == peer * ROWS_D + r)
        serving_ref[r * EMB : (r + 1) * EMB, :] = dot(served, pick, 0, 0).astype(BF16)
    line = iota((2 * PEERS, ALL_D), 0)
    slot = iota((2 * PEERS, ALL_D), 1)
    pick = onehot(slot == lax.shift_right_logical(line, 1) * ROWS_D + 4 + (line & 1))
    bottom_ref[...] = dot(pick, served)


def call(kernel, outs, *args, scratch=(), flops=0, hbm=(), limit=VMEM_LIMIT):
    moved = sum(x.size * x.dtype.itemsize for x in args)
    spaces = [pltpu.HBM if i in hbm else pltpu.VMEM for i in range(len(args))]
    return pl.pallas_call(
        kernel,
        out_shape=[jax.ShapeDtypeStruct(shape, kind) for shape, kind in outs],
        in_specs=[pl.BlockSpec(memory_space=space) for space in spaces],
        scratch_shapes=list(scratch),
        compiler_params=pltpu.CompilerParams(vmem_limit_bytes=limit),
        cost_estimate=pl.CostEstimate(flops=flops, bytes_accessed=moved, transcendentals=0),
    )(*args)


def over_rows(chunks, rows):
    split = chunks.reshape(PEERS, rows // 2, 2, EMB)
    split = lax.all_to_all(split, "rows", split_axis=0, concat_axis=0, tiled=True)
    return split.reshape(PEERS * rows, EMB)


def over_serve(pieces):
    return lax.all_to_all(pieces, "serve", split_axis=0, concat_axis=0, tiled=True)


def per_device(
    table_rows,
    row_accum,
    lookup_rows,
    bag_lengths,
    bag_owner,
    bag_target,
    bottom_in,
    labels,
    w_bottom,
    cross_u,
    cross_v,
    cross_bias,
    w_out,
    serve_owner,
):
    touched = table_rows.shape[0]
    lookups = lookup_rows.reshape(1, -1)
    lengths = bag_lengths.reshape(1, -1)
    bags = lengths.shape[1]
    owners = bag_owner.reshape(1, -1)
    targets = bag_target.reshape(1, -1)
    dense_in = bottom_in.reshape(-1, bottom_in.shape[-1])
    samples = dense_in.shape[0]
    width = cross_u.shape[0]
    serves = lax.axis_size("serve")
    cols = EMB // serves

    outgoing, slots = call(
        pool_kernel,
        [((ALL_A, EMB), BF16), ((1, bags), jnp.int32)],
        lengths,
        lookups,
        owners,
        targets,
        table_rows,
        scratch=(
            pltpu.VMEM(lengths.shape, jnp.int32),
            pltpu.VMEM(lookups.shape, jnp.int32),
            pltpu.VMEM(owners.shape, jnp.int32),
            pltpu.VMEM(targets.shape, jnp.int32),
            pltpu.VMEM(table_rows.shape, F32),
            pltpu.SemaphoreType.DMA((5,)),
        ),
        flops=2 * 700 * 10**6,
        hbm=range(5),
        limit=60 * 1024 * 1024,
    )
    arrived = over_rows(outgoing, ROWS_A)
    routed, steps_to, block, table_cols, u_turned = call(
        ready_kernel,
        [
            ((ALL_A, touched), BF16),
            ((ALL_D, touched), BF16),
            ((1, touched), jnp.int32),
            ((cols, touched), F32),
            (cross_u.shape[::-1], BF16),
        ],
        lengths,
        lookups,
        slots,
        serve_owner.reshape(1, -1),
        table_rows,
        cross_u,
        scratch=(pltpu.VMEM((EMB, touched), F32),),
        flops=2 * 1600 * 10**6,
        limit=60 * 1024 * 1024,
    )
    operands = (
        arrived,
        dense_in,
        w_bottom,
        cross_u,
        cross_bias.reshape(1, -1),
        w_out.reshape(1, -1),
        labels.reshape(-1, 1),
        cross_v,
        u_turned,
    )
    (replies,) = call(
        owner_kernel,
        [((ALL_A, EMB), BF16)],
        *operands,
        scratch=tuple(pltpu.VMEM(x.shape, x.dtype) for x in operands[1:])
        + (
            pltpu.VMEM((samples, width), BF16),
            pltpu.VMEM((samples, width), F32),
            pltpu.VMEM((samples * TABLES + 2 * PEERS, EMB), BF16),
            pltpu.VMEM((ALL_A, PEERS), BF16),
            pltpu.VMEM((ALL_A, PEERS), BF16),
            pltpu.VMEM((ALL_A, 2 * PEERS), BF16),
            pltpu.SemaphoreType.DMA((len(operands) - 1,)),
        ),
        flops=2 * 1600 * 10**6,
        hbm=range(1, len(operands)),
        limit=52 * 1024 * 1024,
    )
    returned = over_rows(replies, ROWS_A)
    grads, bottom = call(
        return_kernel,
        [((EMB, touched), BF16), ((8, EMB), F32)],
        returned,
        routed,
        flops=2 * 160 * 10**6,
    )
    pieces = over_serve(grads.reshape(serves, cols, touched))
    total, message = call(
        total_kernel,
        [((cols, touched), F32), ((serves, 1, touched + 2 * EMB), F32)],
        pieces,
        bottom,
    )
    messages = over_serve(message)
    new_rows, new_accum, steps = call(
        step_kernel,
        [((cols, touched), F32), ((1, touched), F32), ((ALL_D, EMB), BF16)],
        messages,
        total,
        row_accum.reshape(1, -1),
        table_cols,
        steps_to,
        block,
        flops=2 * 100 * 10**6,
    )
    served = over_rows(steps, ROWS_D)
    serving, grad_bottom = call(
        final_kernel, [((4 * EMB, PEERS), BF16), ((2 * PEERS, EMB), F32)], served, flops=2 * 50 * 10**6
    )
    serving = serving.reshape(16, cols, PEERS).transpose(2, 0, 1)[None]
    return (new_rows.T, new_accum.reshape(-1), serving, grad_bottom)


def solution(mesh):
    return jax.shard_map(
        per_device,
        mesh=mesh,
        in_specs=(
            P("rows", None),
            P("rows"),
            P("serve", "rows", None),
            P("serve", "rows", None),
            P("serve", "rows", None, None),
            P("serve", "rows", None),
            P("serve", "rows", None),
            P("serve", "rows"),
            P(),
            P(),
            P(),
            P(),
            P(),
            P("rows", None),
        ),
        out_specs=(P("rows", "serve"), P("rows"), P("rows", None, None, "serve"), P()),
        check_vma=False,
    )
```

```python
import functools

import jax
import jax.numpy as jnp
from jax import lax
from jax.experimental import pallas as pl
from jax.experimental.pallas import tpu as pltpu
from jax.sharding import PartitionSpec as P

TABLES = 26
LEARN_RATE = 0.1
EMB = 128
PEERS = 128
CAP = 8
ROWS_A = 10
ALL_A = PEERS * ROWS_A
ROWS_D = 6
ALL_D = PEERS * ROWS_D
F32 = jnp.float32
BF16 = jnp.bfloat16
VMEM_LIMIT = 32 * 1024 * 1024


def dot(a, b, ca=1, cb=0):
    return lax.dot_general(a, b, (((ca,), (cb,)), ((), ())), preferred_element_type=F32)


def iota(shape, dim):
    return lax.broadcasted_iota(jnp.int32, shape, dim)


def onehot(mask):
    return jnp.where(mask, 1.0, 0.0).astype(BF16)


def divide_floor(values, by):
    return jnp.floor((values.astype(F32) + 0.5) * (1.0 / by)).astype(jnp.int32)


def step_place(owners):
    return (lax.shift_right_logical(owners, 1) & 15) * 8 + lax.shift_right_logical(owners, 5) * 2 + (owners & 1)


def served_place(sources):
    return lax.shift_right_logical(sources, 5) * 32 + (sources & 1) * 16 + (lax.shift_right_logical(sources, 1) & 15)


def fetch(sources, targets, sems):
    copies = [pltpu.make_async_copy(s, t, sems.at[i]) for i, (s, t) in enumerate(zip(sources, targets))]
    for copy in copies:
        copy.start()
    return copies


def bag_ends(lengths_ref):
    bags = lengths_ref.shape[1]
    row_id = iota((bags, bags), 0)
    col_id = iota((bags, bags), 1)
    lens = jnp.broadcast_to(lengths_ref[...].astype(F32), (8, bags)).astype(BF16)
    starts = dot(onehot(col_id < row_id), lens, 1, 1)[:, 0:1].astype(jnp.int32)
    ends = dot(onehot(col_id <= row_id), lens, 1, 1)[:, 0:1].astype(jnp.int32)
    return starts, ends


def pool_kernel(
    lengths_hbm,
    lookups_hbm,
    owners_hbm,
    targets_hbm,
    table_hbm,
    out_ref,
    slots_ref,
    lengths_ref,
    lookups_ref,
    owners_ref,
    targets_ref,
    table_ref,
    sems,
):
    copies = fetch(
        (lengths_hbm, lookups_hbm, owners_hbm, targets_hbm, table_hbm),
        (lengths_ref, lookups_ref, owners_ref, targets_ref, table_ref),
        sems,
    )
    bags = lengths_ref.shape[1]
    looks = lookups_ref.shape[1]
    touched = table_ref.shape[0]
    for copy in copies[:4]:
        copy.wait()
    owners = owners_ref[...]
    of_owner = jnp.where(iota((PEERS, bags), 0) == owners, 1.0, 0.0)
    before = dot(of_owner.astype(BF16), onehot(iota((bags, bags), 0) < iota((bags, bags), 1)))
    rank = jnp.sum(before * of_owner, axis=0, keepdims=True).astype(jnp.int32)
    slots = owners * ROWS_A + rank
    slots_ref[...] = slots
    targets = targets_ref[...]
    sample = divide_floor(targets, TABLES)
    table_of = targets - sample * TABLES
    lane = iota((EMB, bags), 0)
    names = jnp.where(lane == rank, sample + 1, 0) + jnp.where(lane == rank + CAP, table_of, 0)
    names = dot(of_owner.astype(BF16), names.astype(F32).astype(BF16), 1, 1).astype(BF16)
    copies[4].wait()
    table = table_ref[...]
    high = table.astype(BF16)
    low = (table - high.astype(F32)).astype(BF16)
    starts, ends = bag_ends(lengths_ref)
    place = iota((bags, looks), 1)
    in_bag = onehot((place >= starts) & (place < ends))
    lookups = jnp.broadcast_to(lookups_ref[...].astype(F32), (128, looks)).T.astype(jnp.int32)
    both = jnp.concatenate([high, low], axis=1)
    lane = iota((512, 128), 1)
    sums = 0.0
    for first in range(0, looks, 512):
        part = lookups[first : first + 512]
        goes = jnp.concatenate([onehot(part == lane + c) for c in range(0, touched, 128)], axis=1)
        sums = sums + dot(in_bag[:, first : first + 512], dot(goes, both).astype(BF16))
    pooled = (sums[:, :EMB] + sums[:, EMB:]).astype(BF16)
    payload = dot(onehot(iota((ALL_A, bags), 0) == slots), pooled)
    ninth = onehot(iota((ALL_A, PEERS), 0) == iota((ALL_A, PEERS), 1) * ROWS_A + CAP)
    out_ref[...] = (payload + dot(ninth, names)).astype(BF16)


def ready_kernel(
    lengths_ref,
    lookups_ref,
    slots_ref,
    owners_ref,
    table_ref,
    cross_u_ref,
    routed_ref,
    steps_ref,
    block_ref,
    cols_ref,
    u_turned_ref,
    turned_ref,
):
    rows = owners_ref.shape[1]
    bags = slots_ref.shape[1]
    looks = lookups_ref.shape[1]
    u_turned_ref[...] = cross_u_ref[...].T
    starts, ends = bag_ends(lengths_ref)
    place = iota((bags, looks), 1)
    in_bag = onehot((place >= starts) & (place < ends))
    of_row = onehot(iota((rows, looks), 0) == lookups_ref[...])
    counts = dot(in_bag, of_row, 1, 1).astype(BF16)
    routed_ref[...] = dot(onehot(iota((ALL_A, bags), 0) == slots_ref[...]), counts).astype(BF16)
    owners = owners_ref[...]
    of_owner = jnp.where(iota((PEERS, rows), 0) == owners, 1.0, 0.0)
    before = dot(of_owner.astype(BF16), onehot(iota((rows, rows), 0) < iota((rows, rows), 1)))
    rank = jnp.sum(before * of_owner, axis=0, keepdims=True).astype(jnp.int32)
    row_of = lax.shift_right_logical(rank, 2)
    block_ref[...] = rank - 4 * row_of
    steps_ref[...] = onehot(iota((ALL_D, rows), 0) == step_place(owners) * ROWS_D + row_of)
    turned_ref[...] = table_ref[...].T
    cols = cols_ref.shape[0]
    cols_ref[...] = turned_ref[pl.ds(pl.multiple_of(lax.axis_index("serve") * cols, cols), cols), :]


def owner_kernel(*refs):
    arrived_ref, *refs = refs
    count = (len(refs) - 10) // 2
    sources, out_ref = refs[:count], refs[count]
    targets = refs[count + 1 : 2 * count + 1]
    cross_ref, mixed_ref, embed_ref, member_ref, table_ref, wanted_ref, reply_ref, sems, out_sems = refs[2 * count + 1 :]
    copies = [pltpu.make_async_copy(s, t, sems.at[i]) for i, (s, t) in enumerate(zip(sources, targets))]
    dense_ref, w_bottom_ref, cross_u_ref, bias_ref, w_out_ref, labels_ref, cross_v_ref, u_turned_ref = targets
    for copy in copies[:7]:
        copy.start()
    samples = dense_ref.shape[0]
    peer = iota((PEERS, ALL_A), 0) * ROWS_A
    slot = iota((PEERS, ALL_A), 1)
    name_row = onehot(slot == peer + CAP)
    chunk = onehot((slot >= peer) & (slot < peer + ROWS_A))
    arrived = arrived_ref[...]
    names = dot(name_row, arrived).astype(BF16)
    spread = dot(names, chunk, 0, 0)
    place = iota((CAP, ALL_A), 1)
    place = place - divide_floor(place, ROWS_A) * ROWS_A
    picks = iota((CAP, ALL_A), 0) == place
    sample_row = jnp.sum(jnp.where(picks, spread[:CAP], 0.0), axis=0, keepdims=True)
    table_row = jnp.sum(jnp.where(picks, spread[CAP : 2 * CAP], 0.0), axis=0, keepdims=True)
    member_f = jnp.where(sample_row.astype(jnp.int32) == iota((samples, ALL_A), 0) + 1, 1.0, 0.0)
    member = member_f.astype(BF16)
    member_ref[...] = member_f.T.astype(BF16)
    table_ref[...] = jnp.broadcast_to(table_row, (samples, ALL_A)).T.astype(BF16)

    for copy in copies[:2]:
        copy.wait()
    dense = dense_ref[...]
    pre_act = dot(dense, w_bottom_ref[...])
    sigma = jax.nn.sigmoid(pre_act)
    cross_ref[:, :EMB] = (pre_act * sigma).astype(BF16)
    table_t = table_ref[...]
    for t in range(0, TABLES, 2):
        both = [jnp.where(table_t == t + u, arrived, 0.0).astype(BF16) for u in range(2)]
        cross_ref[:, (t + 1) * EMB : (t + 3) * EMB] = dot(member, jnp.concatenate(both, axis=1)).astype(BF16)

    for copy in copies[2:6]:
        copy.wait()
    copies[7].start()
    low_rank = dot(cross_ref[...], cross_u_ref[...]).astype(BF16)
    copies[6].wait()
    w_out = w_out_ref[...]
    mixed_ref[...] = (dot(low_rank, cross_v_ref[...]) + (bias_ref[...] + 1.0)) * w_out
    cross_f = cross_ref[...].astype(F32)
    logits = jnp.sum(cross_f * mixed_ref[...], axis=1, keepdims=True)
    logit_grad = jax.nn.sigmoid(logits) - labels_ref[...].astype(F32)
    mix_grad = (logit_grad * w_out * cross_f).astype(BF16)
    low_grad = dot(mix_grad, cross_v_ref[...], 1, 1).astype(BF16)
    copies[7].wait()
    in_grad = logit_grad * mixed_ref[...] + dot(low_grad, u_turned_ref[...])
    pre_grad = (in_grad[:, :EMB] * (sigma * (1.0 + pre_act * (1.0 - sigma)))).astype(BF16)
    for t in range(TABLES):
        embed_ref[t * samples : (t + 1) * samples, :] = in_grad[:, (t + 1) * EMB : (t + 2) * EMB].astype(BF16)
    line = iota((1, 2 * PEERS), 1)
    line = lax.shift_right_logical(line, 1) * ROWS_A + CAP + (line & 1)
    wanted_ref[...] = onehot(iota((ALL_A, 2 * PEERS), 0) == line)
    embed_ref[TABLES * samples :, :] = dot(dense, pre_grad, 0, 0).astype(BF16)

    step = ALL_A // 2
    sent = []
    for c in range(ALL_A // step):
        rows = slice(c * step, (c + 1) * step)
        member_c = member_ref[rows, :]
        table_c = table_ref[rows, :]
        wide = [jnp.where(table_c == t, member_c, 0.0).astype(BF16) for t in range(TABLES)]
        wide = jnp.concatenate(wide + [wanted_ref[rows, :]], axis=1)
        reply_ref[rows, :] = dot(wide, embed_ref[...]).astype(BF16)
        sent.append(pltpu.make_async_copy(reply_ref.at[rows], out_ref.at[rows], out_sems.at[c]))
        sent[c].start()
    for copy in sent:
        copy.wait()


def return_kernel(returned_ref, routed_ref, grads_ref, bottom_ref):
    returned = returned_ref[...]
    grads_ref[...] = dot(returned, routed_ref[...], 0, 0).astype(BF16)
    slot = iota((8, ALL_A), 1)
    place = slot - divide_floor(slot, ROWS_A) * ROWS_A
    bottom_ref[...] = dot(onehot(place == iota((8, ALL_A), 0) + CAP), returned)


def total_kernel(grads_ref, bottom_ref, total_ref, message_ref):
    total = grads_ref[0].astype(F32)
    for s in range(1, grads_ref.shape[0]):
        total = total + grads_ref[s].astype(F32)
    total_ref[...] = total
    squares = jnp.sum(total * total, axis=0, keepdims=True)
    bottom = bottom_ref[...]
    message = jnp.concatenate([squares, bottom[0:1], bottom[1:2]], axis=1)
    for s in range(message_ref.shape[0]):
        message_ref[s] = message


def step_kernel(
    message_ref, total_ref, accum_ref, table_ref, steps_ref, block_ref, rows_ref, accum_out_ref, out_ref
):
    rows = accum_ref.shape[1]
    message = message_ref[0]
    for s in range(1, message_ref.shape[0]):
        message = message + message_ref[s]
    accum = accum_ref[...] + message[:, :rows] * (1.0 / EMB)
    accum_out_ref[...] = accum
    step = total_ref[...] * (1.0 / jnp.sqrt(accum))
    rows_ref[...] = table_ref[...] - LEARN_RATE * step
    block = block_ref[...]
    wide = jnp.concatenate([jnp.where(block == a, step, 0.0) for a in range(4)], axis=0).astype(BF16)
    payload = dot(steps_ref[...], wide, 1, 1)
    slot = iota((ALL_D, EMB), 0)
    place = slot - divide_floor(slot, ROWS_D) * ROWS_D
    payload = jnp.where(place == 4, message[:, rows : rows + EMB], payload)
    payload = jnp.where(place == 5, message[:, rows + EMB : rows + 2 * EMB], payload)
    out_ref[...] = payload.astype(BF16)


def final_kernel(served_ref, serving_ref, bottom_ref):
    served = served_ref[...]
    slot = iota((ALL_D, PEERS), 0)
    first = served_place(iota((ALL_D, PEERS), 1)) * ROWS_D
    for r in range(4):
        pick = onehot(slot == first + r)
        serving_ref[r * EMB : (r + 1) * EMB, :] = dot(served, pick, 0, 0).astype(BF16)
    line = iota((2 * PEERS, ALL_D), 0)
    slot = iota((2 * PEERS, ALL_D), 1)
    pick = onehot(slot == served_place(lax.shift_right_logical(line, 1)) * ROWS_D + 4 + (line & 1))
    bottom_ref[...] = dot(pick, served)


def call(kernel, outs, *args, scratch=(), flops=0, hbm=(), limit=VMEM_LIMIT, hbm_out=False):
    moved = sum(x.size * x.dtype.itemsize for x in args)
    spaces = [pltpu.HBM if i in hbm else pltpu.VMEM for i in range(len(args))]
    return pl.pallas_call(
        kernel,
        out_shape=[jax.ShapeDtypeStruct(shape, kind) for shape, kind in outs],
        in_specs=[pl.BlockSpec(memory_space=space) for space in spaces],
        out_specs=[pl.BlockSpec(memory_space=pltpu.HBM if hbm_out else pltpu.VMEM)] * len(outs),
        scratch_shapes=list(scratch),
        compiler_params=pltpu.CompilerParams(vmem_limit_bytes=limit),
        cost_estimate=pl.CostEstimate(flops=flops, bytes_accessed=moved, transcendentals=0),
    )(*args)


def over_rows(chunks, rows):
    split = chunks.reshape(PEERS, rows // 2, 2, EMB)
    split = lax.all_to_all(split, "rows", split_axis=0, concat_axis=0, tiled=True)
    return split.reshape(PEERS * rows, EMB)


def over_rows_in_two(chunks, rows):
    along_z = [[y * 32 + z * 2 + c for z in range(16)] for y in range(4) for c in range(2)]
    across = [[y * 32 + z * 2 + c for y in range(4) for c in range(2)] for z in range(16)]
    split = chunks.reshape(16, 8, rows // 2, 2, EMB)
    split = lax.all_to_all(split, "rows", 0, 0, axis_index_groups=along_z, tiled=True)
    split = split.transpose(1, 0, 2, 3, 4)
    split = lax.all_to_all(split, "rows", 0, 0, axis_index_groups=across, tiled=True)
    return split.reshape(PEERS * rows, EMB)


def over_serve(pieces):
    return lax.all_to_all(pieces, "serve", split_axis=0, concat_axis=0, tiled=True)


def per_device(
    table_rows,
    row_accum,
    lookup_rows,
    bag_lengths,
    bag_owner,
    bag_target,
    bottom_in,
    labels,
    w_bottom,
    cross_u,
    cross_v,
    cross_bias,
    w_out,
    serve_owner,
):
    touched = table_rows.shape[0]
    lookups = lookup_rows.reshape(1, -1)
    lengths = bag_lengths.reshape(1, -1)
    bags = lengths.shape[1]
    owners = bag_owner.reshape(1, -1)
    targets = bag_target.reshape(1, -1)
    dense_in = bottom_in.reshape(-1, bottom_in.shape[-1])
    samples = dense_in.shape[0]
    width = cross_u.shape[0]
    serves = lax.axis_size("serve")
    cols = EMB // serves

    outgoing, slots = call(
        pool_kernel,
        [((ALL_A, EMB), BF16), ((1, bags), jnp.int32)],
        lengths,
        lookups,
        owners,
        targets,
        table_rows,
        scratch=(
            pltpu.VMEM(lengths.shape, jnp.int32),
            pltpu.VMEM(lookups.shape, jnp.int32),
            pltpu.VMEM(owners.shape, jnp.int32),
            pltpu.VMEM(targets.shape, jnp.int32),
            pltpu.VMEM(table_rows.shape, F32),
            pltpu.SemaphoreType.DMA((5,)),
        ),
        flops=2 * 700 * 10**6,
        hbm=range(5),
        limit=60 * 1024 * 1024,
    )
    arrived = over_rows(outgoing, ROWS_A)
    routed, steps_to, block, table_cols, u_turned = call(
        ready_kernel,
        [
            ((ALL_A, touched), BF16),
            ((ALL_D, touched), BF16),
            ((1, touched), jnp.int32),
            ((cols, touched), F32),
            (cross_u.shape[::-1], BF16),
        ],
        lengths,
        lookups,
        slots,
        serve_owner.reshape(1, -1),
        table_rows,
        cross_u,
        scratch=(pltpu.VMEM((EMB, touched), F32),),
        flops=2 * 1600 * 10**6,
        limit=60 * 1024 * 1024,
    )
    operands = (
        arrived,
        dense_in,
        w_bottom,
        cross_u,
        cross_bias.reshape(1, -1),
        w_out.reshape(1, -1),
        labels.reshape(-1, 1),
        cross_v,
        u_turned,
    )
    (replies,) = call(
        owner_kernel,
        [((ALL_A, EMB), BF16)],
        *operands,
        scratch=tuple(pltpu.VMEM(x.shape, x.dtype) for x in operands[1:])
        + (
            pltpu.VMEM((samples, width), BF16),
            pltpu.VMEM((samples, width), F32),
            pltpu.VMEM((samples * TABLES + 2 * PEERS, EMB), BF16),
            pltpu.VMEM((ALL_A, PEERS), BF16),
            pltpu.VMEM((ALL_A, PEERS), BF16),
            pltpu.VMEM((ALL_A, 2 * PEERS), BF16),
            pltpu.VMEM((ALL_A, EMB), BF16),
            pltpu.SemaphoreType.DMA((len(operands) - 1,)),
            pltpu.SemaphoreType.DMA((2,)),
        ),
        flops=2 * 1600 * 10**6,
        hbm=range(1, len(operands)),
        limit=52 * 1024 * 1024,
        hbm_out=True,
    )
    returned = over_rows(replies, ROWS_A)
    grads, bottom = call(
        return_kernel,
        [((EMB, touched), BF16), ((8, EMB), F32)],
        returned,
        routed,
        flops=2 * 160 * 10**6,
    )
    pieces = over_serve(grads.reshape(serves, cols, touched))
    total, message = call(
        total_kernel,
        [((cols, touched), F32), ((serves, 1, touched + 2 * EMB), F32)],
        pieces,
        bottom,
    )
    messages = over_serve(message)
    new_rows, new_accum, steps = call(
        step_kernel,
        [((cols, touched), F32), ((1, touched), F32), ((ALL_D, EMB), BF16)],
        messages,
        total,
        row_accum.reshape(1, -1),
        table_cols,
        steps_to,
        block,
        flops=2 * 100 * 10**6,
    )
    served = over_rows_in_two(steps, ROWS_D)
    serving, grad_bottom = call(
        final_kernel, [((4 * EMB, PEERS), BF16), ((2 * PEERS, EMB), F32)], served, flops=2 * 50 * 10**6
    )
    serving = serving.reshape(16, cols, PEERS).transpose(2, 0, 1)[None]
    return (new_rows.T, new_accum.reshape(-1), serving, grad_bottom)


def solution(mesh):
    return jax.shard_map(
        per_device,
        mesh=mesh,
        in_specs=(
            P("rows", None),
            P("rows"),
            P("serve", "rows", None),
            P("serve", "rows", None),
            P("serve", "rows", None, None),
            P("serve", "rows", None),
            P("serve", "rows", None),
            P("serve", "rows"),
            P(),
            P(),
            P(),
            P(),
            P(),
            P("rows", None),
        ),
        out_specs=(P("rows", "serve"), P("rows"), P("rows", None, None, "serve"), P()),
        check_vma=False,
    )
```

```python
import functools

import jax
import jax.numpy as jnp
from jax import lax
from jax.experimental import pallas as pl
from jax.experimental.pallas import tpu as pltpu
from jax.sharding import PartitionSpec as P

TABLES = 26
LEARN_RATE = 0.1
EMB = 128
PEERS = 128
CAP = 8
ROWS_A = 10
ALL_A = PEERS * ROWS_A
ROWS_D = 6
ALL_D = PEERS * ROWS_D
F32 = jnp.float32
SMALL = jnp.int8
BF16 = jnp.bfloat16
VMEM_LIMIT = 32 * 1024 * 1024


def dot(a, b, ca=1, cb=0):
    return lax.dot_general(a, b, (((ca,), (cb,)), ((), ())), preferred_element_type=F32)


def iota(shape, dim):
    return lax.broadcasted_iota(jnp.int32, shape, dim)


def onehot(mask):
    return jnp.where(mask, 1.0, 0.0).astype(BF16)


def divide_floor(values, by):
    return jnp.floor((values.astype(F32) + 0.5) * (1.0 / by)).astype(jnp.int32)


def owner_place(owners):
    return owners


def fetch(sources, targets, sems):
    copies = [pltpu.make_async_copy(s, t, sems.at[i]) for i, (s, t) in enumerate(zip(sources, targets))]
    for copy in copies:
        copy.start()
    return copies


def bag_ends(lengths_ref):
    bags = lengths_ref.shape[1]
    row_id = iota((bags, bags), 0)
    col_id = iota((bags, bags), 1)
    lens = jnp.broadcast_to(lengths_ref[...].astype(F32), (8, bags)).astype(BF16)
    starts = dot(onehot(col_id < row_id), lens, 1, 1)[:, 0:1].astype(jnp.int32)
    ends = dot(onehot(col_id <= row_id), lens, 1, 1)[:, 0:1].astype(jnp.int32)
    return starts, ends


def pool_kernel(
    lengths_hbm,
    lookups_hbm,
    owners_hbm,
    targets_hbm,
    table_hbm,
    out_ref,
    slots_ref,
    lengths_ref,
    lookups_ref,
    owners_ref,
    targets_ref,
    table_ref,
    sems,
):
    copies = fetch(
        (lengths_hbm, lookups_hbm, owners_hbm, targets_hbm, table_hbm),
        (lengths_ref, lookups_ref, owners_ref, targets_ref, table_ref),
        sems,
    )
    bags = lengths_ref.shape[1]
    looks = lookups_ref.shape[1]
    touched = table_ref.shape[0]
    for copy in copies[:4]:
        copy.wait()
    owners = owners_ref[...]
    of_owner = jnp.where(iota((PEERS, bags), 0) == owners, 1.0, 0.0)
    before = dot(of_owner.astype(BF16), onehot(iota((bags, bags), 0) < iota((bags, bags), 1)))
    rank = jnp.sum(before * of_owner, axis=0, keepdims=True).astype(jnp.int32)
    slots = owner_place(owners) * ROWS_A + rank
    slots_ref[...] = slots
    targets = targets_ref[...]
    sample = divide_floor(targets, TABLES)
    table_of = targets - sample * TABLES
    lane = iota((EMB, bags), 0)
    names = jnp.where(lane == rank, sample + 1, 0) + jnp.where(lane == rank + CAP, table_of, 0)
    names = dot(of_owner.astype(BF16), names.astype(F32).astype(BF16), 1, 1).astype(BF16)
    copies[4].wait()
    table = table_ref[...]
    high = table.astype(BF16)
    low = (table - high.astype(F32)).astype(BF16)
    starts, ends = bag_ends(lengths_ref)
    place = iota((bags, looks), 1)
    in_bag = onehot((place >= starts) & (place < ends))
    lookups = jnp.broadcast_to(lookups_ref[...].astype(F32), (128, looks)).T.astype(jnp.int32)
    both = jnp.concatenate([high, low], axis=1)
    lane = iota((512, 128), 1)
    sums = 0.0
    for first in range(0, looks, 512):
        part = lookups[first : first + 512]
        goes = jnp.concatenate([onehot(part == lane + c) for c in range(0, touched, 128)], axis=1)
        sums = sums + dot(in_bag[:, first : first + 512], dot(goes, both).astype(BF16))
    pooled = (sums[:, :EMB] + sums[:, EMB:]).astype(BF16)
    payload = dot(onehot(iota((ALL_A, bags), 0) == slots), pooled)
    ninth = onehot(iota((ALL_A, PEERS), 0) == owner_place(iota((ALL_A, PEERS), 1)) * ROWS_A + CAP)
    out_ref[...] = (payload + dot(ninth, names)).astype(BF16)


def ready_kernel(
    lengths_ref,
    lookups_ref,
    slots_ref,
    owners_ref,
    table_ref,
    routed_ref,
    steps_ref,
    block_ref,
    cols_ref,
    turned_ref,
):
    rows = owners_ref.shape[1]
    bags = slots_ref.shape[1]
    looks = lookups_ref.shape[1]
    starts, ends = bag_ends(lengths_ref)
    place = iota((bags, looks), 1)
    in_bag = onehot((place >= starts) & (place < ends))
    of_row = onehot(iota((rows, looks), 0) == lookups_ref[...])
    counts = dot(in_bag, of_row, 1, 1).astype(BF16)
    routed_ref[...] = dot(onehot(iota((ALL_A, bags), 0) == slots_ref[...]), counts).astype(jnp.int32).astype(SMALL)
    owners = owners_ref[...]
    of_owner = jnp.where(iota((PEERS, rows), 0) == owners, 1.0, 0.0)
    before = dot(of_owner.astype(BF16), onehot(iota((rows, rows), 0) < iota((rows, rows), 1)))
    rank = jnp.sum(before * of_owner, axis=0, keepdims=True).astype(jnp.int32)
    row_of = lax.shift_right_logical(rank, 2)
    block_ref[...] = rank - 4 * row_of
    steps_ref[...] = onehot(iota((ALL_D, rows), 0) == owner_place(owners) * ROWS_D + row_of)
    turned_ref[...] = table_ref[...].T
    cols = cols_ref.shape[0]
    cols_ref[...] = turned_ref[pl.ds(pl.multiple_of(lax.axis_index("serve") * cols, cols), cols), :]


def owner_kernel(*refs):
    arrived_ref, _, *refs = refs
    count = (len(refs) - 10) // 2
    sources, out_ref = refs[:count], refs[count]
    targets = refs[count + 1 : 2 * count + 1]
    cross_ref, mixed_ref, embed_ref, member_ref, table_ref, wanted_ref, *refs = refs[2 * count + 1 :]
    u_turned_ref, v_turned_ref, sems = refs
    copies = [pltpu.make_async_copy(s, t, sems.at[i]) for i, (s, t) in enumerate(zip(sources, targets))]
    dense_ref, w_bottom_ref, cross_u_ref, bias_ref, w_out_ref, labels_ref, cross_v_ref = targets
    for copy in copies:
        copy.start()
    samples = dense_ref.shape[0]
    peer = iota((PEERS, ALL_A), 0) * ROWS_A
    slot = iota((PEERS, ALL_A), 1)
    name_row = onehot(slot == peer + CAP)
    chunk = onehot((slot >= peer) & (slot < peer + ROWS_A))
    arrived = arrived_ref[...]
    names = dot(name_row, arrived).astype(BF16)
    spread = dot(names, chunk, 0, 0)
    place = iota((CAP, ALL_A), 1)
    place = place - divide_floor(place, ROWS_A) * ROWS_A
    picks = iota((CAP, ALL_A), 0) == place
    sample_row = jnp.sum(jnp.where(picks, spread[:CAP], 0.0), axis=0, keepdims=True)
    table_row = jnp.sum(jnp.where(picks, spread[CAP : 2 * CAP], 0.0), axis=0, keepdims=True)
    member_f = jnp.where(sample_row.astype(jnp.int32) == iota((samples, ALL_A), 0) + 1, 1.0, 0.0)
    member = member_f.astype(BF16)
    member_ref[...] = member_f.T.astype(BF16)
    table_ref[...] = jnp.broadcast_to(table_row, (samples, ALL_A)).T.astype(BF16)

    for copy in copies[:2]:
        copy.wait()
    dense = dense_ref[...]
    pre_act = dot(dense, w_bottom_ref[...])
    sigma = jax.nn.sigmoid(pre_act)
    cross_ref[:, :EMB] = (pre_act * sigma).astype(BF16)
    table_t = table_ref[...]
    for t in range(0, TABLES, 2):
        if t == 14:
            for copy in copies[2:6]:
                copy.wait()
            u_turned_ref[...] = cross_u_ref[...].T
        both = [jnp.where(table_t == t + u, arrived, 0.0).astype(BF16) for u in range(2)]
        cross_ref[:, (t + 1) * EMB : (t + 3) * EMB] = dot(member, jnp.concatenate(both, axis=1)).astype(BF16)

    copies[6].wait()
    v_turned_ref[...] = cross_v_ref[...].T
    low_rank = dot(cross_ref[...], cross_u_ref[...]).astype(BF16)
    w_out = w_out_ref[...]
    mixed_ref[...] = (dot(low_rank, cross_v_ref[...]) + (bias_ref[...] + 1.0)) * w_out
    cross_f = cross_ref[...].astype(F32)
    logits = jnp.sum(cross_f * mixed_ref[...], axis=1, keepdims=True)
    logit_grad = jax.nn.sigmoid(logits) - labels_ref[...].astype(F32)
    mix_grad = (logit_grad * w_out * cross_f).astype(BF16)
    low_grad = dot(mix_grad, v_turned_ref[...]).astype(BF16)
    in_grad = logit_grad * mixed_ref[...] + dot(low_grad, u_turned_ref[...])
    pre_grad = (in_grad[:, :EMB] * (sigma * (1.0 + pre_act * (1.0 - sigma)))).astype(BF16)
    for t in range(TABLES):
        embed_ref[t * samples : (t + 1) * samples, :] = in_grad[:, (t + 1) * EMB : (t + 2) * EMB].astype(BF16)
    line = iota((1, 2 * PEERS), 1)
    line = lax.shift_right_logical(line, 1) * ROWS_A + CAP + (line & 1)
    wanted_ref[...] = onehot(iota((ALL_A, 2 * PEERS), 0) == line)
    embed_ref[TABLES * samples :, :] = dot(dense, pre_grad, 0, 0).astype(BF16)

    step = ALL_A // 2
    for c in range(ALL_A // step):
        rows = slice(c * step, (c + 1) * step)
        member_c = member_ref[rows, :]
        table_c = table_ref[rows, :]
        wide = [jnp.where(table_c == t, member_c, 0.0).astype(BF16) for t in range(TABLES)]
        wide = jnp.concatenate(wide + [wanted_ref[rows, :]], axis=1)
        out_ref[rows, :] = dot(wide, embed_ref[...]).astype(BF16)


def return_kernel(returned_ref, routed_ref, grads_ref, bottom_ref):
    returned = returned_ref[...]
    grads_ref[...] = dot(returned, routed_ref[...].astype(BF16), 0, 0).astype(BF16)
    slot = iota((8, ALL_A), 1)
    place = slot - divide_floor(slot, ROWS_A) * ROWS_A
    bottom_ref[...] = dot(onehot(place == iota((8, ALL_A), 0) + CAP), returned)


def total_kernel(grads_ref, bottom_ref, total_ref, message_ref):
    total = grads_ref[0].astype(F32)
    for s in range(1, grads_ref.shape[0]):
        total = total + grads_ref[s].astype(F32)
    total_ref[...] = total
    squares = jnp.sum(total * total, axis=0, keepdims=True)
    bottom = bottom_ref[...]
    message = jnp.concatenate([squares, bottom[0:1], bottom[1:2]], axis=1)
    for s in range(message_ref.shape[0]):
        message_ref[s] = message


def step_kernel(
    message_ref, total_ref, accum_ref, table_ref, steps_ref, block_ref, rows_ref, accum_out_ref, out_ref
):
    rows = accum_ref.shape[1]
    message = message_ref[0]
    for s in range(1, message_ref.shape[0]):
        message = message + message_ref[s]
    accum = accum_ref[...] + message[:, :rows] * (1.0 / EMB)
    accum_out_ref[...] = accum
    step = total_ref[...] * (1.0 / jnp.sqrt(accum))
    rows_ref[...] = table_ref[...] - LEARN_RATE * step
    block = block_ref[...]
    wide = jnp.concatenate([jnp.where(block == a, step, 0.0) for a in range(4)], axis=0).astype(BF16)
    payload = dot(steps_ref[...], wide, 1, 1)
    slot = iota((ALL_D, EMB), 0)
    place = slot - divide_floor(slot, ROWS_D) * ROWS_D
    payload = jnp.where(place == 4, message[:, rows : rows + EMB], payload)
    payload = jnp.where(place == 5, message[:, rows + EMB : rows + 2 * EMB], payload)
    out_ref[...] = payload.astype(BF16)


def final_kernel(served_ref, serving_ref, bottom_ref):
    served = served_ref[...]
    slot = iota((ALL_D, PEERS), 0)
    peer = iota((ALL_D, PEERS), 1)
    for r in range(4):
        pick = onehot(slot == peer * ROWS_D + r)
        serving_ref[r * EMB : (r + 1) * EMB, :] = dot(served, pick, 0, 0).astype(BF16)
    line = iota((2 * PEERS, ALL_D), 0)
    slot = iota((2 * PEERS, ALL_D), 1)
    pick = onehot(slot == lax.shift_right_logical(line, 1) * ROWS_D + 4 + (line & 1))
    bottom_ref[...] = dot(pick, served)


def call(kernel, outs, *args, scratch=(), flops=0, hbm=(), limit=VMEM_LIMIT):
    moved = sum(x.size * x.dtype.itemsize for x in args)
    spaces = [pltpu.HBM if i in hbm else pltpu.VMEM for i in range(len(args))]
    return pl.pallas_call(
        kernel,
        out_shape=[jax.ShapeDtypeStruct(shape, kind) for shape, kind in outs],
        in_specs=[pl.BlockSpec(memory_space=space) for space in spaces],
        scratch_shapes=list(scratch),
        compiler_params=pltpu.CompilerParams(vmem_limit_bytes=limit),
        cost_estimate=pl.CostEstimate(flops=flops, bytes_accessed=moved, transcendentals=0),
    )(*args)


def over_rows(chunks, rows):
    split = chunks.reshape(PEERS, rows // 2, 2, EMB)
    split = lax.all_to_all(split, "rows", split_axis=0, concat_axis=0, tiled=True)
    return split.reshape(PEERS * rows, EMB)


def over_serve(pieces):
    return lax.all_to_all(pieces, "serve", split_axis=0, concat_axis=0, tiled=True)


def per_device(
    table_rows,
    row_accum,
    lookup_rows,
    bag_lengths,
    bag_owner,
    bag_target,
    bottom_in,
    labels,
    w_bottom,
    cross_u,
    cross_v,
    cross_bias,
    w_out,
    serve_owner,
):
    touched = table_rows.shape[0]
    lookups = lookup_rows.reshape(1, -1)
    lengths = bag_lengths.reshape(1, -1)
    bags = lengths.shape[1]
    owners = bag_owner.reshape(1, -1)
    targets = bag_target.reshape(1, -1)
    dense_in = bottom_in.reshape(-1, bottom_in.shape[-1])
    samples = dense_in.shape[0]
    width = cross_u.shape[0]
    serves = lax.axis_size("serve")
    cols = EMB // serves

    outgoing, slots = call(
        pool_kernel,
        [((ALL_A, EMB), BF16), ((1, bags), jnp.int32)],
        lengths,
        lookups,
        owners,
        targets,
        table_rows,
        scratch=(
            pltpu.VMEM(lengths.shape, jnp.int32),
            pltpu.VMEM(lookups.shape, jnp.int32),
            pltpu.VMEM(owners.shape, jnp.int32),
            pltpu.VMEM(targets.shape, jnp.int32),
            pltpu.VMEM(table_rows.shape, F32),
            pltpu.SemaphoreType.DMA((5,)),
        ),
        flops=2 * 700 * 10**6,
        hbm=range(5),
        limit=60 * 1024 * 1024,
    )
    arrived = over_rows(outgoing, ROWS_A)
    routed, steps_to, block, table_cols = call(
        ready_kernel,
        [
            ((ALL_A, touched), SMALL),
            ((ALL_D, touched), BF16),
            ((1, touched), jnp.int32),
            ((cols, touched), F32),
        ],
        lengths,
        lookups,
        slots,
        serve_owner.reshape(1, -1),
        table_rows,
        scratch=(pltpu.VMEM((EMB, touched), F32),),
        flops=2 * 1600 * 10**6,
        limit=60 * 1024 * 1024,
    )
    operands = (
        arrived,
        steps_to,
        dense_in,
        w_bottom,
        cross_u,
        cross_bias.reshape(1, -1),
        w_out.reshape(1, -1),
        labels.reshape(-1, 1),
        cross_v,
    )
    (replies,) = call(
        owner_kernel,
        [((ALL_A, EMB), BF16)],
        *operands,
        scratch=tuple(pltpu.VMEM(x.shape, x.dtype) for x in operands[2:])
        + (
            pltpu.VMEM((samples, width), BF16),
            pltpu.VMEM((samples, width), F32),
            pltpu.VMEM((samples * TABLES + 2 * PEERS, EMB), BF16),
            pltpu.VMEM((ALL_A, PEERS), BF16),
            pltpu.VMEM((ALL_A, PEERS), BF16),
            pltpu.VMEM((ALL_A, 2 * PEERS), BF16),
            pltpu.VMEM(cross_u.shape[::-1], BF16),
            pltpu.VMEM(cross_v.shape[::-1], BF16),
            pltpu.SemaphoreType.DMA((len(operands) - 2,)),
        ),
        flops=2 * 1600 * 10**6,
        hbm=range(1, len(operands)),
        limit=52 * 1024 * 1024,
    )
    returned = over_rows(replies, ROWS_A)
    grads, bottom = call(
        return_kernel,
        [((EMB, touched), BF16), ((8, EMB), F32)],
        returned,
        routed,
        flops=2 * 160 * 10**6,
    )
    pieces = over_serve(grads.reshape(serves, cols, touched))
    total, message = call(
        total_kernel,
        [((cols, touched), F32), ((serves, 1, touched + 2 * EMB), F32)],
        pieces,
        bottom,
    )
    messages = over_serve(message)
    new_rows, new_accum, steps = call(
        step_kernel,
        [((cols, touched), F32), ((1, touched), F32), ((ALL_D, EMB), BF16)],
        messages,
        total,
        row_accum.reshape(1, -1),
        table_cols,
        steps_to,
        block,
        flops=2 * 100 * 10**6,
    )
    served = over_rows(steps, ROWS_D)
    serving, grad_bottom = call(
        final_kernel, [((4 * EMB, PEERS), BF16), ((2 * PEERS, EMB), F32)], served, flops=2 * 50 * 10**6
    )
    serving = serving.reshape(16, cols, PEERS).transpose(2, 0, 1)[None]
    return (new_rows.T, new_accum.reshape(-1), serving, grad_bottom)


def solution(mesh):
    return jax.shard_map(
        per_device,
        mesh=mesh,
        in_specs=(
            P("rows", None),
            P("rows"),
            P("serve", "rows", None),
            P("serve", "rows", None),
            P("serve", "rows", None, None),
            P("serve", "rows", None),
            P("serve", "rows", None),
            P("serve", "rows"),
            P(),
            P(),
            P(),
            P(),
            P(),
            P("rows", None),
        ),
        out_specs=(P("rows", "serve"), P("rows"), P("rows", None, None, "serve"), P()),
        check_vma=False,
    )
```

```python
import functools

import jax
import jax.numpy as jnp
from jax import lax
from jax.experimental import pallas as pl
from jax.experimental.pallas import tpu as pltpu
from jax.sharding import PartitionSpec as P

TABLES = 26
LEARN_RATE = 0.1
EMB = 128
PEERS = 128
CAP = 8
ROWS_A = 10
ALL_A = PEERS * ROWS_A
ROWS_D = 6
ALL_D = PEERS * ROWS_D
F32 = jnp.float32
SMALL = jnp.int8
BF16 = jnp.bfloat16
VMEM_LIMIT = 32 * 1024 * 1024


def dot(a, b, ca=1, cb=0):
    return lax.dot_general(a, b, (((ca,), (cb,)), ((), ())), preferred_element_type=F32)


def iota(shape, dim):
    return lax.broadcasted_iota(jnp.int32, shape, dim)


def onehot(mask):
    return jnp.where(mask, 1.0, 0.0).astype(BF16)


def divide_floor(values, by):
    return jnp.floor((values.astype(F32) + 0.5) * (1.0 / by)).astype(jnp.int32)


def owner_place(owners):
    return owners


def fetch(sources, targets, sems):
    copies = [pltpu.make_async_copy(s, t, sems.at[i]) for i, (s, t) in enumerate(zip(sources, targets))]
    for copy in copies:
        copy.start()
    return copies


def bag_ends(lengths_ref):
    bags = lengths_ref.shape[1]
    row_id = iota((bags, bags), 0)
    col_id = iota((bags, bags), 1)
    lens = jnp.broadcast_to(lengths_ref[...].astype(F32), (8, bags)).astype(BF16)
    starts = dot(onehot(col_id < row_id), lens, 1, 1)[:, 0:1].astype(jnp.int32)
    ends = dot(onehot(col_id <= row_id), lens, 1, 1)[:, 0:1].astype(jnp.int32)
    return starts, ends


def pool_kernel(
    lengths_hbm,
    lookups_hbm,
    owners_hbm,
    targets_hbm,
    table_hbm,
    out_ref,
    slots_ref,
    lengths_ref,
    lookups_ref,
    owners_ref,
    targets_ref,
    table_ref,
    sems,
):
    copies = fetch(
        (lengths_hbm, lookups_hbm, owners_hbm, targets_hbm, table_hbm),
        (lengths_ref, lookups_ref, owners_ref, targets_ref, table_ref),
        sems,
    )
    bags = lengths_ref.shape[1]
    looks = lookups_ref.shape[1]
    touched = table_ref.shape[0]
    for copy in copies[:4]:
        copy.wait()
    owners = owners_ref[...]
    of_owner = jnp.where(iota((PEERS, bags), 0) == owners, 1.0, 0.0)
    before = dot(of_owner.astype(BF16), onehot(iota((bags, bags), 0) < iota((bags, bags), 1)))
    rank = jnp.sum(before * of_owner, axis=0, keepdims=True).astype(jnp.int32)
    slots = owner_place(owners) * ROWS_A + rank
    slots_ref[...] = slots
    targets = targets_ref[...]
    sample = divide_floor(targets, TABLES)
    table_of = targets - sample * TABLES
    lane = iota((EMB, bags), 0)
    names = jnp.where(lane == rank, sample + 1, 0) + jnp.where(lane == rank + CAP, table_of, 0)
    names = dot(of_owner.astype(BF16), names.astype(F32).astype(BF16), 1, 1).astype(BF16)
    copies[4].wait()
    table = table_ref[...]
    high = table.astype(BF16)
    low = (table - high.astype(F32)).astype(BF16)
    starts, ends = bag_ends(lengths_ref)
    place = iota((bags, looks), 1)
    in_bag = onehot((place >= starts) & (place < ends))
    lookups = jnp.broadcast_to(lookups_ref[...].astype(F32), (128, looks)).T.astype(jnp.int32)
    both = jnp.concatenate([high, low], axis=1)
    lane = iota((512, 128), 1)
    sums = 0.0
    for first in range(0, looks, 512):
        part = lookups[first : first + 512]
        goes = jnp.concatenate([onehot(part == lane + c) for c in range(0, touched, 128)], axis=1)
        sums = sums + dot(in_bag[:, first : first + 512], dot(goes, both).astype(BF16))
    pooled = (sums[:, :EMB] + sums[:, EMB:]).astype(BF16)
    payload = dot(onehot(iota((ALL_A, bags), 0) == slots), pooled)
    ninth = onehot(iota((ALL_A, PEERS), 0) == owner_place(iota((ALL_A, PEERS), 1)) * ROWS_A + CAP)
    out_ref[...] = (payload + dot(ninth, names)).astype(BF16)


def ready_kernel(
    lengths_ref,
    lookups_ref,
    slots_ref,
    owners_ref,
    table_ref,
    routed_ref,
    steps_ref,
    block_ref,
    cols_ref,
    turned_ref,
):
    rows = owners_ref.shape[1]
    bags = slots_ref.shape[1]
    looks = lookups_ref.shape[1]
    starts, ends = bag_ends(lengths_ref)
    place = iota((bags, looks), 1)
    in_bag = onehot((place >= starts) & (place < ends))
    of_row = onehot(iota((rows, looks), 0) == lookups_ref[...])
    counts = dot(in_bag, of_row, 1, 1).astype(BF16)
    routed_ref[...] = dot(onehot(iota((ALL_A, bags), 0) == slots_ref[...]), counts).astype(jnp.int32).astype(SMALL)
    owners = owners_ref[...]
    of_owner = jnp.where(iota((PEERS, rows), 0) == owners, 1.0, 0.0)
    before = dot(of_owner.astype(BF16), onehot(iota((rows, rows), 0) < iota((rows, rows), 1)))
    rank = jnp.sum(before * of_owner, axis=0, keepdims=True).astype(jnp.int32)
    row_of = lax.shift_right_logical(rank, 2)
    block_ref[...] = rank - 4 * row_of
    steps_ref[...] = onehot(iota((ALL_D, rows), 0) == owner_place(owners) * ROWS_D + row_of)
    turned_ref[...] = table_ref[...].T
    cols = cols_ref.shape[0]
    cols_ref[...] = turned_ref[pl.ds(pl.multiple_of(lax.axis_index("serve") * cols, cols), cols), :]


def owner_kernel(*refs):
    arrived_ref, _, *refs = refs
    count = (len(refs) - 10) // 2
    sources, out_ref = refs[:count], refs[count]
    targets = refs[count + 1 : 2 * count + 1]
    cross_ref, mixed_ref, embed_ref, member_ref, table_ref, wanted_ref, *refs = refs[2 * count + 1 :]
    u_turned_ref, v_turned_ref, sems = refs
    copies = [pltpu.make_async_copy(s, t, sems.at[i]) for i, (s, t) in enumerate(zip(sources, targets))]
    dense_ref, w_bottom_ref, cross_u_ref, bias_ref, w_out_ref, labels_ref, cross_v_ref = targets
    for copy in copies[:6]:
        copy.start()
    samples = dense_ref.shape[0]
    peer = iota((PEERS, ALL_A), 0) * ROWS_A
    slot = iota((PEERS, ALL_A), 1)
    name_row = onehot(slot == peer + CAP)
    chunk = onehot(iota((PEERS, ALL_A), 0) == divide_floor(iota((1, ALL_A), 1), ROWS_A))
    arrived = arrived_ref[...]
    names = dot(name_row, arrived).astype(BF16)
    spread = dot(names, chunk, 0, 0)
    place = iota((1, ALL_A), 1)
    place = place - divide_floor(place, ROWS_A) * ROWS_A
    picks = iota((CAP, ALL_A), 0) == place
    sample_row = jnp.sum(jnp.where(picks, spread[:CAP], 0.0), axis=0, keepdims=True)
    table_row = jnp.sum(jnp.where(picks, spread[CAP : 2 * CAP], 0.0), axis=0, keepdims=True)
    member_f = jnp.where(sample_row.astype(jnp.int32) == iota((samples, ALL_A), 0) + 1, 1.0, 0.0)
    member = member_f.astype(BF16)
    member_ref[...] = member_f.T.astype(BF16)
    table_ref[...] = jnp.broadcast_to(table_row, (samples, ALL_A)).T.astype(BF16)

    copies[6].start()
    for copy in copies[:2]:
        copy.wait()
    dense = dense_ref[...]
    pre_act = dot(dense, w_bottom_ref[...])
    sigma = jax.nn.sigmoid(pre_act)
    cross_ref[:, :EMB] = (pre_act * sigma).astype(BF16)
    table_t = table_ref[...]
    for t in range(0, TABLES, 2):
        both = [jnp.where(table_t == t + u, arrived, 0.0).astype(BF16) for u in range(2)]
        cross_ref[:, (t + 1) * EMB : (t + 3) * EMB] = dot(member, jnp.concatenate(both, axis=1)).astype(BF16)

    for copy in copies[2:6]:
        copy.wait()
    low_rank = dot(cross_ref[...], cross_u_ref[...]).astype(BF16)
    u_turned_ref[...] = cross_u_ref[...].T
    copies[6].wait()
    v_turned_ref[...] = cross_v_ref[...].T
    w_out = w_out_ref[...]
    mixed_ref[...] = (dot(low_rank, cross_v_ref[...]) + (bias_ref[...] + 1.0)) * w_out
    cross_f = cross_ref[...].astype(F32)
    logits = jnp.sum(cross_f * mixed_ref[...], axis=1, keepdims=True)
    logit_grad = jax.nn.sigmoid(logits) - labels_ref[...].astype(F32)
    mix_grad = (logit_grad * w_out * cross_f).astype(BF16)
    low_grad = dot(mix_grad, v_turned_ref[...]).astype(BF16)
    in_grad = logit_grad * mixed_ref[...] + dot(low_grad, u_turned_ref[...])
    pre_grad = (in_grad[:, :EMB] * (sigma * (1.0 + pre_act * (1.0 - sigma)))).astype(BF16)
    for t in range(TABLES):
        embed_ref[t * samples : (t + 1) * samples, :] = in_grad[:, (t + 1) * EMB : (t + 2) * EMB].astype(BF16)
    line = iota((1, 2 * PEERS), 1)
    line = lax.shift_right_logical(line, 1) * ROWS_A + CAP + (line & 1)
    wanted_ref[...] = onehot(iota((ALL_A, 2 * PEERS), 0) == line)
    embed_ref[TABLES * samples :, :] = dot(dense, pre_grad, 0, 0).astype(BF16)

    step = ALL_A // 2
    for c in range(ALL_A // step):
        rows = slice(c * step, (c + 1) * step)
        member_c = member_ref[rows, :]
        table_c = table_ref[rows, :]
        wide = [jnp.where(table_c == t, member_c, 0.0).astype(BF16) for t in range(TABLES)]
        wide = jnp.concatenate(wide + [wanted_ref[rows, :]], axis=1)
        out_ref[rows, :] = dot(wide, embed_ref[...]).astype(BF16)


def return_kernel(returned_ref, routed_ref, grads_ref, bottom_ref):
    returned = returned_ref[...]
    grads_ref[...] = dot(returned, routed_ref[...].astype(BF16), 0, 0).astype(BF16)
    slot = iota((8, ALL_A), 1)
    place = slot - divide_floor(slot, ROWS_A) * ROWS_A
    bottom_ref[...] = dot(onehot(place == iota((8, ALL_A), 0) + CAP), returned)


def total_kernel(grads_ref, bottom_ref, total_ref, message_ref):
    total = grads_ref[0].astype(F32)
    for s in range(1, grads_ref.shape[0]):
        total = total + grads_ref[s].astype(F32)
    total_ref[...] = total
    squares = jnp.sum(total * total, axis=0, keepdims=True)
    bottom = bottom_ref[...]
    message = jnp.concatenate([squares, bottom[0:1], bottom[1:2]], axis=1)
    for s in range(message_ref.shape[0]):
        message_ref[s] = message


def step_kernel(
    message_ref, total_ref, accum_ref, table_ref, steps_ref, block_ref, rows_ref, accum_out_ref, out_ref
):
    rows = accum_ref.shape[1]
    message = message_ref[0]
    for s in range(1, message_ref.shape[0]):
        message = message + message_ref[s]
    accum = accum_ref[...] + message[:, :rows] * (1.0 / EMB)
    accum_out_ref[...] = accum
    step = total_ref[...] * (1.0 / jnp.sqrt(accum))
    rows_ref[...] = table_ref[...] - LEARN_RATE * step
    block = block_ref[...]
    wide = jnp.concatenate([jnp.where(block == a, step, 0.0) for a in range(4)], axis=0).astype(BF16)
    payload = dot(steps_ref[...], wide, 1, 1)
    slot = iota((ALL_D, EMB), 0)
    place = slot - divide_floor(slot, ROWS_D) * ROWS_D
    payload = jnp.where(place == 4, message[:, rows : rows + EMB], payload)
    payload = jnp.where(place == 5, message[:, rows + EMB : rows + 2 * EMB], payload)
    out_ref[...] = payload.astype(BF16)


def final_kernel(served_ref, serving_ref, bottom_ref):
    served = served_ref[...]
    slot = iota((ALL_D, PEERS), 0) - iota((ALL_D, PEERS), 1) * ROWS_D
    picks = jnp.concatenate([onehot(slot == r) for r in range(ROWS_D)], axis=1)
    lines = dot(served, picks, 0, 0)
    serving_ref[...] = jnp.concatenate([lines[:, r * PEERS : (r + 1) * PEERS] for r in range(4)], axis=0).astype(BF16)
    line = iota((2 * PEERS, ALL_D), 0)
    slot = iota((2 * PEERS, ALL_D), 1)
    pick = onehot(slot == lax.shift_right_logical(line, 1) * ROWS_D + 4 + (line & 1))
    bottom_ref[...] = dot(pick, served)


def call(kernel, outs, *args, scratch=(), flops=0, hbm=(), limit=VMEM_LIMIT):
    moved = sum(x.size * x.dtype.itemsize for x in args)
    spaces = [pltpu.HBM if i in hbm else pltpu.VMEM for i in range(len(args))]
    return pl.pallas_call(
        kernel,
        out_shape=[jax.ShapeDtypeStruct(shape, kind) for shape, kind in outs],
        in_specs=[pl.BlockSpec(memory_space=space) for space in spaces],
        scratch_shapes=list(scratch),
        compiler_params=pltpu.CompilerParams(vmem_limit_bytes=limit),
        cost_estimate=pl.CostEstimate(flops=flops, bytes_accessed=moved, transcendentals=0),
    )(*args)


def over_rows(chunks, rows):
    split = chunks.reshape(PEERS, rows // 2, 2, EMB)
    split = lax.all_to_all(split, "rows", split_axis=0, concat_axis=0, tiled=True)
    return split.reshape(PEERS * rows, EMB)


def over_serve(pieces):
    return lax.all_to_all(pieces, "serve", split_axis=0, concat_axis=0, tiled=True)


def per_device(
    table_rows,
    row_accum,
    lookup_rows,
    bag_lengths,
    bag_owner,
    bag_target,
    bottom_in,
    labels,
    w_bottom,
    cross_u,
    cross_v,
    cross_bias,
    w_out,
    serve_owner,
):
    touched = table_rows.shape[0]
    lookups = lookup_rows.reshape(1, -1)
    lengths = bag_lengths.reshape(1, -1)
    bags = lengths.shape[1]
    owners = bag_owner.reshape(1, -1)
    targets = bag_target.reshape(1, -1)
    dense_in = bottom_in.reshape(-1, bottom_in.shape[-1])
    samples = dense_in.shape[0]
    width = cross_u.shape[0]
    serves = lax.axis_size("serve")
    cols = EMB // serves

    outgoing, slots = call(
        pool_kernel,
        [((ALL_A, EMB), BF16), ((1, bags), jnp.int32)],
        lengths,
        lookups,
        owners,
        targets,
        table_rows,
        scratch=(
            pltpu.VMEM(lengths.shape, jnp.int32),
            pltpu.VMEM(lookups.shape, jnp.int32),
            pltpu.VMEM(owners.shape, jnp.int32),
            pltpu.VMEM(targets.shape, jnp.int32),
            pltpu.VMEM(table_rows.shape, F32),
            pltpu.SemaphoreType.DMA((5,)),
        ),
        flops=2 * 700 * 10**6,
        hbm=range(5),
        limit=60 * 1024 * 1024,
    )
    arrived = over_rows(outgoing, ROWS_A)
    routed, steps_to, block, table_cols = call(
        ready_kernel,
        [
            ((ALL_A, touched), SMALL),
            ((ALL_D, touched), BF16),
            ((1, touched), jnp.int32),
            ((cols, touched), F32),
        ],
        lengths,
        lookups,
        slots,
        serve_owner.reshape(1, -1),
        table_rows,
        scratch=(pltpu.VMEM((EMB, touched), F32),),
        flops=2 * 1600 * 10**6,
        limit=60 * 1024 * 1024,
    )
    operands = (
        arrived,
        steps_to,
        dense_in,
        w_bottom,
        cross_u,
        cross_bias.reshape(1, -1),
        w_out.reshape(1, -1),
        labels.reshape(-1, 1),
        cross_v,
    )
    (replies,) = call(
        owner_kernel,
        [((ALL_A, EMB), BF16)],
        *operands,
        scratch=tuple(pltpu.VMEM(x.shape, x.dtype) for x in operands[2:])
        + (
            pltpu.VMEM((samples, width), BF16),
            pltpu.VMEM((samples, width), F32),
            pltpu.VMEM((samples * TABLES + 2 * PEERS, EMB), BF16),
            pltpu.VMEM((ALL_A, PEERS), BF16),
            pltpu.VMEM((ALL_A, PEERS), BF16),
            pltpu.VMEM((ALL_A, 2 * PEERS), BF16),
            pltpu.VMEM(cross_u.shape[::-1], BF16),
            pltpu.VMEM(cross_v.shape[::-1], BF16),
            pltpu.SemaphoreType.DMA((len(operands) - 2,)),
        ),
        flops=2 * 1600 * 10**6,
        hbm=range(1, len(operands)),
        limit=52 * 1024 * 1024,
    )
    returned = over_rows(replies, ROWS_A)
    grads, bottom = call(
        return_kernel,
        [((EMB, touched), BF16), ((8, EMB), F32)],
        returned,
        routed,
        flops=2 * 160 * 10**6,
    )
    pieces = over_serve(grads.reshape(serves, cols, touched))
    total, message = call(
        total_kernel,
        [((cols, touched), F32), ((serves, 1, touched + 2 * EMB), F32)],
        pieces,
        bottom,
    )
    messages = over_serve(message)
    new_rows, new_accum, steps = call(
        step_kernel,
        [((cols, touched), F32), ((1, touched), F32), ((ALL_D, EMB), BF16)],
        messages,
        total,
        row_accum.reshape(1, -1),
        table_cols,
        steps_to,
        block,
        flops=2 * 100 * 10**6,
    )
    served = over_rows(steps, ROWS_D)
    serving, grad_bottom = call(
        final_kernel, [((4 * EMB, PEERS), BF16), ((2 * PEERS, EMB), F32)], served, flops=2 * 50 * 10**6
    )
    serving = serving.reshape(16, cols, PEERS).transpose(2, 0, 1)[None]
    return (new_rows.T, new_accum.reshape(-1), serving, grad_bottom)


def solution(mesh):
    return jax.shard_map(
        per_device,
        mesh=mesh,
        in_specs=(
            P("rows", None),
            P("rows"),
            P("serve", "rows", None),
            P("serve", "rows", None),
            P("serve", "rows", None, None),
            P("serve", "rows", None),
            P("serve", "rows", None),
            P("serve", "rows"),
            P(),
            P(),
            P(),
            P(),
            P(),
            P("rows", None),
        ),
        out_specs=(P("rows", "serve"), P("rows"), P("rows", None, None, "serve"), P()),
        check_vma=False,
    )
```

```python
import functools

import jax
import jax.numpy as jnp
from jax import lax
from jax.experimental import pallas as pl
from jax.experimental.pallas import tpu as pltpu
from jax.sharding import PartitionSpec as P

TABLES = 26
LEARN_RATE = 0.1
EMB = 128
PEERS = 128
CAP = 8
ROWS_A = 10
ALL_A = PEERS * ROWS_A
ROWS_D = 6
ALL_D = PEERS * ROWS_D
F32 = jnp.float32
SMALL = jnp.int8
BF16 = jnp.bfloat16
VMEM_LIMIT = 32 * 1024 * 1024


def dot(a, b, ca=1, cb=0):
    return lax.dot_general(a, b, (((ca,), (cb,)), ((), ())), preferred_element_type=F32)


def iota(shape, dim):
    return lax.broadcasted_iota(jnp.int32, shape, dim)


def onehot(mask):
    return jnp.where(mask, 1.0, 0.0).astype(BF16)


def divide_floor(values, by):
    return jnp.floor((values.astype(F32) + 0.5) * (1.0 / by)).astype(jnp.int32)


def owner_place(owners):
    return owners


def fetch(sources, targets, sems):
    copies = [pltpu.make_async_copy(s, t, sems.at[i]) for i, (s, t) in enumerate(zip(sources, targets))]
    for copy in copies:
        copy.start()
    return copies


def bag_ends(lengths_ref):
    bags = lengths_ref.shape[1]
    row_id = iota((bags, bags), 0)
    col_id = iota((bags, bags), 1)
    lens = jnp.broadcast_to(lengths_ref[...].astype(F32), (8, bags)).astype(BF16)
    starts = dot(onehot(col_id < row_id), lens, 1, 1)[:, 0:1].astype(jnp.int32)
    ends = dot(onehot(col_id <= row_id), lens, 1, 1)[:, 0:1].astype(jnp.int32)
    return starts, ends


def pool_kernel(
    lengths_hbm,
    lookups_hbm,
    owners_hbm,
    targets_hbm,
    table_hbm,
    out_ref,
    slots_ref,
    lengths_ref,
    lookups_ref,
    owners_ref,
    targets_ref,
    table_ref,
    sems,
):
    copies = fetch(
        (lengths_hbm, lookups_hbm, owners_hbm, targets_hbm, table_hbm),
        (lengths_ref, lookups_ref, owners_ref, targets_ref, table_ref),
        sems,
    )
    bags = lengths_ref.shape[1]
    looks = lookups_ref.shape[1]
    touched = table_ref.shape[0]
    for copy in copies[:4]:
        copy.wait()
    owners = owners_ref[...]
    of_owner = jnp.where(iota((PEERS, bags), 0) == owners, 1.0, 0.0)
    before = dot(of_owner.astype(BF16), onehot(iota((bags, bags), 0) < iota((bags, bags), 1)))
    rank = jnp.sum(before * of_owner, axis=0, keepdims=True).astype(jnp.int32)
    slots = owner_place(owners) * ROWS_A + rank
    slots_ref[...] = slots
    targets = targets_ref[...]
    sample = divide_floor(targets, TABLES)
    table_of = targets - sample * TABLES
    lane = iota((EMB, bags), 0)
    names = jnp.where(lane == rank, sample + 1, 0) + jnp.where(lane == rank + CAP, table_of, 0)
    names = dot(of_owner.astype(BF16), names.astype(F32).astype(BF16), 1, 1).astype(BF16)
    copies[4].wait()
    table = table_ref[...]
    high = table.astype(BF16)
    low = (table - high.astype(F32)).astype(BF16)
    starts, ends = bag_ends(lengths_ref)
    place = iota((bags, looks), 1)
    in_bag = onehot((place >= starts) & (place < ends))
    lookups = jnp.broadcast_to(lookups_ref[...].astype(F32), (128, looks)).T.astype(jnp.int32)
    both = jnp.concatenate([high, low], axis=1)
    lane = iota((512, 128), 1)
    sums = 0.0
    for first in range(0, looks, 512):
        part = lookups[first : first + 512]
        goes = jnp.concatenate([onehot(part == lane + c) for c in range(0, touched, 128)], axis=1)
        sums = sums + dot(in_bag[:, first : first + 512], dot(goes, both).astype(BF16))
    pooled = (sums[:, :EMB] + sums[:, EMB:]).astype(BF16)
    payload = dot(onehot(iota((ALL_A, bags), 0) == slots), pooled)
    ninth = onehot(iota((ALL_A, PEERS), 0) == owner_place(iota((ALL_A, PEERS), 1)) * ROWS_A + CAP)
    out_ref[...] = (payload + dot(ninth, names)).astype(BF16)


def ready_kernel(
    lengths_ref,
    lookups_ref,
    slots_ref,
    owners_ref,
    table_ref,
    routed_ref,
    steps_ref,
    block_ref,
    cols_ref,
    turned_ref,
):
    rows = owners_ref.shape[1]
    bags = slots_ref.shape[1]
    looks = lookups_ref.shape[1]
    starts, ends = bag_ends(lengths_ref)
    place = iota((bags, looks), 1)
    in_bag = onehot((place >= starts) & (place < ends))
    of_row = onehot(iota((rows, looks), 0) == lookups_ref[...])
    counts = dot(in_bag, of_row, 1, 1).astype(BF16)
    routed_ref[...] = dot(onehot(iota((ALL_A, bags), 0) == slots_ref[...]), counts).astype(jnp.int32).astype(SMALL)
    owners = owners_ref[...]
    of_owner = jnp.where(iota((PEERS, rows), 0) == owners, 1.0, 0.0)
    before = dot(of_owner.astype(BF16), onehot(iota((rows, rows), 0) < iota((rows, rows), 1)))
    rank = jnp.sum(before * of_owner, axis=0, keepdims=True).astype(jnp.int32)
    row_of = lax.shift_right_logical(rank, 2)
    block_ref[...] = rank - 4 * row_of
    steps_ref[...] = onehot(iota((ALL_D, rows), 0) == owner_place(owners) * ROWS_D + row_of)
    turned_ref[...] = table_ref[...].T
    cols = cols_ref.shape[0]
    cols_ref[...] = turned_ref[pl.ds(pl.multiple_of(lax.axis_index("serve") * cols, cols), cols), :]


def owner_kernel(*refs):
    arrived_ref, _, *refs = refs
    count = (len(refs) - 10) // 2
    sources, out_ref = refs[:count], refs[count]
    targets = refs[count + 1 : 2 * count + 1]
    cross_ref, mixed_ref, embed_ref, member_ref, table_ref, wanted_ref, *refs = refs[2 * count + 1 :]
    u_turned_ref, v_turned_ref, sems = refs
    copies = [pltpu.make_async_copy(s, t, sems.at[i]) for i, (s, t) in enumerate(zip(sources, targets))]
    dense_ref, w_bottom_ref, cross_u_ref, bias_ref, w_out_ref, labels_ref, cross_v_ref = targets
    for copy in copies[:6]:
        copy.start()
    samples = dense_ref.shape[0]
    peer = iota((PEERS, ALL_A), 0) * ROWS_A
    slot = iota((PEERS, ALL_A), 1)
    name_row = onehot(slot == peer + CAP)
    chunk = onehot(iota((PEERS, ALL_A), 0) == divide_floor(iota((1, ALL_A), 1), ROWS_A))
    arrived = arrived_ref[...]
    names = dot(name_row, arrived).astype(BF16)
    spread = dot(names, chunk, 0, 0)
    place = iota((1, ALL_A), 1)
    place = place - divide_floor(place, ROWS_A) * ROWS_A
    picks = iota((CAP, ALL_A), 0) == place
    sample_row = jnp.sum(jnp.where(picks, spread[:CAP], 0.0), axis=0, keepdims=True)
    table_row = jnp.sum(jnp.where(picks, spread[CAP : 2 * CAP], 0.0), axis=0, keepdims=True)
    member_f = jnp.where(sample_row.astype(jnp.int32) == iota((samples, ALL_A), 0) + 1, 1.0, 0.0)
    member = member_f.astype(BF16)
    member_ref[...] = member_f.T.astype(BF16)
    table_ref[...] = jnp.broadcast_to(table_row, (samples, ALL_A)).T.astype(BF16)

    copies[6].start()
    for copy in copies[:2]:
        copy.wait()
    dense = dense_ref[...]
    pre_act = dot(dense, w_bottom_ref[...])
    sigma = jax.nn.sigmoid(pre_act)
    cross_ref[:, :EMB] = (pre_act * sigma).astype(BF16)
    table_t = table_ref[...]
    for t in range(0, TABLES, 2):
        both = [jnp.where(table_t == t + u, arrived, 0.0).astype(BF16) for u in range(2)]
        cross_ref[:, (t + 1) * EMB : (t + 3) * EMB] = dot(member, jnp.concatenate(both, axis=1)).astype(BF16)

    for copy in copies[2:6]:
        copy.wait()
    low_rank = dot(cross_ref[...], cross_u_ref[...]).astype(BF16)
    u_turned_ref[...] = cross_u_ref[...].T
    copies[6].wait()
    v_turned_ref[...] = cross_v_ref[...].T
    w_out = w_out_ref[...]
    mixed_ref[...] = (dot(low_rank, cross_v_ref[...]) + (bias_ref[...] + 1.0)) * w_out
    cross_f = cross_ref[...].astype(F32)
    logits = jnp.sum(cross_f * mixed_ref[...], axis=1, keepdims=True)
    logit_grad = jax.nn.sigmoid(logits) - labels_ref[...].astype(F32)
    mix_grad = (logit_grad * w_out * cross_f).astype(BF16)
    low_grad = dot(mix_grad, v_turned_ref[...]).astype(BF16)
    in_grad = logit_grad * mixed_ref[...] + dot(low_grad, u_turned_ref[...])
    pre_grad = (in_grad[:, :EMB] * (sigma * (1.0 + pre_act * (1.0 - sigma)))).astype(BF16)
    for t in range(TABLES):
        embed_ref[t * samples : (t + 1) * samples, :] = in_grad[:, (t + 1) * EMB : (t + 2) * EMB].astype(BF16)
    line = iota((1, 2 * PEERS), 1)
    line = lax.shift_right_logical(line, 1) * ROWS_A + CAP + (line & 1)
    wanted_ref[...] = onehot(iota((ALL_A, 2 * PEERS), 0) == line)
    embed_ref[TABLES * samples :, :] = dot(dense, pre_grad, 0, 0).astype(BF16)

    step = ALL_A // 2
    for c in range(ALL_A // step):
        rows = slice(c * step, (c + 1) * step)
        member_c = member_ref[rows, :]
        table_c = table_ref[rows, :]
        wide = [jnp.where(table_c == t, member_c, 0.0).astype(BF16) for t in range(TABLES)]
        wide = jnp.concatenate(wide + [wanted_ref[rows, :]], axis=1)
        out_ref[rows, :] = dot(wide, embed_ref[...]).astype(BF16)


def return_kernel(returned_ref, routed_ref, grads_ref, bottom_ref):
    returned = returned_ref[...]
    grads_ref[...] = dot(returned, routed_ref[...].astype(BF16), 0, 0).astype(BF16)
    slot = iota((8, ALL_A), 1)
    place = slot - divide_floor(slot, ROWS_A) * ROWS_A
    bottom_ref[...] = dot(onehot(place == iota((8, ALL_A), 0) + CAP), returned)


def total_kernel(grads_ref, bottom_ref, total_ref, message_ref):
    total = grads_ref[0].astype(F32)
    for s in range(1, grads_ref.shape[0]):
        total = total + grads_ref[s].astype(F32)
    total_ref[...] = total
    squares = jnp.sum(total * total, axis=0, keepdims=True)
    bottom = bottom_ref[...]
    message = jnp.concatenate([squares, bottom[0:1], bottom[1:2]], axis=1)
    for s in range(message_ref.shape[0]):
        message_ref[s] = message


def step_kernel(
    message_ref, total_ref, accum_ref, table_ref, steps_ref, block_ref, rows_ref, accum_out_ref, out_ref
):
    rows = accum_ref.shape[1]
    message = message_ref[0]
    for s in range(1, message_ref.shape[0]):
        message = message + message_ref[s]
    accum = accum_ref[...] + message[:, :rows] * (1.0 / EMB)
    accum_out_ref[...] = accum
    step = total_ref[...] * (1.0 / jnp.sqrt(accum))
    rows_ref[...] = table_ref[...] - LEARN_RATE * step
    block = block_ref[...]
    wide = jnp.concatenate([jnp.where(block == a, step, 0.0) for a in range(4)], axis=0).astype(BF16)
    payload = dot(steps_ref[...], wide, 1, 1)
    slot = iota((ALL_D, EMB), 0)
    place = slot - divide_floor(slot, ROWS_D) * ROWS_D
    payload = jnp.where(place == 4, message[:, rows : rows + EMB], payload)
    payload = jnp.where(place == 5, message[:, rows + EMB : rows + 2 * EMB], payload)
    out_ref[...] = payload.astype(BF16)


def final_kernel(served_ref, serving_ref, bottom_ref):
    served = served_ref[...]
    slot = iota((ALL_D, PEERS), 0) - iota((ALL_D, PEERS), 1) * ROWS_D
    picks = jnp.concatenate([onehot(slot == r) for r in range(ROWS_D)], axis=1)
    lines = dot(served, picks, 0, 0)
    serving_ref[...] = jnp.concatenate([lines[:, r * PEERS : (r + 1) * PEERS] for r in range(4)], axis=0).astype(BF16)
    line = iota((2 * PEERS, ALL_D), 0)
    slot = iota((2 * PEERS, ALL_D), 1)
    pick = onehot(slot == lax.shift_right_logical(line, 1) * ROWS_D + 4 + (line & 1))
    bottom_ref[...] = dot(pick, served)


def call(kernel, outs, *args, scratch=(), flops=0, hbm=(), limit=VMEM_LIMIT):
    moved = sum(x.size * x.dtype.itemsize for x in args)
    spaces = [pltpu.HBM if i in hbm else pltpu.VMEM for i in range(len(args))]
    return pl.pallas_call(
        kernel,
        out_shape=[jax.ShapeDtypeStruct(shape, kind) for shape, kind in outs],
        in_specs=[pl.BlockSpec(memory_space=space) for space in spaces],
        scratch_shapes=list(scratch),
        compiler_params=pltpu.CompilerParams(vmem_limit_bytes=limit),
        cost_estimate=pl.CostEstimate(flops=flops, bytes_accessed=moved, transcendentals=0),
    )(*args)


def over_rows(chunks, rows):
    split = chunks.reshape(PEERS, rows // 2, 2, EMB)
    split = lax.all_to_all(split, "rows", split_axis=0, concat_axis=0, tiled=True)
    return split.reshape(PEERS * rows, EMB)


def over_serve(pieces):
    return lax.all_to_all(pieces, "serve", split_axis=0, concat_axis=0, tiled=True)


def per_device(
    table_rows,
    row_accum,
    lookup_rows,
    bag_lengths,
    bag_owner,
    bag_target,
    bottom_in,
    labels,
    w_bottom,
    cross_u,
    cross_v,
    cross_bias,
    w_out,
    serve_owner,
):
    touched = table_rows.shape[0]
    lookups = lookup_rows.reshape(1, -1)
    lengths = bag_lengths.reshape(1, -1)
    bags = lengths.shape[1]
    owners = bag_owner.reshape(1, -1)
    targets = bag_target.reshape(1, -1)
    dense_in = bottom_in.reshape(-1, bottom_in.shape[-1])
    samples = dense_in.shape[0]
    width = cross_u.shape[0]
    serves = lax.axis_size("serve")
    cols = EMB // serves

    outgoing, slots = call(
        pool_kernel,
        [((ALL_A, EMB), BF16), ((1, bags), jnp.int32)],
        lengths,
        lookups,
        owners,
        targets,
        table_rows,
        scratch=(
            pltpu.VMEM(lengths.shape, jnp.int32),
            pltpu.VMEM(lookups.shape, jnp.int32),
            pltpu.VMEM(owners.shape, jnp.int32),
            pltpu.VMEM(targets.shape, jnp.int32),
            pltpu.VMEM(table_rows.shape, F32),
            pltpu.SemaphoreType.DMA((5,)),
        ),
        flops=2 * 700 * 10**6,
        hbm=range(5),
        limit=60 * 1024 * 1024,
    )
    arrived = over_rows(outgoing, ROWS_A)
    routed, steps_to, block, table_cols = call(
        ready_kernel,
        [
            ((ALL_A, touched), SMALL),
            ((ALL_D, touched), BF16),
            ((1, touched), jnp.int32),
            ((cols, touched), F32),
        ],
        lengths,
        lookups,
        slots,
        serve_owner.reshape(1, -1),
        table_rows,
        scratch=(pltpu.VMEM((EMB, touched), F32),),
        flops=2 * 1600 * 10**6,
        limit=60 * 1024 * 1024,
    )
    operands = (
        arrived,
        block,
        dense_in,
        w_bottom,
        cross_u,
        cross_bias.reshape(1, -1),
        w_out.reshape(1, -1),
        labels.reshape(-1, 1),
        cross_v,
    )
    (replies,) = call(
        owner_kernel,
        [((ALL_A, EMB), BF16)],
        *operands,
        scratch=tuple(pltpu.VMEM(x.shape, x.dtype) for x in operands[2:])
        + (
            pltpu.VMEM((samples, width), BF16),
            pltpu.VMEM((samples, width), F32),
            pltpu.VMEM((samples * TABLES + 2 * PEERS, EMB), BF16),
            pltpu.VMEM((ALL_A, PEERS), BF16),
            pltpu.VMEM((ALL_A, PEERS), BF16),
            pltpu.VMEM((ALL_A, 2 * PEERS), BF16),
            pltpu.VMEM(cross_u.shape[::-1], BF16),
            pltpu.VMEM(cross_v.shape[::-1], BF16),
            pltpu.SemaphoreType.DMA((len(operands) - 2,)),
        ),
        flops=2 * 1600 * 10**6,
        hbm=range(1, len(operands)),
        limit=51 * 1024 * 1024,
    )
    returned = over_rows(replies, ROWS_A)
    grads, bottom = call(
        return_kernel,
        [((EMB, touched), BF16), ((8, EMB), F32)],
        returned,
        routed,
        flops=2 * 160 * 10**6,
    )
    pieces = over_serve(grads.reshape(serves, cols, touched))
    total, message = call(
        total_kernel,
        [((cols, touched), F32), ((serves, 1, touched + 2 * EMB), F32)],
        pieces,
        bottom,
    )
    messages = over_serve(message)
    new_rows, new_accum, steps = call(
        step_kernel,
        [((cols, touched), F32), ((1, touched), F32), ((ALL_D, EMB), BF16)],
        messages,
        total,
        row_accum.reshape(1, -1),
        table_cols,
        steps_to,
        block,
        flops=2 * 100 * 10**6,
    )
    served = over_rows(steps, ROWS_D)
    serving, grad_bottom = call(
        final_kernel, [((4 * EMB, PEERS), BF16), ((2 * PEERS, EMB), F32)], served, flops=2 * 50 * 10**6
    )
    serving = serving.reshape(16, cols, PEERS).transpose(2, 0, 1)[None]
    return (new_rows.T, new_accum.reshape(-1), serving, grad_bottom)


def solution(mesh):
    return jax.shard_map(
        per_device,
        mesh=mesh,
        in_specs=(
            P("rows", None),
            P("rows"),
            P("serve", "rows", None),
            P("serve", "rows", None),
            P("serve", "rows", None, None),
            P("serve", "rows", None),
            P("serve", "rows", None),
            P("serve", "rows"),
            P(),
            P(),
            P(),
            P(),
            P(),
            P("rows", None),
        ),
        out_specs=(P("rows", "serve"), P("rows"), P("rows", None, None, "serve"), P()),
        check_vma=False,
    )
```

```python
import functools

import jax
import jax.numpy as jnp
from jax import lax
from jax.experimental import pallas as pl
from jax.experimental.pallas import tpu as pltpu
from jax.sharding import PartitionSpec as P

TABLES = 26
LEARN_RATE = 0.1
EMB = 128
PEERS = 128
CAP = 8
ROWS_A = 10
ALL_A = PEERS * ROWS_A
ROWS_D = 6
ALL_D = PEERS * ROWS_D
F32 = jnp.float32
SMALL = jnp.int8
BF16 = jnp.bfloat16
VMEM_LIMIT = 32 * 1024 * 1024


def dot(a, b, ca=1, cb=0):
    return lax.dot_general(a, b, (((ca,), (cb,)), ((), ())), preferred_element_type=F32)


def iota(shape, dim):
    return lax.broadcasted_iota(jnp.int32, shape, dim)


def onehot(mask):
    return jnp.where(mask, 1.0, 0.0).astype(BF16)


def divide_floor(values, by):
    return jnp.floor((values.astype(F32) + 0.5) * (1.0 / by)).astype(jnp.int32)


def owner_place(owners):
    return owners


def fetch(sources, targets, sems):
    copies = [pltpu.make_async_copy(s, t, sems.at[i]) for i, (s, t) in enumerate(zip(sources, targets))]
    for copy in copies:
        copy.start()
    return copies


def bag_ends(lengths_ref, earlier):
    lens = jnp.broadcast_to(lengths_ref[...].astype(F32), (8, lengths_ref.shape[1]))
    starts = dot(lens.astype(BF16), earlier)
    return starts.T[:, 0:1].astype(jnp.int32), (starts + lens).T[:, 0:1].astype(jnp.int32)


def earlier_than(count):
    return onehot(iota((count, count), 0) < iota((count, count), 1))


def pool_kernel(
    lengths_hbm,
    lookups_hbm,
    owners_hbm,
    targets_hbm,
    table_hbm,
    out_ref,
    slots_ref,
    lengths_ref,
    lookups_ref,
    owners_ref,
    targets_ref,
    table_ref,
    sems,
):
    copies = fetch(
        (lengths_hbm, lookups_hbm, owners_hbm, targets_hbm, table_hbm),
        (lengths_ref, lookups_ref, owners_ref, targets_ref, table_ref),
        sems,
    )
    bags = lengths_ref.shape[1]
    looks = lookups_ref.shape[1]
    touched = table_ref.shape[0]
    for copy in copies[:4]:
        copy.wait()
    earlier = earlier_than(bags)
    starts, ends = bag_ends(lengths_ref, earlier)
    owners = owners_ref[...]
    of_owner = jnp.where(iota((PEERS, bags), 0) == owners, 1.0, 0.0)
    before = dot(of_owner.astype(BF16), earlier)
    rank = jnp.sum(before * of_owner, axis=0, keepdims=True).astype(jnp.int32)
    slots = owner_place(owners) * ROWS_A + rank
    slots_ref[...] = slots
    targets = targets_ref[...]
    sample = divide_floor(targets, TABLES)
    table_of = targets - sample * TABLES
    lane = iota((EMB, bags), 0)
    names = jnp.where(lane == rank, sample + 1, 0) + jnp.where(lane == rank + CAP, table_of, 0)
    names = dot(of_owner.astype(BF16), names.astype(F32).astype(BF16), 1, 1).astype(BF16)
    copies[4].wait()
    table = table_ref[...]
    high = table.astype(BF16)
    low = (table - high.astype(F32)).astype(BF16)
    place = iota((bags, looks), 1)
    in_bag = onehot((place >= starts) & (place < ends))
    lookups = jnp.broadcast_to(lookups_ref[...].astype(F32), (128, looks)).T.astype(jnp.int32)
    both = jnp.concatenate([high, low], axis=1)
    lane = iota((512, 128), 1)
    sums = 0.0
    for first in range(0, looks, 512):
        part = lookups[first : first + 512]
        goes = jnp.concatenate([onehot(part == lane + c) for c in range(0, touched, 128)], axis=1)
        sums = sums + dot(in_bag[:, first : first + 512], dot(goes, both).astype(BF16))
    pooled = (sums[:, :EMB] + sums[:, EMB:]).astype(BF16)
    step = ALL_A // 2
    for c in range(0, ALL_A, step):
        ninth = onehot(iota((step, PEERS), 0) + c == iota((1, PEERS), 1) * ROWS_A + CAP)
        payload = dot(onehot(iota((step, bags), 0) + c == slots), pooled) + dot(ninth, names)
        out_ref[c : c + step, :] = payload.astype(BF16)


def ready_kernel(
    lengths_ref,
    lookups_ref,
    slots_ref,
    owners_ref,
    table_ref,
    cross_v_hbm,
    routed_ref,
    steps_ref,
    block_ref,
    cols_ref,
    cross_v_out,
    turned_ref,
    sem,
):
    handed = pltpu.make_async_copy(cross_v_hbm, cross_v_out, sem)
    handed.start()
    rows = owners_ref.shape[1]
    bags = slots_ref.shape[1]
    looks = lookups_ref.shape[1]
    starts, ends = bag_ends(lengths_ref, earlier_than(bags))
    place = iota((bags, looks), 1)
    in_bag = onehot((place >= starts) & (place < ends))
    of_row = onehot(iota((rows, looks), 0) == lookups_ref[...])
    counts = dot(in_bag, of_row, 1, 1).astype(BF16)
    routed_ref[...] = dot(onehot(iota((ALL_A, bags), 0) == slots_ref[...]), counts).astype(jnp.int32).astype(SMALL)
    owners = owners_ref[...]
    of_owner = jnp.where(iota((PEERS, rows), 0) == owners, 1.0, 0.0)
    before = dot(of_owner.astype(BF16), onehot(iota((rows, rows), 0) < iota((rows, rows), 1)))
    rank = jnp.sum(before * of_owner, axis=0, keepdims=True).astype(jnp.int32)
    row_of = lax.shift_right_logical(rank, 2)
    block_ref[...] = rank - 4 * row_of
    steps_ref[...] = onehot(iota((ALL_D, rows), 0) == owner_place(owners) * ROWS_D + row_of)
    turned_ref[...] = table_ref[...].T
    cols = cols_ref.shape[0]
    cols_ref[...] = turned_ref[pl.ds(pl.multiple_of(lax.axis_index("serve") * cols, cols), cols), :]
    handed.wait()


def owner_kernel(*refs):
    arrived_ref, cross_u_ref, *refs = refs
    count = (len(refs) - 10) // 2
    sources, out_ref = refs[:count], refs[count]
    targets = refs[count + 1 : 2 * count + 1]
    cross_ref, mixed_ref, embed_ref, member_ref, table_ref, wanted_ref, *refs = refs[2 * count + 1 :]
    u_turned_ref, v_turned_ref, sems = refs
    copies = [pltpu.make_async_copy(s, t, sems.at[i]) for i, (s, t) in enumerate(zip(sources, targets))]
    dense_ref, w_bottom_ref, bias_ref, w_out_ref, labels_ref, cross_v_ref = targets
    for copy in copies:
        copy.start()
    samples = dense_ref.shape[0]
    peer = iota((PEERS, ALL_A), 0) * ROWS_A
    slot = iota((PEERS, ALL_A), 1)
    name_row = onehot(slot == peer + CAP)
    chunk = onehot(iota((PEERS, ALL_A), 0) == divide_floor(iota((1, ALL_A), 1), ROWS_A))
    arrived = arrived_ref[...]
    names = dot(name_row, arrived).astype(BF16)
    spread = dot(names, chunk, 0, 0)
    place = iota((1, ALL_A), 1)
    place = place - divide_floor(place, ROWS_A) * ROWS_A
    picks = iota((CAP, ALL_A), 0) == place
    sample_row = jnp.sum(jnp.where(picks, spread[:CAP], 0.0), axis=0, keepdims=True)
    table_row = jnp.sum(jnp.where(picks, spread[CAP : 2 * CAP], 0.0), axis=0, keepdims=True)
    member_f = jnp.where(sample_row.astype(jnp.int32) == iota((samples, ALL_A), 0) + 1, 1.0, 0.0)
    member = member_f.astype(BF16)
    member_ref[...] = member_f.T.astype(BF16)
    table_ref[...] = jnp.broadcast_to(table_row, (samples, ALL_A)).T.astype(BF16)

    for copy in copies[:2]:
        copy.wait()
    dense = dense_ref[...]
    pre_act = dot(dense, w_bottom_ref[...])
    sigma = jax.nn.sigmoid(pre_act)
    cross_ref[:, :EMB] = (pre_act * sigma).astype(BF16)
    table_t = table_ref[...]
    for t in range(0, TABLES, 2):
        both = [jnp.where(table_t == t + u, arrived, 0.0).astype(BF16) for u in range(2)]
        cross_ref[:, (t + 1) * EMB : (t + 3) * EMB] = dot(member, jnp.concatenate(both, axis=1)).astype(BF16)

    for copy in copies[2:5]:
        copy.wait()
    low_rank = dot(cross_ref[...], cross_u_ref[...]).astype(BF16)
    u_turned_ref[...] = cross_u_ref[...].T
    copies[5].wait()
    v_turned_ref[...] = cross_v_ref[...].T
    w_out = w_out_ref[...]
    mixed_ref[...] = (dot(low_rank, cross_v_ref[...]) + (bias_ref[...] + 1.0)) * w_out
    cross_f = cross_ref[...].astype(F32)
    logits = jnp.sum(cross_f * mixed_ref[...], axis=1, keepdims=True)
    logit_grad = jax.nn.sigmoid(logits) - labels_ref[...].astype(F32)
    mix_grad = (logit_grad * w_out * cross_f).astype(BF16)
    low_grad = dot(mix_grad, v_turned_ref[...]).astype(BF16)
    in_grad = logit_grad * mixed_ref[...] + dot(low_grad, u_turned_ref[...])
    pre_grad = (in_grad[:, :EMB] * (sigma * (1.0 + pre_act * (1.0 - sigma)))).astype(BF16)
    for t in range(TABLES):
        embed_ref[t * samples : (t + 1) * samples, :] = in_grad[:, (t + 1) * EMB : (t + 2) * EMB].astype(BF16)
    line = iota((1, 2 * PEERS), 1)
    line = lax.shift_right_logical(line, 1) * ROWS_A + CAP + (line & 1)
    wanted_ref[...] = onehot(iota((ALL_A, 2 * PEERS), 0) == line)
    embed_ref[TABLES * samples :, :] = dot(dense, pre_grad, 0, 0).astype(BF16)

    step = ALL_A // 2
    for c in range(ALL_A // step):
        rows = slice(c * step, (c + 1) * step)
        member_c = member_ref[rows, :]
        table_c = table_ref[rows, :]
        wide = [jnp.where(table_c == t, member_c, 0.0).astype(BF16) for t in range(TABLES)]
        wide = jnp.concatenate(wide + [wanted_ref[rows, :]], axis=1)
        out_ref[rows, :] = dot(wide, embed_ref[...]).astype(BF16)


def return_kernel(returned_ref, routed_ref, grads_ref, bottom_ref):
    returned = returned_ref[...]
    grads_ref[...] = dot(returned, routed_ref[...].astype(BF16), 0, 0).astype(BF16)
    slot = iota((8, ALL_A), 1)
    place = slot - divide_floor(slot, ROWS_A) * ROWS_A
    bottom_ref[...] = dot(onehot(place == iota((8, ALL_A), 0) + CAP), returned)


def total_kernel(grads_ref, bottom_ref, total_ref, message_ref):
    total = grads_ref[0].astype(F32)
    for s in range(1, grads_ref.shape[0]):
        total = total + grads_ref[s].astype(F32)
    total_ref[...] = total
    squares = jnp.sum(total * total, axis=0, keepdims=True)
    bottom = bottom_ref[...]
    message = jnp.concatenate([squares, bottom[0:1], bottom[1:2]], axis=1)
    for s in range(message_ref.shape[0]):
        message_ref[s] = message


def step_kernel(
    message_ref, total_ref, accum_ref, table_ref, steps_ref, block_ref, rows_ref, accum_out_ref, out_ref
):
    rows = accum_ref.shape[1]
    message = message_ref[0]
    for s in range(1, message_ref.shape[0]):
        message = message + message_ref[s]
    accum = accum_ref[...] + message[:, :rows] * (1.0 / EMB)
    accum_out_ref[...] = accum
    step = total_ref[...] * (1.0 / jnp.sqrt(accum))
    rows_ref[...] = table_ref[...] - LEARN_RATE * step
    block = block_ref[...]
    wide = jnp.concatenate([jnp.where(block == a, step, 0.0) for a in range(4)], axis=0).astype(BF16)
    payload = dot(steps_ref[...], wide, 1, 1)
    slot = iota((ALL_D, EMB), 0)
    place = slot - divide_floor(slot, ROWS_D) * ROWS_D
    payload = jnp.where(place == 4, message[:, rows : rows + EMB], payload)
    payload = jnp.where(place == 5, message[:, rows + EMB : rows + 2 * EMB], payload)
    out_ref[...] = payload.astype(BF16)


def final_kernel(served_ref, serving_ref, bottom_ref):
    served = served_ref[...]
    slot = iota((ALL_D, PEERS), 0) - iota((ALL_D, PEERS), 1) * ROWS_D
    picks = jnp.concatenate([onehot(slot == r) for r in range(ROWS_D)], axis=1)
    lines = dot(served, picks, 0, 0)
    serving_ref[...] = jnp.concatenate([lines[:, r * PEERS : (r + 1) * PEERS] for r in range(4)], axis=0).astype(BF16)
    line = iota((2 * PEERS, ALL_D), 0)
    slot = iota((2 * PEERS, ALL_D), 1)
    pick = onehot(slot == lax.shift_right_logical(line, 1) * ROWS_D + 4 + (line & 1))
    bottom_ref[...] = dot(pick, served)


def call(kernel, outs, *args, scratch=(), flops=0, hbm=(), hbm_out=(), limit=VMEM_LIMIT):
    moved = sum(x.size * x.dtype.itemsize for x in args)
    spaces = [pltpu.HBM if i in hbm else pltpu.VMEM for i in range(len(args))]
    return pl.pallas_call(
        kernel,
        out_shape=[jax.ShapeDtypeStruct(shape, kind) for shape, kind in outs],
        in_specs=[pl.BlockSpec(memory_space=space) for space in spaces],
        out_specs=[pl.BlockSpec(memory_space=pltpu.HBM if i in hbm_out else pltpu.VMEM) for i in range(len(outs))],
        scratch_shapes=list(scratch),
        compiler_params=pltpu.CompilerParams(vmem_limit_bytes=limit),
        cost_estimate=pl.CostEstimate(flops=flops, bytes_accessed=moved, transcendentals=0),
    )(*args)


def over_rows(chunks, rows):
    split = chunks.reshape(PEERS, rows // 2, 2, EMB)
    split = lax.all_to_all(split, "rows", split_axis=0, concat_axis=0, tiled=True)
    return split.reshape(PEERS * rows, EMB)


def over_serve(pieces):
    return lax.all_to_all(pieces, "serve", split_axis=0, concat_axis=0, tiled=True)


def per_device(
    table_rows,
    row_accum,
    lookup_rows,
    bag_lengths,
    bag_owner,
    bag_target,
    bottom_in,
    labels,
    w_bottom,
    cross_u,
    cross_v,
    cross_bias,
    w_out,
    serve_owner,
):
    touched = table_rows.shape[0]
    lookups = lookup_rows.reshape(1, -1)
    lengths = bag_lengths.reshape(1, -1)
    bags = lengths.shape[1]
    owners = bag_owner.reshape(1, -1)
    targets = bag_target.reshape(1, -1)
    dense_in = bottom_in.reshape(-1, bottom_in.shape[-1])
    samples = dense_in.shape[0]
    width = cross_u.shape[0]
    serves = lax.axis_size("serve")
    cols = EMB // serves

    outgoing, slots = call(
        pool_kernel,
        [((ALL_A, EMB), BF16), ((1, bags), jnp.int32)],
        lengths,
        lookups,
        owners,
        targets,
        table_rows,
        scratch=(
            pltpu.VMEM(lengths.shape, jnp.int32),
            pltpu.VMEM(lookups.shape, jnp.int32),
            pltpu.VMEM(owners.shape, jnp.int32),
            pltpu.VMEM(targets.shape, jnp.int32),
            pltpu.VMEM(table_rows.shape, F32),
            pltpu.SemaphoreType.DMA((5,)),
        ),
        flops=2 * 700 * 10**6,
        hbm=range(5),
        limit=60 * 1024 * 1024,
    )
    arrived = over_rows(outgoing, ROWS_A)
    routed, steps_to, block, table_cols, cross_v = call(
        ready_kernel,
        [
            ((ALL_A, touched), SMALL),
            ((ALL_D, touched), BF16),
            ((1, touched), jnp.int32),
            ((cols, touched), F32),
            (cross_v.shape, BF16),
        ],
        lengths,
        lookups,
        slots,
        serve_owner.reshape(1, -1),
        table_rows,
        cross_v,
        scratch=(pltpu.VMEM((EMB, touched), F32), pltpu.SemaphoreType.DMA(())),
        hbm=(5,),
        hbm_out=(4,),
        flops=2 * 1600 * 10**6,
        limit=60 * 1024 * 1024,
    )
    operands = (
        arrived,
        cross_u,
        dense_in,
        w_bottom,
        cross_bias.reshape(1, -1),
        w_out.reshape(1, -1),
        labels.reshape(-1, 1),
        cross_v,
    )
    (replies,) = call(
        owner_kernel,
        [((ALL_A, EMB), BF16)],
        *operands,
        scratch=tuple(pltpu.VMEM(x.shape, x.dtype) for x in operands[2:])
        + (
            pltpu.VMEM((samples, width), BF16),
            pltpu.VMEM((samples, width), F32),
            pltpu.VMEM((samples * TABLES + 2 * PEERS, EMB), BF16),
            pltpu.VMEM((ALL_A, PEERS), BF16),
            pltpu.VMEM((ALL_A, PEERS), BF16),
            pltpu.VMEM((ALL_A, 2 * PEERS), BF16),
            pltpu.VMEM(cross_u.shape[::-1], BF16),
            pltpu.VMEM(cross_v.shape[::-1], BF16),
            pltpu.SemaphoreType.DMA((len(operands) - 2,)),
        ),
        flops=2 * 1600 * 10**6,
        hbm=range(2, len(operands)),
        limit=51 * 1024 * 1024,
    )
    returned = over_rows(replies, ROWS_A)
    grads, bottom = call(
        return_kernel,
        [((EMB, touched), BF16), ((8, EMB), F32)],
        returned,
        routed,
        flops=2 * 160 * 10**6,
    )
    pieces = over_serve(grads.reshape(serves, cols, touched))
    total, message = call(
        total_kernel,
        [((cols, touched), F32), ((serves, 1, touched + 2 * EMB), F32)],
        pieces,
        bottom,
    )
    messages = over_serve(message)
    new_rows, new_accum, steps = call(
        step_kernel,
        [((cols, touched), F32), ((1, touched), F32), ((ALL_D, EMB), BF16)],
        messages,
        total,
        row_accum.reshape(1, -1),
        table_cols,
        steps_to,
        block,
        flops=2 * 100 * 10**6,
    )
    served = over_rows(steps, ROWS_D)
    serving, grad_bottom = call(
        final_kernel, [((4 * EMB, PEERS), BF16), ((2 * PEERS, EMB), F32)], served, flops=2 * 50 * 10**6
    )
    serving = serving.reshape(16, cols, PEERS).transpose(2, 0, 1)[None]
    return (new_rows.T, new_accum.reshape(-1), serving, grad_bottom)


def solution(mesh):
    return jax.shard_map(
        per_device,
        mesh=mesh,
        in_specs=(
            P("rows", None),
            P("rows"),
            P("serve", "rows", None),
            P("serve", "rows", None),
            P("serve", "rows", None, None),
            P("serve", "rows", None),
            P("serve", "rows", None),
            P("serve", "rows"),
            P(),
            P(),
            P(),
            P(),
            P(),
            P("rows", None),
        ),
        out_specs=(P("rows", "serve"), P("rows"), P("rows", None, None, "serve"), P()),
        check_vma=False,
    )
```

```python
import functools

import jax
import jax.numpy as jnp
from jax import lax
from jax.experimental import pallas as pl
from jax.experimental.pallas import tpu as pltpu
from jax.sharding import PartitionSpec as P

TABLES = 26
LEARN_RATE = 0.1
EMB = 128
PEERS = 128
CAP = 8
ROWS_A = 10
ALL_A = PEERS * ROWS_A
ROWS_D = 6
ALL_D = PEERS * ROWS_D
F32 = jnp.float32
SMALL = jnp.int8
BF16 = jnp.bfloat16
VMEM_LIMIT = 32 * 1024 * 1024


def dot(a, b, ca=1, cb=0):
    return lax.dot_general(a, b, (((ca,), (cb,)), ((), ())), preferred_element_type=F32)


def iota(shape, dim):
    return lax.broadcasted_iota(jnp.int32, shape, dim)


def onehot(mask):
    return jnp.where(mask, 1.0, 0.0).astype(BF16)


def divide_floor(values, by):
    return jnp.floor((values.astype(F32) + 0.5) * (1.0 / by)).astype(jnp.int32)


def owner_place(owners):
    return owners


def fetch(sources, targets, sems):
    copies = [pltpu.make_async_copy(s, t, sems.at[i]) for i, (s, t) in enumerate(zip(sources, targets))]
    for copy in copies:
        copy.start()
    return copies


def bag_ends(lengths_ref, earlier):
    lens = jnp.broadcast_to(lengths_ref[...].astype(F32), (8, lengths_ref.shape[1]))
    starts = dot(lens.astype(BF16), earlier)
    return starts.T[:, 0:1].astype(jnp.int32), (starts + lens).T[:, 0:1].astype(jnp.int32)


def earlier_than(count):
    return onehot(iota((count, count), 0) < iota((count, count), 1))


def pool_kernel(
    lengths_hbm,
    lookups_hbm,
    owners_hbm,
    targets_hbm,
    table_hbm,
    out_ref,
    slots_ref,
    lengths_ref,
    lookups_ref,
    owners_ref,
    targets_ref,
    table_ref,
    sems,
):
    copies = fetch(
        (lengths_hbm, lookups_hbm, owners_hbm, targets_hbm, table_hbm),
        (lengths_ref, lookups_ref, owners_ref, targets_ref, table_ref),
        sems,
    )
    bags = lengths_ref.shape[1]
    looks = lookups_ref.shape[1]
    touched = table_ref.shape[0]
    for copy in copies[:4]:
        copy.wait()
    earlier = earlier_than(bags)
    starts, ends = bag_ends(lengths_ref, earlier)
    owners = owners_ref[...]
    of_owner = jnp.where(iota((PEERS, bags), 0) == owners, 1.0, 0.0)
    before = dot(of_owner.astype(BF16), earlier)
    rank = jnp.sum(before * of_owner, axis=0, keepdims=True).astype(jnp.int32)
    slots = owner_place(owners) * ROWS_A + rank
    slots_ref[...] = slots
    targets = targets_ref[...]
    sample = divide_floor(targets, TABLES)
    table_of = targets - sample * TABLES
    lane = iota((EMB, bags), 0)
    names = jnp.where(lane == rank, sample + 1, 0) + jnp.where(lane == rank + CAP, table_of, 0)
    names = dot(of_owner.astype(BF16), names.astype(F32).astype(BF16), 1, 1).astype(BF16)
    copies[4].wait()
    table = table_ref[...]
    high = table.astype(BF16)
    low = (table - high.astype(F32)).astype(BF16)
    place = iota((bags, looks), 1)
    in_bag = onehot((place >= starts) & (place < ends))
    lookups = jnp.broadcast_to(lookups_ref[...].astype(F32), (128, looks)).T.astype(jnp.int32)
    both = jnp.concatenate([high, low], axis=1)
    lane = iota((512, 128), 1)
    sums = 0.0
    for first in range(0, looks, 512):
        part = lookups[first : first + 512]
        goes = jnp.concatenate([onehot(part == lane + c) for c in range(0, touched, 128)], axis=1)
        sums = sums + dot(in_bag[:, first : first + 512], dot(goes, both).astype(BF16))
    pooled = (sums[:, :EMB] + sums[:, EMB:]).astype(BF16)
    step = ALL_A // 2
    for c in range(0, ALL_A, step):
        ninth = onehot(iota((step, PEERS), 0) + c == iota((1, PEERS), 1) * ROWS_A + CAP)
        payload = dot(onehot(iota((step, bags), 0) + c == slots), pooled) + dot(ninth, names)
        out_ref[c : c + step, :] = payload.astype(BF16)


def ready_kernel(
    lengths_ref,
    lookups_ref,
    slots_ref,
    owners_ref,
    table_ref,
    routed_ref,
    steps_ref,
    block_ref,
    cols_ref,
    turned_ref,
):
    rows = owners_ref.shape[1]
    bags = slots_ref.shape[1]
    looks = lookups_ref.shape[1]
    starts, ends = bag_ends(lengths_ref, earlier_than(bags))
    place = iota((bags, looks), 1)
    in_bag = onehot((place >= starts) & (place < ends))
    of_row = onehot(iota((rows, looks), 0) == lookups_ref[...])
    counts = dot(in_bag, of_row, 1, 1).astype(BF16)
    routed_ref[...] = dot(onehot(iota((ALL_A, bags), 0) == slots_ref[...]), counts).astype(jnp.int32).astype(SMALL)
    owners = owners_ref[...]
    of_owner = jnp.where(iota((PEERS, rows), 0) == owners, 1.0, 0.0)
    before = dot(of_owner.astype(BF16), onehot(iota((rows, rows), 0) < iota((rows, rows), 1)))
    rank = jnp.sum(before * of_owner, axis=0, keepdims=True).astype(jnp.int32)
    row_of = lax.shift_right_logical(rank, 2)
    block_ref[...] = rank - 4 * row_of
    steps_ref[...] = onehot(iota((ALL_D, rows), 0) == owner_place(owners) * ROWS_D + row_of)
    turned_ref[...] = table_ref[...].T
    cols = cols_ref.shape[0]
    cols_ref[...] = turned_ref[pl.ds(pl.multiple_of(lax.axis_index("serve") * cols, cols), cols), :]


def owner_kernel(*refs):
    arrived_ref, _, *refs = refs
    count = (len(refs) - 10) // 2
    sources, out_ref = refs[:count], refs[count]
    targets = refs[count + 1 : 2 * count + 1]
    cross_ref, mixed_ref, embed_ref, member_ref, table_ref, wanted_ref, *refs = refs[2 * count + 1 :]
    u_turned_ref, v_turned_ref, sems = refs
    copies = [pltpu.make_async_copy(s, t, sems.at[i]) for i, (s, t) in enumerate(zip(sources, targets))]
    dense_ref, w_bottom_ref, cross_u_ref, bias_ref, w_out_ref, labels_ref, cross_v_ref = targets
    for copy in copies[:6]:
        copy.start()
    samples = dense_ref.shape[0]
    peer = iota((PEERS, ALL_A), 0) * ROWS_A
    slot = iota((PEERS, ALL_A), 1)
    name_row = onehot(slot == peer + CAP)
    chunk = onehot(iota((PEERS, ALL_A), 0) == divide_floor(iota((1, ALL_A), 1), ROWS_A))
    arrived = arrived_ref[...]
    names = dot(name_row, arrived).astype(BF16)
    spread = dot(names, chunk, 0, 0)
    place = iota((1, ALL_A), 1)
    place = place - divide_floor(place, ROWS_A) * ROWS_A
    picks = iota((CAP, ALL_A), 0) == place
    sample_row = jnp.sum(jnp.where(picks, spread[:CAP], 0.0), axis=0, keepdims=True)
    table_row = jnp.sum(jnp.where(picks, spread[CAP : 2 * CAP], 0.0), axis=0, keepdims=True)
    member_f = jnp.where(sample_row.astype(jnp.int32) == iota((samples, ALL_A), 0) + 1, 1.0, 0.0)
    member = member_f.astype(BF16)
    member_ref[...] = member_f.T.astype(BF16)
    table_ref[...] = jnp.broadcast_to(table_row, (samples, ALL_A)).T.astype(BF16)

    copies[6].start()
    for copy in copies[:2]:
        copy.wait()
    dense = dense_ref[...]
    pre_act = dot(dense, w_bottom_ref[...])
    sigma = jax.nn.sigmoid(pre_act)
    cross_ref[:, :EMB] = (pre_act * sigma).astype(BF16)
    table_t = table_ref[...]
    for t in range(0, TABLES, 2):
        both = [jnp.where(table_t == t + u, arrived, 0.0).astype(BF16) for u in range(2)]
        cross_ref[:, (t + 1) * EMB : (t + 3) * EMB] = dot(member, jnp.concatenate(both, axis=1)).astype(BF16)

    for copy in copies[2:6]:
        copy.wait()
    low_rank = dot(cross_ref[...], cross_u_ref[...]).astype(BF16)
    u_turned_ref[...] = cross_u_ref[...].T
    copies[6].wait()
    v_turned_ref[...] = cross_v_ref[...].T
    w_out = w_out_ref[...]
    mixed_ref[...] = (dot(low_rank, cross_v_ref[...]) + (bias_ref[...] + 1.0)) * w_out
    cross_f = cross_ref[...].astype(F32)
    logits = jnp.sum(cross_f * mixed_ref[...], axis=1, keepdims=True)
    logit_grad = jax.nn.sigmoid(logits) - labels_ref[...].astype(F32)
    mix_grad = (logit_grad * w_out * cross_f).astype(BF16)
    low_grad = dot(mix_grad, v_turned_ref[...]).astype(BF16)
    in_grad = logit_grad * mixed_ref[...] + dot(low_grad, u_turned_ref[...])
    pre_grad = (in_grad[:, :EMB] * (sigma * (1.0 + pre_act * (1.0 - sigma)))).astype(BF16)
    for t in range(TABLES):
        embed_ref[t * samples : (t + 1) * samples, :] = in_grad[:, (t + 1) * EMB : (t + 2) * EMB].astype(BF16)
    line = iota((1, 2 * PEERS), 1)
    line = lax.shift_right_logical(line, 1) * ROWS_A + CAP + (line & 1)
    wanted_ref[...] = onehot(iota((ALL_A, 2 * PEERS), 0) == line)
    embed_ref[TABLES * samples :, :] = dot(dense, pre_grad, 0, 0).astype(BF16)

    step = ALL_A // 2
    for c in range(ALL_A // step):
        rows = slice(c * step, (c + 1) * step)
        member_c = member_ref[rows, :]
        table_c = table_ref[rows, :]
        wide = [jnp.where(table_c == t, member_c, 0.0).astype(BF16) for t in range(TABLES)]
        wide = jnp.concatenate(wide + [wanted_ref[rows, :]], axis=1)
        out_ref[rows, :] = dot(wide, embed_ref[...]).astype(BF16)


def return_kernel(returned_ref, routed_ref, grads_ref, bottom_ref):
    returned = returned_ref[...]
    grads_ref[...] = dot(returned, routed_ref[...].astype(BF16), 0, 0).astype(BF16)
    slot = iota((8, ALL_A), 1)
    place = slot - divide_floor(slot, ROWS_A) * ROWS_A
    bottom_ref[...] = dot(onehot(place == iota((8, ALL_A), 0) + CAP), returned)


def total_kernel(grads_ref, bottom_ref, total_ref, message_ref):
    total = grads_ref[0].astype(F32)
    for s in range(1, grads_ref.shape[0]):
        total = total + grads_ref[s].astype(F32)
    total_ref[...] = total
    squares = jnp.sum(total * total, axis=0, keepdims=True)
    bottom = bottom_ref[...]
    message = jnp.concatenate([squares, bottom[0:1], bottom[1:2]], axis=1)
    for s in range(message_ref.shape[0]):
        message_ref[s] = message


def step_kernel(
    message_ref, total_ref, accum_ref, table_ref, steps_ref, block_ref, rows_ref, accum_out_ref, out_ref
):
    rows = accum_ref.shape[1]
    message = message_ref[0]
    for s in range(1, message_ref.shape[0]):
        message = message + message_ref[s]
    accum = accum_ref[...] + message[:, :rows] * (1.0 / EMB)
    accum_out_ref[...] = accum
    step = total_ref[...] * (1.0 / jnp.sqrt(accum))
    rows_ref[...] = table_ref[...] - LEARN_RATE * step
    block = block_ref[...]
    wide = jnp.concatenate([jnp.where(block == a, step, 0.0) for a in range(4)], axis=0).astype(BF16)
    payload = dot(steps_ref[...], wide, 1, 1)
    slot = iota((ALL_D, EMB), 0)
    place = slot - divide_floor(slot, ROWS_D) * ROWS_D
    payload = jnp.where(place == 4, message[:, rows : rows + EMB], payload)
    payload = jnp.where(place == 5, message[:, rows + EMB : rows + 2 * EMB], payload)
    out_ref[...] = payload.astype(BF16)


def final_kernel(served_ref, serving_ref, bottom_ref):
    served = served_ref[...]
    slot = iota((ALL_D, PEERS), 0) - iota((ALL_D, PEERS), 1) * ROWS_D
    picks = jnp.concatenate([onehot(slot == r) for r in range(ROWS_D)], axis=1)
    lines = dot(served, picks, 0, 0)
    serving_ref[...] = jnp.concatenate([lines[:, r * PEERS : (r + 1) * PEERS] for r in range(4)], axis=0).astype(BF16)
    line = iota((2 * PEERS, ALL_D), 0)
    slot = iota((2 * PEERS, ALL_D), 1)
    pick = onehot(slot == lax.shift_right_logical(line, 1) * ROWS_D + 4 + (line & 1))
    bottom_ref[...] = dot(pick, served)


def call(kernel, outs, *args, scratch=(), flops=0, hbm=(), limit=VMEM_LIMIT):
    moved = sum(x.size * x.dtype.itemsize for x in args)
    spaces = [pltpu.HBM if i in hbm else pltpu.VMEM for i in range(len(args))]
    return pl.pallas_call(
        kernel,
        out_shape=[jax.ShapeDtypeStruct(shape, kind) for shape, kind in outs],
        in_specs=[pl.BlockSpec(memory_space=space) for space in spaces],
        scratch_shapes=list(scratch),
        compiler_params=pltpu.CompilerParams(vmem_limit_bytes=limit),
        cost_estimate=pl.CostEstimate(flops=flops, bytes_accessed=moved, transcendentals=0),
    )(*args)


def over_rows(chunks, rows):
    split = chunks.reshape(PEERS, rows // 2, 2, EMB)
    split = lax.all_to_all(split, "rows", split_axis=0, concat_axis=0, tiled=True)
    return split.reshape(PEERS * rows, EMB)


def over_serve(pieces):
    return lax.all_to_all(pieces, "serve", split_axis=0, concat_axis=0, tiled=True)


def per_device(
    table_rows,
    row_accum,
    lookup_rows,
    bag_lengths,
    bag_owner,
    bag_target,
    bottom_in,
    labels,
    w_bottom,
    cross_u,
    cross_v,
    cross_bias,
    w_out,
    serve_owner,
):
    touched = table_rows.shape[0]
    lookups = lookup_rows.reshape(1, -1)
    lengths = bag_lengths.reshape(1, -1)
    bags = lengths.shape[1]
    owners = bag_owner.reshape(1, -1)
    targets = bag_target.reshape(1, -1)
    dense_in = bottom_in.reshape(-1, bottom_in.shape[-1])
    samples = dense_in.shape[0]
    width = cross_u.shape[0]
    serves = lax.axis_size("serve")
    cols = EMB // serves

    outgoing, slots = call(
        pool_kernel,
        [((ALL_A, EMB), BF16), ((1, bags), jnp.int32)],
        lengths,
        lookups,
        owners,
        targets,
        table_rows,
        scratch=(
            pltpu.VMEM(lengths.shape, jnp.int32),
            pltpu.VMEM(lookups.shape, jnp.int32),
            pltpu.VMEM(owners.shape, jnp.int32),
            pltpu.VMEM(targets.shape, jnp.int32),
            pltpu.VMEM(table_rows.shape, F32),
            pltpu.SemaphoreType.DMA((5,)),
        ),
        flops=2 * 700 * 10**6,
        hbm=range(5),
        limit=60 * 1024 * 1024,
    )
    arrived = over_rows(outgoing, ROWS_A)
    routed, steps_to, block, table_cols = call(
        ready_kernel,
        [
            ((ALL_A, touched), SMALL),
            ((ALL_D, touched), BF16),
            ((1, touched), jnp.int32),
            ((cols, touched), F32),
        ],
        lengths,
        lookups,
        slots,
        serve_owner.reshape(1, -1),
        table_rows,
        scratch=(pltpu.VMEM((EMB, touched), F32),),
        flops=2 * 1600 * 10**6,
        limit=60 * 1024 * 1024,
    )
    operands = (
        arrived,
        steps_to,
        dense_in,
        w_bottom,
        cross_u,
        cross_bias.reshape(1, -1),
        w_out.reshape(1, -1),
        labels.reshape(-1, 1),
        cross_v,
    )
    (replies,) = call(
        owner_kernel,
        [((ALL_A, EMB), BF16)],
        *operands,
        scratch=tuple(pltpu.VMEM(x.shape, x.dtype) for x in operands[2:])
        + (
            pltpu.VMEM((samples, width), BF16),
            pltpu.VMEM((samples, width), F32),
            pltpu.VMEM((samples * TABLES + 2 * PEERS, EMB), BF16),
            pltpu.VMEM((ALL_A, PEERS), BF16),
            pltpu.VMEM((ALL_A, PEERS), BF16),
            pltpu.VMEM((ALL_A, 2 * PEERS), BF16),
            pltpu.VMEM(cross_u.shape[::-1], BF16),
            pltpu.VMEM(cross_v.shape[::-1], BF16),
            pltpu.SemaphoreType.DMA((len(operands) - 2,)),
        ),
        flops=2 * 1600 * 10**6,
        hbm=range(1, len(operands)),
        limit=52 * 1024 * 1024,
    )
    returned = over_rows(replies, ROWS_A)
    grads, bottom = call(
        return_kernel,
        [((EMB, touched), BF16), ((8, EMB), F32)],
        returned,
        routed,
        flops=2 * 160 * 10**6,
    )
    pieces = over_serve(grads.reshape(serves, cols, touched))
    total, message = call(
        total_kernel,
        [((cols, touched), F32), ((serves, 1, touched + 2 * EMB), F32)],
        pieces,
        bottom,
    )
    messages = over_serve(message)
    new_rows, new_accum, steps = call(
        step_kernel,
        [((cols, touched), F32), ((1, touched), F32), ((ALL_D, EMB), BF16)],
        messages,
        total,
        row_accum.reshape(1, -1),
        table_cols,
        steps_to,
        block,
        flops=2 * 100 * 10**6,
    )
    served = over_rows(steps, ROWS_D)
    serving, grad_bottom = call(
        final_kernel, [((4 * EMB, PEERS), BF16), ((2 * PEERS, EMB), F32)], served, flops=2 * 50 * 10**6
    )
    serving = serving.reshape(16, cols, PEERS).transpose(2, 0, 1)[None]
    return (new_rows.T, new_accum.reshape(-1), serving, grad_bottom)


def solution(mesh):
    return jax.shard_map(
        per_device,
        mesh=mesh,
        in_specs=(
            P("rows", None),
            P("rows"),
            P("serve", "rows", None),
            P("serve", "rows", None),
            P("serve", "rows", None, None),
            P("serve", "rows", None),
            P("serve", "rows", None),
            P("serve", "rows"),
            P(),
            P(),
            P(),
            P(),
            P(),
            P("rows", None),
        ),
        out_specs=(P("rows", "serve"), P("rows"), P("rows", None, None, "serve"), P()),
        check_vma=False,
    )
```

```python
import functools

import jax
import jax.numpy as jnp
from jax import lax
from jax.experimental import pallas as pl
from jax.experimental.pallas import tpu as pltpu
from jax.sharding import PartitionSpec as P

TABLES = 26
LEARN_RATE = 0.1
EMB = 128
PEERS = 128
CAP = 8
ROWS_A = 10
ALL_A = PEERS * ROWS_A
ROWS_D = 6
ALL_D = PEERS * ROWS_D
F32 = jnp.float32
SMALL = jnp.int8
BF16 = jnp.bfloat16
VMEM_LIMIT = 32 * 1024 * 1024


def dot(a, b, ca=1, cb=0):
    return lax.dot_general(a, b, (((ca,), (cb,)), ((), ())), preferred_element_type=F32)


def iota(shape, dim):
    return lax.broadcasted_iota(jnp.int32, shape, dim)


def onehot(mask):
    return jnp.where(mask, 1.0, 0.0).astype(BF16)


def divide_floor(values, by):
    return jnp.floor((values.astype(F32) + 0.5) * (1.0 / by)).astype(jnp.int32)


def owner_place(owners):
    return owners


def fetch(sources, targets, sems):
    copies = [pltpu.make_async_copy(s, t, sems.at[i]) for i, (s, t) in enumerate(zip(sources, targets))]
    for copy in copies:
        copy.start()
    return copies


def bag_ends(lengths_ref, earlier):
    lens = jnp.broadcast_to(lengths_ref[...].astype(F32), (8, lengths_ref.shape[1]))
    starts = dot(lens.astype(BF16), earlier)
    return starts.T[:, 0:1].astype(jnp.int32), (starts + lens).T[:, 0:1].astype(jnp.int32)


def earlier_than(count):
    return onehot(iota((count, count), 0) < iota((count, count), 1))


def pool_kernel(
    lengths_hbm,
    lookups_hbm,
    owners_hbm,
    targets_hbm,
    table_hbm,
    out_ref,
    slots_ref,
    lengths_ref,
    lookups_ref,
    owners_ref,
    targets_ref,
    table_ref,
    sems,
):
    copies = fetch(
        (lengths_hbm, lookups_hbm, owners_hbm, targets_hbm, table_hbm),
        (lengths_ref, lookups_ref, owners_ref, targets_ref, table_ref),
        sems,
    )
    bags = lengths_ref.shape[1]
    looks = lookups_ref.shape[1]
    touched = table_ref.shape[0]
    for copy in copies[:4]:
        copy.wait()
    earlier = earlier_than(bags)
    starts, ends = bag_ends(lengths_ref, earlier)
    owners = owners_ref[...]
    of_owner = jnp.where(iota((PEERS, bags), 0) == owners, 1.0, 0.0)
    before = dot(of_owner.astype(BF16), earlier)
    rank = jnp.sum(before * of_owner, axis=0, keepdims=True).astype(jnp.int32)
    slots = owner_place(owners) * ROWS_A + rank
    slots_ref[...] = slots
    targets = targets_ref[...]
    sample = divide_floor(targets, TABLES)
    table_of = targets - sample * TABLES
    lane = iota((EMB, bags), 0)
    names = jnp.where(lane == rank, sample + 1, 0) + jnp.where(lane == rank + CAP, table_of, 0)
    names = dot(of_owner.astype(BF16), names.astype(F32).astype(BF16), 1, 1).astype(BF16)
    copies[4].wait()
    table = table_ref[...]
    high = table.astype(BF16)
    low = (table - high.astype(F32)).astype(BF16)
    place = iota((bags, looks), 1)
    in_bag = onehot((place >= starts) & (place < ends))
    lookups = jnp.broadcast_to(lookups_ref[...].astype(F32), (128, looks)).T.astype(jnp.int32)
    both = jnp.concatenate([high, low], axis=1)
    lane = iota((512, 128), 1)
    sums = 0.0
    for first in range(0, looks, 512):
        part = lookups[first : first + 512]
        goes = jnp.concatenate([onehot(part == lane + c) for c in range(0, touched, 128)], axis=1)
        sums = sums + dot(in_bag[:, first : first + 512], dot(goes, both).astype(BF16))
    pooled = (sums[:, :EMB] + sums[:, EMB:]).astype(BF16)
    step = ALL_A // 2
    for c in range(0, ALL_A, step):
        ninth = onehot(iota((step, PEERS), 0) + c == iota((1, PEERS), 1) * ROWS_A + CAP)
        payload = dot(onehot(iota((step, bags), 0) + c == slots), pooled) + dot(ninth, names)
        out_ref[c : c + step, :] = payload.astype(BF16)


def ready_kernel(
    lengths_ref,
    lookups_ref,
    slots_ref,
    owners_ref,
    table_ref,
    routed_ref,
    steps_ref,
    block_ref,
    cols_ref,
    turned_ref,
):
    rows = owners_ref.shape[1]
    bags = slots_ref.shape[1]
    looks = lookups_ref.shape[1]
    starts, ends = bag_ends(lengths_ref, earlier_than(bags))
    place = iota((bags, looks), 1)
    in_bag = onehot((place >= starts) & (place < ends))
    of_row = onehot(iota((rows, looks), 0) == lookups_ref[...])
    counts = dot(in_bag, of_row, 1, 1).astype(BF16)
    routed_ref[...] = dot(onehot(iota((ALL_A, bags), 0) == slots_ref[...]), counts).astype(jnp.int32).astype(SMALL)
    owners = owners_ref[...]
    of_owner = jnp.where(iota((PEERS, rows), 0) == owners, 1.0, 0.0)
    before = dot(of_owner.astype(BF16), onehot(iota((rows, rows), 0) < iota((rows, rows), 1)))
    rank = jnp.sum(before * of_owner, axis=0, keepdims=True).astype(jnp.int32)
    row_of = lax.shift_right_logical(rank, 2)
    block_ref[...] = rank - 4 * row_of
    steps_ref[...] = onehot(iota((ALL_D, rows), 0) == owner_place(owners) * ROWS_D + row_of)
    turned_ref[...] = table_ref[...].T
    cols = cols_ref.shape[0]
    cols_ref[...] = turned_ref[pl.ds(pl.multiple_of(lax.axis_index("serve") * cols, cols), cols), :]


def owner_kernel(*refs):
    arrived_ref, dense_ref, w_bottom_ref, bias_ref, w_out_ref, labels_ref, *refs = refs
    refs = refs[1:]
    count = (len(refs) - 10) // 2
    sources, out_ref = refs[:count], refs[count]
    targets = refs[count + 1 : 2 * count + 1]
    cross_ref, mixed_ref, embed_ref, member_ref, table_ref, wanted_ref, *refs = refs[2 * count + 1 :]
    u_turned_ref, v_turned_ref, sems = refs
    copies = [pltpu.make_async_copy(s, t, sems.at[i]) for i, (s, t) in enumerate(zip(sources, targets))]
    cross_u_ref, cross_v_ref = targets
    copies[0].start()
    samples = dense_ref.shape[0]
    peer = iota((PEERS, ALL_A), 0) * ROWS_A
    slot = iota((PEERS, ALL_A), 1)
    name_row = onehot(slot == peer + CAP)
    chunk = onehot(iota((PEERS, ALL_A), 0) == divide_floor(iota((1, ALL_A), 1), ROWS_A))
    arrived = arrived_ref[...]
    names = dot(name_row, arrived).astype(BF16)
    spread = dot(names, chunk, 0, 0)
    place = iota((1, ALL_A), 1)
    place = place - divide_floor(place, ROWS_A) * ROWS_A
    picks = iota((CAP, ALL_A), 0) == place
    sample_row = jnp.sum(jnp.where(picks, spread[:CAP], 0.0), axis=0, keepdims=True)
    table_row = jnp.sum(jnp.where(picks, spread[CAP : 2 * CAP], 0.0), axis=0, keepdims=True)
    member_f = jnp.where(sample_row.astype(jnp.int32) == iota((samples, ALL_A), 0) + 1, 1.0, 0.0)
    member = member_f.astype(BF16)
    member_ref[...] = member_f.T.astype(BF16)
    table_ref[...] = jnp.broadcast_to(table_row, (samples, ALL_A)).T.astype(BF16)

    copies[1].start()
    dense = dense_ref[...]
    pre_act = dot(dense, w_bottom_ref[...])
    sigma = jax.nn.sigmoid(pre_act)
    cross_ref[:, :EMB] = (pre_act * sigma).astype(BF16)
    table_t = table_ref[...]
    for t in range(0, TABLES, 2):
        both = [jnp.where(table_t == t + u, arrived, 0.0).astype(BF16) for u in range(2)]
        cross_ref[:, (t + 1) * EMB : (t + 3) * EMB] = dot(member, jnp.concatenate(both, axis=1)).astype(BF16)

    copies[0].wait()
    low_rank = dot(cross_ref[...], cross_u_ref[...]).astype(BF16)
    u_turned_ref[...] = cross_u_ref[...].T
    copies[1].wait()
    v_turned_ref[...] = cross_v_ref[...].T
    w_out = w_out_ref[...]
    mixed_ref[...] = (dot(low_rank, cross_v_ref[...]) + (bias_ref[...] + 1.0)) * w_out
    cross_f = cross_ref[...].astype(F32)
    logits = jnp.sum(cross_f * mixed_ref[...], axis=1, keepdims=True)
    logit_grad = jax.nn.sigmoid(logits) - labels_ref[...].astype(F32)
    mix_grad = (logit_grad * w_out * cross_f).astype(BF16)
    low_grad = dot(mix_grad, v_turned_ref[...]).astype(BF16)
    in_grad = logit_grad * mixed_ref[...] + dot(low_grad, u_turned_ref[...])
    pre_grad = (in_grad[:, :EMB] * (sigma * (1.0 + pre_act * (1.0 - sigma)))).astype(BF16)
    for t in range(TABLES):
        embed_ref[t * samples : (t + 1) * samples, :] = in_grad[:, (t + 1) * EMB : (t + 2) * EMB].astype(BF16)
    line = iota((1, 2 * PEERS), 1)
    line = lax.shift_right_logical(line, 1) * ROWS_A + CAP + (line & 1)
    wanted_ref[...] = onehot(iota((ALL_A, 2 * PEERS), 0) == line)
    embed_ref[TABLES * samples :, :] = dot(dense, pre_grad, 0, 0).astype(BF16)

    step = ALL_A // 2
    for c in range(ALL_A // step):
        rows = slice(c * step, (c + 1) * step)
        member_c = member_ref[rows, :]
        table_c = table_ref[rows, :]
        wide = [jnp.where(table_c == t, member_c, 0.0).astype(BF16) for t in range(TABLES)]
        wide = jnp.concatenate(wide + [wanted_ref[rows, :]], axis=1)
        out_ref[rows, :] = dot(wide, embed_ref[...]).astype(BF16)


def return_kernel(returned_ref, routed_ref, grads_ref, bottom_ref):
    returned = returned_ref[...]
    grads_ref[...] = dot(returned, routed_ref[...].astype(BF16), 0, 0).astype(BF16)
    slot = iota((8, ALL_A), 1)
    place = slot - divide_floor(slot, ROWS_A) * ROWS_A
    bottom_ref[...] = dot(onehot(place == iota((8, ALL_A), 0) + CAP), returned)


def total_kernel(grads_ref, bottom_ref, total_ref, message_ref):
    total = grads_ref[0].astype(F32)
    for s in range(1, grads_ref.shape[0]):
        total = total + grads_ref[s].astype(F32)
    total_ref[...] = total
    squares = jnp.sum(total * total, axis=0, keepdims=True)
    bottom = bottom_ref[...]
    message = jnp.concatenate([squares, bottom[0:1], bottom[1:2]], axis=1)
    for s in range(message_ref.shape[0]):
        message_ref[s] = message


def step_kernel(
    message_ref, total_ref, accum_ref, table_ref, steps_ref, block_ref, rows_ref, accum_out_ref, out_ref
):
    rows = accum_ref.shape[1]
    message = message_ref[0]
    for s in range(1, message_ref.shape[0]):
        message = message + message_ref[s]
    accum = accum_ref[...] + message[:, :rows] * (1.0 / EMB)
    accum_out_ref[...] = accum
    step = total_ref[...] * (1.0 / jnp.sqrt(accum))
    rows_ref[...] = table_ref[...] - LEARN_RATE * step
    block = block_ref[...]
    wide = jnp.concatenate([jnp.where(block == a, step, 0.0) for a in range(4)], axis=0).astype(BF16)
    payload = dot(steps_ref[...], wide, 1, 1)
    slot = iota((ALL_D, EMB), 0)
    place = slot - divide_floor(slot, ROWS_D) * ROWS_D
    payload = jnp.where(place == 4, message[:, rows : rows + EMB], payload)
    payload = jnp.where(place == 5, message[:, rows + EMB : rows + 2 * EMB], payload)
    out_ref[...] = payload.astype(BF16)


def final_kernel(served_ref, serving_ref, bottom_ref):
    served = served_ref[...]
    slot = iota((ALL_D, PEERS), 0) - iota((ALL_D, PEERS), 1) * ROWS_D
    picks = jnp.concatenate([onehot(slot == r) for r in range(ROWS_D)], axis=1)
    lines = dot(served, picks, 0, 0)
    serving_ref[...] = jnp.concatenate([lines[:, r * PEERS : (r + 1) * PEERS] for r in range(4)], axis=0).astype(BF16)
    line = iota((2 * PEERS, ALL_D), 0)
    slot = iota((2 * PEERS, ALL_D), 1)
    pick = onehot(slot == lax.shift_right_logical(line, 1) * ROWS_D + 4 + (line & 1))
    bottom_ref[...] = dot(pick, served)


def call(kernel, outs, *args, scratch=(), flops=0, hbm=(), limit=VMEM_LIMIT):
    moved = sum(x.size * x.dtype.itemsize for x in args)
    spaces = [pltpu.HBM if i in hbm else pltpu.VMEM for i in range(len(args))]
    return pl.pallas_call(
        kernel,
        out_shape=[jax.ShapeDtypeStruct(shape, kind) for shape, kind in outs],
        in_specs=[pl.BlockSpec(memory_space=space) for space in spaces],
        scratch_shapes=list(scratch),
        compiler_params=pltpu.CompilerParams(vmem_limit_bytes=limit),
        cost_estimate=pl.CostEstimate(flops=flops, bytes_accessed=moved, transcendentals=0),
    )(*args)


def over_rows(chunks, rows):
    split = chunks.reshape(PEERS, rows // 2, 2, EMB)
    split = lax.all_to_all(split, "rows", split_axis=0, concat_axis=0, tiled=True)
    return split.reshape(PEERS * rows, EMB)


def over_serve(pieces):
    return lax.all_to_all(pieces, "serve", split_axis=0, concat_axis=0, tiled=True)


def per_device(
    table_rows,
    row_accum,
    lookup_rows,
    bag_lengths,
    bag_owner,
    bag_target,
    bottom_in,
    labels,
    w_bottom,
    cross_u,
    cross_v,
    cross_bias,
    w_out,
    serve_owner,
):
    touched = table_rows.shape[0]
    lookups = lookup_rows.reshape(1, -1)
    lengths = bag_lengths.reshape(1, -1)
    bags = lengths.shape[1]
    owners = bag_owner.reshape(1, -1)
    targets = bag_target.reshape(1, -1)
    dense_in = bottom_in.reshape(-1, bottom_in.shape[-1])
    samples = dense_in.shape[0]
    width = cross_u.shape[0]
    serves = lax.axis_size("serve")
    cols = EMB // serves

    outgoing, slots = call(
        pool_kernel,
        [((ALL_A, EMB), BF16), ((1, bags), jnp.int32)],
        lengths,
        lookups,
        owners,
        targets,
        table_rows,
        scratch=(
            pltpu.VMEM(lengths.shape, jnp.int32),
            pltpu.VMEM(lookups.shape, jnp.int32),
            pltpu.VMEM(owners.shape, jnp.int32),
            pltpu.VMEM(targets.shape, jnp.int32),
            pltpu.VMEM(table_rows.shape, F32),
            pltpu.SemaphoreType.DMA((5,)),
        ),
        flops=2 * 700 * 10**6,
        hbm=range(5),
        limit=60 * 1024 * 1024,
    )
    arrived = over_rows(outgoing, ROWS_A)
    routed, steps_to, block, table_cols = call(
        ready_kernel,
        [
            ((ALL_A, touched), SMALL),
            ((ALL_D, touched), BF16),
            ((1, touched), jnp.int32),
            ((cols, touched), F32),
        ],
        lengths,
        lookups,
        slots,
        serve_owner.reshape(1, -1),
        table_rows,
        scratch=(pltpu.VMEM((EMB, touched), F32),),
        flops=2 * 1600 * 10**6,
        limit=60 * 1024 * 1024,
    )
    operands = (
        arrived,
        dense_in,
        w_bottom,
        cross_bias.reshape(1, -1),
        w_out.reshape(1, -1),
        labels.reshape(-1, 1),
        steps_to,
        cross_u,
        cross_v,
    )
    (replies,) = call(
        owner_kernel,
        [((ALL_A, EMB), BF16)],
        *operands,
        scratch=tuple(pltpu.VMEM(x.shape, x.dtype) for x in operands[7:])
        + (
            pltpu.VMEM((samples, width), BF16),
            pltpu.VMEM((samples, width), F32),
            pltpu.VMEM((samples * TABLES + 2 * PEERS, EMB), BF16),
            pltpu.VMEM((ALL_A, PEERS), BF16),
            pltpu.VMEM((ALL_A, PEERS), BF16),
            pltpu.VMEM((ALL_A, 2 * PEERS), BF16),
            pltpu.VMEM(cross_u.shape[::-1], BF16),
            pltpu.VMEM(cross_v.shape[::-1], BF16),
            pltpu.SemaphoreType.DMA((2,)),
        ),
        flops=2 * 1600 * 10**6,
        hbm=(6, 7, 8),
        limit=52 * 1024 * 1024,
    )
    returned = over_rows(replies, ROWS_A)
    grads, bottom = call(
        return_kernel,
        [((EMB, touched), BF16), ((8, EMB), F32)],
        returned,
        routed,
        flops=2 * 160 * 10**6,
    )
    pieces = over_serve(grads.reshape(serves, cols, touched))
    total, message = call(
        total_kernel,
        [((cols, touched), F32), ((serves, 1, touched + 2 * EMB), F32)],
        pieces,
        bottom,
    )
    messages = over_serve(message)
    new_rows, new_accum, steps = call(
        step_kernel,
        [((cols, touched), F32), ((1, touched), F32), ((ALL_D, EMB), BF16)],
        messages,
        total,
        row_accum.reshape(1, -1),
        table_cols,
        steps_to,
        block,
        flops=2 * 100 * 10**6,
    )
    served = over_rows(steps, ROWS_D)
    serving, grad_bottom = call(
        final_kernel, [((4 * EMB, PEERS), BF16), ((2 * PEERS, EMB), F32)], served, flops=2 * 50 * 10**6
    )
    serving = serving.reshape(16, cols, PEERS).transpose(2, 0, 1)[None]
    return (new_rows.T, new_accum.reshape(-1), serving, grad_bottom)


def solution(mesh):
    return jax.shard_map(
        per_device,
        mesh=mesh,
        in_specs=(
            P("rows", None),
            P("rows"),
            P("serve", "rows", None),
            P("serve", "rows", None),
            P("serve", "rows", None, None),
            P("serve", "rows", None),
            P("serve", "rows", None),
            P("serve", "rows"),
            P(),
            P(),
            P(),
            P(),
            P(),
            P("rows", None),
        ),
        out_specs=(P("rows", "serve"), P("rows"), P("rows", None, None, "serve"), P()),
        check_vma=False,
    )
```
